32 devices in a mesh: grp: 2 (over y), blk: 4 (over z), aux: 4 (over x, core).
Axes of the slice: x: 2, y: 2, z: 4, core: 2. Of those that a mesh axis runs over, the one named last changes fastest.
Arguments:
- integrals: bfloat16 [64, 4, 128, 128], P(('grp', 'blk'), 'aux'), parts along dimension 0, may hold values from -0.796875 to 0.796875
- pair_codes: int32 [64], P(('grp', 'blk')), parts along dimension 0, may hold values from 0 to 3, as said below
- counts: int32 [32], P(('grp', 'blk')), parts along dimension 0, may hold values from 0 to 2, as said below
- coeff: bfloat16 [2048, 768], P(('grp', 'blk')), parts along dimension 0, may hold values from -0.375 to 0.375
Outputs:
- exchange_rows: float32 [2048, 768], P(('grp', 'blk', 'aux')), parts along dimension 0
The draws below stay inside these ranges and needn't reach their ends.
There are 2 independent parts, one for each index of `grp`. The reference program is written for one: setup_inputs(seed, part) draws one part's arguments, and reference() takes and returns one part's arrays. A program takes and returns all parts, laid end to end along the dimension named above; each array names one. Nothing has to cross between parts.
Inputs may be any that keep to these rules, and one draw needn't show every extreme that they name: `pair_codes`: within each batch the 2 codes differ; code c names the local row block c // 2 of the target and the local column block c % 2 of the source. `counts`: entry g holds the live slots of batch g (source blk index g // the number of blk indices, target g % it); live slots come first in a batch. Some target receives 2 live slots from every source.
All inputs are finite; a program needn't handle non-finite values.
Results may differ from the reference program's by a relative error of at most 0.012.
Values may be sent and summed in bfloat16 or wider, within the bound.
No kernel may reach another device: no remote copies, remote signals or barrier semaphores. Data moves between devices by JAX's collectives and lax.ppermute only.
A program may use at most 128 MiB of HBM per device.

```python
import jax
import jax.numpy as jnp
from jax import lax

BS = 128
BLK_DEV = 2
NOCC = 768
CAP = 2
NBF = 1024
AUX = 4
SLOTS = 32
N_BLK = 4


def draw_pair_codes(key, part):
    key = jax.random.fold_in(key, 11)
    first_key, step_key = jax.random.split(key)
    batches = N_BLK * N_BLK
    square = BLK_DEV * BLK_DEV
    first = jax.random.randint(first_key, (batches,), 0, square, dtype=jnp.int32)
    first = jnp.where(jnp.arange(batches) == 0, square - 1, first)
    stride = jax.random.randint(step_key, (batches,), 1, square, dtype=jnp.int32)
    second = (first + stride) % square
    return jnp.stack([first, second], axis=1).reshape(batches * CAP).astype(jnp.int32)


def draw_counts(key, part):
    key = jax.random.fold_in(key, 23)
    base_key, full_key = jax.random.split(key)
    base = jax.random.randint(base_key, (N_BLK, N_BLK), 0, CAP + 1, dtype=jnp.int32)
    full = jax.random.randint(full_key, (), 0, N_BLK, dtype=jnp.int32)
    base = jnp.where(jnp.arange(N_BLK, dtype=jnp.int32)[None, :] == full, CAP, base)
    return base.reshape(N_BLK * N_BLK).astype(jnp.int32)


def shard_levels(key, shape, cuts, least, high):
    loudness, own = 1.0, jax.random.fold_in(key, 6)
    for dim, blocks in cuts:
        draws = jnp.exp(jax.random.uniform(jax.random.fold_in(own, dim), (blocks,), jnp.float32, least / len(cuts), high / len(cuts)))
        loudness = loudness * jnp.repeat(draws, shape[dim] // blocks).reshape([-1 if axis == dim else 1 for axis in range(len(shape))])
    return loudness


def scatter_about(own_key, extent, width, bound, cuts=(), held_as=jnp.bfloat16):
    factor_of = shard_levels(own_key, extent, cuts, -0.22, 0.18) if cuts else 1.0
    array = jax.random.normal(own_key, extent, jnp.float32) * width * factor_of
    return jnp.minimum(jnp.maximum(array, -bound), bound).astype(held_as)


def setup_inputs(seed: int = 0, part: int = 0) -> dict:
    arg_keys = jax.random.split(jax.random.key(seed), 5)
    part_keys = jax.random.split(jax.random.fold_in(arg_keys[4], part), 5)
    integrals = scatter_about(part_keys[0], (SLOTS, AUX, BS, BS), 0.1, 0.796875, ((0, 4), (1, 4)))
    pair_codes = draw_pair_codes(jax.random.fold_in(jax.random.fold_in(arg_keys[4], part), 71), part)
    counts = draw_counts(jax.random.fold_in(jax.random.fold_in(arg_keys[4], part), 71), part)
    coeff = scatter_about(part_keys[3], (NBF, NOCC), (64 * N_BLK) ** -0.5, 0.375, ((0, 4),))
    return {"integrals": integrals, "pair_codes": pair_codes, "counts": counts, "coeff": coeff}


def reference(integrals, pair_codes, counts, coeff):
    nblocks = N_BLK * BLK_DEV
    per_src = N_BLK * CAP
    slot_ids = jnp.arange(SLOTS, dtype=jnp.int32)
    batch = slot_ids // CAP
    source = batch // N_BLK
    target = batch % N_BLK
    live = (slot_ids % CAP < counts[batch]).astype(jnp.float32)
    row_block = (target * BLK_DEV + pair_codes // BLK_DEV).astype(jnp.int32)
    col_block = (source * BLK_DEV + pair_codes % BLK_DEV).astype(jnp.int32)
    blocks = coeff.astype(jnp.float32).reshape(nblocks, BS, NOCC)

    def add_source(fitted, inputs):
        ints, alive, rows, cols = inputs
        chosen = blocks[cols]
        half = jnp.einsum('spml,sli->spmi', ints.astype(jnp.float32) * alive[:, None, None, None], chosen)
        half = half.astype(jnp.bfloat16).astype(jnp.float32)
        return fitted.at[rows].add(half), None

    start = jnp.zeros((nblocks, AUX, BS, NOCC), jnp.float32)
    fitted, _ = lax.scan(add_source, start, (
        integrals.reshape(N_BLK, per_src, AUX, BS, BS),
        live.reshape(N_BLK, per_src),
        row_block.reshape(N_BLK, per_src),
        col_block.reshape(N_BLK, per_src)))
    fitted = fitted.astype(jnp.bfloat16).astype(jnp.float32)
    fitted_groups = fitted.reshape(N_BLK, BLK_DEV, AUX, BS, NOCC)
    coeff_groups = coeff.astype(jnp.float32).reshape(N_BLK, BLK_DEV, BS, NOCC)

    def add_group(total, inputs):
        rows_c, rows_f = inputs
        partial_value = jnp.einsum('qnj,qpni->pji', rows_c, rows_f)
        partial_value = lax.optimization_barrier(partial_value.astype(jnp.bfloat16))
        return total + partial_value.astype(jnp.float32), None

    occupied, _ = lax.scan(add_group, jnp.zeros((AUX, NOCC, NOCC), jnp.float32), (coeff_groups, fitted_groups))
    occupied = occupied.astype(jnp.bfloat16).astype(jnp.float32)
    result = jnp.einsum('bpnj,pji->bni', fitted, occupied)
    return result.reshape(NBF, NOCC)
```

```python
import functools

import jax
import jax.numpy as jnp
from jax import lax
from jax.experimental import pallas as pl
from jax.experimental.pallas import tpu as pltpu
from jax.sharding import PartitionSpec as P

BF16 = jnp.bfloat16
META = 16


def transform_slots(ints, columns, blocks):
    slots, paux, width, _ = ints.shape
    nocc = blocks.shape[2]

    def one_group(inputs):
        group_ints, group_cols = inputs
        chosen = blocks[group_cols]
        return jnp.einsum(
            "spml,sli->spmi", group_ints, chosen, preferred_element_type=jnp.float32
        ).astype(BF16)

    grouped = lax.map(
        one_group, (ints.reshape(slots // 8, 8, paux, width, width), columns.reshape(slots // 8, 8))
    )
    return grouped.reshape(slots, paux, width, nocc)


def local_long(integrals, pair_codes, counts, coeff):
    slots, paux, width, _ = integrals.shape
    nocc = coeff.shape[1]
    nblk = lax.axis_size("blk")
    per_dev = coeff.shape[0] // width
    cap = slots // nblk
    alive = (jnp.arange(cap)[None, :] < counts[:, None]).reshape(slots)
    masked = integrals * alive.astype(BF16)[:, None, None, None]
    local_blocks = coeff.reshape(per_dev, width, nocc)
    half = transform_slots(masked, pair_codes % per_dev, local_blocks)
    half_in, rows_in = (
        lax.all_to_all(half, "blk", split_axis=0, concat_axis=0, tiled=True),
        lax.all_to_all(pair_codes // per_dev, "blk", split_axis=0, concat_axis=0, tiled=True),
    )
    selector = (rows_in[:, None] == jnp.arange(per_dev, dtype=jnp.int32)[None, :]).astype(BF16)
    fitted = jnp.einsum("sk,spmi->pkmi", selector, half_in, preferred_element_type=jnp.float32)
    fitted = fitted.astype(BF16).reshape(paux, per_dev * width, nocc)
    partial_value = jnp.einsum(
        "nj,pni->pji", coeff, fitted, preferred_element_type=jnp.float32
    ).astype(BF16)
    occupied = lax.psum(partial_value.astype(jnp.float32).astype(BF16), "blk")
    return lax.psum_scatter(
        jnp.einsum("pnj,pji->ni", fitted, occupied, preferred_element_type=jnp.float32).astype(BF16),
        "aux",
        scatter_dimension=0,
        tiled=True,
    ).astype(jnp.float32)


def gather_line(x):
    near = lax.ppermute(x, "blk", [(0, 1), (1, 0), (2, 3), (3, 2)])
    m3 = lax.ppermute(x, "blk", [(1, 2), (2, 1)])
    m2 = lax.ppermute(near, "blk", [(1, 2), (2, 1)])
    e2 = lax.ppermute(m3, "blk", [(1, 0), (2, 3)])
    e3 = lax.ppermute(near, "blk", [(1, 3), (2, 0)])
    return near, m2, m3, e2, e3


def on_end():
    z = lax.axis_index("blk")
    return (z == 0) | (z == lax.axis_size("blk") - 1)


def overlap_kernel(own, q0, q1, q2, q3, coeff_out, overlap_out):
    z, a = lax.axis_index("blk"), lax.axis_index("aux")
    rows = own.shape[0]
    part = rows // 4
    coeff_out[pl.ds(pl.multiple_of(z * rows, rows), rows), :] = own[...]
    for j, ref in enumerate((q0, q1, q2, q3)):
        for k in (1, 2, 3):
            at = (z ^ k) * rows + (a ^ j) * part
            coeff_out[pl.ds(pl.multiple_of(at, part), part), :] = ref[k - 1, :part, :]
    total = coeff_out.shape[0]
    for at in range(0, total, rows):
        overlap_out[at : at + rows, :] = lax.dot_general(
            coeff_out[at : at + rows, :],
            coeff_out[...],
            (((1,), (1,)), ((), ())),
            preferred_element_type=jnp.float32,
        ).astype(BF16)


def exchange_kernel(
    codes, i0, i1, m2, m3, e2, e3, overlap, coeff, mine, p1, p2, p3, dense, total
):
    z, a = lax.axis_index("blk"), lax.axis_index("aux")
    slots, width, _ = i0.shape
    rows = mine.shape[0] * 4
    cap = slots // 4
    dense[...] = jnp.zeros_like(dense)

    def place(ref, k):
        for s in range(slots):
            code = codes[k, s]

            @pl.when(code >= 0)
            def _():
                row = (s // cap) * rows + (code // 2) * width
                col = (z ^ k) * rows + (code % 2) * width
                dense[
                    pl.ds(pl.multiple_of(row, width), width),
                    pl.ds(pl.multiple_of(col, width), width),
                ] = ref[s]

    place(i0, 0)
    place(i1, 1)
    end = on_end()

    @pl.when(end)
    def _():
        place(e2, 2)
        place(e3, 3)

    @pl.when(jnp.logical_not(end))
    def _():
        place(m2, 2)
        place(m3, 3)

    f32 = jnp.float32
    here = dense[pl.ds(pl.multiple_of(z * rows, rows), rows), :]
    left = jnp.dot(here, overlap[...], preferred_element_type=f32).astype(BF16)
    left = jnp.dot(left, dense[...], preferred_element_type=f32).astype(BF16)
    total[...] = jnp.dot(left, coeff[...], preferred_element_type=f32)
    part = mine.shape[0]
    mine[...] = total[pl.ds(pl.multiple_of(a * part, part), part), :]
    for j, out in enumerate((p1, p2, p3), 1):
        out[...] = total[pl.ds(pl.multiple_of((a ^ j) * part, part), part), :].astype(BF16)


def local_line(integrals, pair_codes, counts, coeff):
    slots, _, width, _ = integrals.shape
    rows, nocc = coeff.shape
    part = rows // 4
    nbf = rows * 4
    cap = slots // 4
    a = lax.axis_index("aux")
    flip = lambda k: [(i, i ^ k) for i in range(4)]
    sds = jax.ShapeDtypeStruct
    vmem = pl.BlockSpec(memory_space=pltpu.VMEM)
    params = pltpu.CompilerParams(vmem_limit_bytes=48 * 2**20)

    alive = (jnp.arange(cap)[None, :] < counts[:, None]).reshape(slots)
    codes = jnp.stack([pair_codes, alive.astype(jnp.int32)])

    quarter = lax.dynamic_slice_in_dim(coeff, a * part, part, 0)
    note = jnp.pad(codes.astype(BF16), ((0, META - 2), (0, nocc - slots)))
    near, m2, m3, e2, e3 = gather_line(jnp.concatenate([quarter, note], 0))
    end = on_end()
    q0 = jnp.stack([near, jnp.where(end, e2, m2), jnp.where(end, e3, m3)])
    q2 = lax.ppermute(q0, "aux", flip(2))
    q1 = lax.ppermute(q0, "aux", flip(1))
    q3 = lax.ppermute(q2, "aux", flip(1))
    codes_in = q0[:, part : part + 2, :slots].astype(jnp.int32)
    codes = jnp.concatenate([codes[None], codes_in], 0)
    codes = jnp.where(codes[:, 1] > 0, codes[:, 0], -1)

    ints = integrals.reshape(slots, width, width)
    inear, im2, im3, ie2, ie3 = gather_line(ints)

    full, overlap = pl.pallas_call(
        overlap_kernel,
        out_shape=(sds((nbf, nocc), BF16), sds((nbf, nbf), BF16)),
        in_specs=[vmem] * 5,
        out_specs=(vmem, vmem),
        compiler_params=params,
        cost_estimate=pl.CostEstimate(
            flops=2 * nbf * nbf * nocc, bytes_accessed=nbf * (nbf + 2 * nocc) * 2, transcendentals=0
        ),
    )(coeff, q0, q1, q2, q3)

    mine, p1, p2, p3 = pl.pallas_call(
        exchange_kernel,
        out_shape=(sds((part, nocc), jnp.float32),) + (sds((part, nocc), BF16),) * 3,
        in_specs=[pl.BlockSpec(memory_space=pltpu.SMEM)] + [vmem] * 8,
        out_specs=(vmem,) * 4,
        scratch_shapes=[pltpu.VMEM((nbf, nbf), BF16), pltpu.VMEM((rows, nocc), jnp.float32)],
        compiler_params=params,
        cost_estimate=pl.CostEstimate(
            flops=2 * rows * nbf * (2 * nbf + nocc),
            bytes_accessed=nbf * (2 * nbf + nocc) * 2,
            transcendentals=0,
        ),
    )(codes, ints, inear, im2, im3, ie2, ie3, overlap, full)
    got = [lax.ppermute(p, "aux", flip(k)) for k, p in ((2, p2), (3, p3), (1, p1))]
    return mine + got[0].astype(jnp.float32) + got[1].astype(jnp.float32) + got[2].astype(jnp.float32)


def local(integrals, pair_codes, counts, coeff):
    if lax.axis_size("blk") == 4 and lax.axis_size("aux") == 4:
        return local_line(integrals, pair_codes, counts, coeff)
    return local_long(integrals, pair_codes, counts, coeff)


def solution(mesh):
    in_specs = (
        P(("grp", "blk"), "aux", None, None),
        P(("grp", "blk")),
        P(("grp", "blk")),
        P(("grp", "blk"), None),
    )
    out_specs = P(("grp", "blk", "aux"), None)
    return jax.shard_map(local, mesh=mesh, in_specs=in_specs, out_specs=out_specs, check_vma=False)
```

```python
import functools

import jax
import jax.numpy as jnp
from jax import lax
from jax.experimental import pallas as pl
from jax.experimental.pallas import tpu as pltpu
from jax.sharding import PartitionSpec as P

BF16 = jnp.bfloat16
META = 16


def transform_slots(ints, columns, blocks):
    slots, paux, width, _ = ints.shape
    nocc = blocks.shape[2]

    def one_group(inputs):
        group_ints, group_cols = inputs
        chosen = blocks[group_cols]
        return jnp.einsum(
            "spml,sli->spmi", group_ints, chosen, preferred_element_type=jnp.float32
        ).astype(BF16)

    grouped = lax.map(
        one_group, (ints.reshape(slots // 8, 8, paux, width, width), columns.reshape(slots // 8, 8))
    )
    return grouped.reshape(slots, paux, width, nocc)


def local_long(integrals, pair_codes, counts, coeff):
    slots, paux, width, _ = integrals.shape
    nocc = coeff.shape[1]
    nblk = lax.axis_size("blk")
    per_dev = coeff.shape[0] // width
    cap = slots // nblk
    alive = (jnp.arange(cap)[None, :] < counts[:, None]).reshape(slots)
    masked = integrals * alive.astype(BF16)[:, None, None, None]
    local_blocks = coeff.reshape(per_dev, width, nocc)
    half = transform_slots(masked, pair_codes % per_dev, local_blocks)
    half_in, rows_in = (
        lax.all_to_all(half, "blk", split_axis=0, concat_axis=0, tiled=True),
        lax.all_to_all(pair_codes // per_dev, "blk", split_axis=0, concat_axis=0, tiled=True),
    )
    selector = (rows_in[:, None] == jnp.arange(per_dev, dtype=jnp.int32)[None, :]).astype(BF16)
    fitted = jnp.einsum("sk,spmi->pkmi", selector, half_in, preferred_element_type=jnp.float32)
    fitted = fitted.astype(BF16).reshape(paux, per_dev * width, nocc)
    partial_value = jnp.einsum(
        "nj,pni->pji", coeff, fitted, preferred_element_type=jnp.float32
    ).astype(BF16)
    occupied = lax.psum(partial_value.astype(jnp.float32).astype(BF16), "blk")
    return lax.psum_scatter(
        jnp.einsum("pnj,pji->ni", fitted, occupied, preferred_element_type=jnp.float32).astype(BF16),
        "aux",
        scatter_dimension=0,
        tiled=True,
    ).astype(jnp.float32)


LANES = 128


def after(x, *others):
    return lax.optimization_barrier((x, *others))[0]


PAIRS = [(0, 1), (1, 0), (2, 3), (3, 2)]
MIDDLE = [(1, 2), (2, 1)]
OUTWARD = [(1, 0), (2, 3)]


def gather_line(x):
    near = lax.ppermute(x, "blk", PAIRS)
    m3 = lax.ppermute(x, "blk", MIDDLE)
    m2 = lax.ppermute(near, "blk", MIDDLE)
    e2 = lax.ppermute(m3, "blk", OUTWARD)
    e3 = lax.ppermute(m2, "blk", OUTWARD)
    return near, m2, m3, e2, e3


def on_end():
    z = lax.axis_index("blk")
    return (z == 0) | (z == lax.axis_size("blk") - 1)


def pack_kernel(codes, counts, coeff, out, quarter, note, sem):
    part, nocc = quarter.shape
    a = lax.axis_index("aux")
    copy = pltpu.make_async_copy(
        coeff.at[pl.ds(pl.multiple_of(a * part, part), part)], quarter, sem
    )
    copy.start()
    note[...] = jnp.zeros_like(note)
    note[0:1, : codes.shape[1]] = codes[...].astype(jnp.float32)
    note[8:9, : counts.shape[1]] = counts[...].astype(jnp.float32)
    top = nocc // LANES * part
    out[top : top + META, :] = note[...].astype(BF16)
    copy.wait()
    for c in range(nocc // LANES):
        out[c * part : (c + 1) * part, :] = quarter[:, c * LANES : (c + 1) * LANES]


def overlap_kernel(own, n0, n1, n2, n3, f0, f1, f2, f3, coeff_out, overlap_out):
    z, a = lax.axis_index("blk"), lax.axis_index("aux")
    rows, nocc = own.shape
    part = rows // 4
    coeff_out[pl.ds(pl.multiple_of(z * rows, rows), rows), :] = own[...]
    second = jnp.where(on_end(), z ^ 2, z ^ 3)
    last = jnp.where(on_end(), z ^ 3, z ^ 2)
    for j, (early, late) in enumerate(((n0, f0), (n1, f1), (n2, f2), (n3, f3))):
        for source, ref in ((z ^ 1, early.at[0]), (second, early.at[1]), (last, late)):
            at = pl.ds(pl.multiple_of(source * rows + (a ^ j) * part, part), part)
            for c in range(nocc // LANES):
                coeff_out[at, c * LANES : (c + 1) * LANES] = ref[c * part : (c + 1) * part, :]
    total = coeff_out.shape[0]
    for at in range(0, total, rows):
        overlap_out[at : at + rows, :] = lax.dot_general(
            coeff_out[at : at + rows, :],
            coeff_out[...],
            (((1,), (1,)), ((), ())),
            preferred_element_type=jnp.float32,
        ).astype(BF16)


def exchange_kernel(
    codes, i0, i1, m2, m3, e2, e3, overlap, coeff, mine, p1, p2, p3, dense, total
):
    z, a = lax.axis_index("blk"), lax.axis_index("aux")
    slots, width, _ = i0.shape
    rows = mine.shape[0] * 4
    cap = slots // 4
    dense[...] = jnp.zeros_like(dense)

    def place(ref, k):
        for s in range(slots):
            code = codes[k, s]

            @pl.when(code >= 0)
            def _():
                row = (s // cap) * rows + (code // 2) * width
                col = (z ^ k) * rows + (code % 2) * width
                dense[
                    pl.ds(pl.multiple_of(row, width), width),
                    pl.ds(pl.multiple_of(col, width), width),
                ] = ref[s]

    place(i0, 0)
    place(i1, 1)
    end = on_end()

    @pl.when(end)
    def _():
        place(e2, 2)
        place(e3, 3)

    @pl.when(jnp.logical_not(end))
    def _():
        place(m2, 2)
        place(m3, 3)

    f32 = jnp.float32
    here = dense[pl.ds(pl.multiple_of(z * rows, rows), rows), :]
    left = jnp.dot(here, overlap[...], preferred_element_type=f32).astype(BF16)
    left = jnp.dot(left, dense[...], preferred_element_type=f32).astype(BF16)
    total[...] = jnp.dot(left, coeff[...], preferred_element_type=f32)
    part = mine.shape[0]
    mine[...] = total[pl.ds(pl.multiple_of(a * part, part), part), :]
    for j, out in enumerate((p1, p2, p3), 1):
        out[...] = total[pl.ds(pl.multiple_of((a ^ j) * part, part), part), :].astype(BF16)


def local_line(integrals, pair_codes, counts, coeff):
    slots, _, width, _ = integrals.shape
    rows, nocc = coeff.shape
    part = rows // 4
    nbf = rows * 4
    cap = slots // 4
    flip = lambda k: [(i, i ^ k) for i in range(4)]
    sds = jax.ShapeDtypeStruct
    vmem = pl.BlockSpec(memory_space=pltpu.VMEM)
    smem = pl.BlockSpec(memory_space=pltpu.SMEM)
    params = pltpu.CompilerParams(vmem_limit_bytes=48 * 2**20)
    cost = lambda flops, size: pl.CostEstimate(
        flops=flops, bytes_accessed=size, transcendentals=0
    )

    ints = integrals.reshape(slots, width, width)
    inear, im2, im3, ie2, ie3 = gather_line(ints)

    top = nocc // LANES * part
    packed = pl.pallas_call(
        pack_kernel,
        out_shape=sds((top + META, LANES), BF16),
        in_specs=[vmem, vmem, pl.BlockSpec(memory_space=pltpu.HBM)],
        out_specs=vmem,
        scratch_shapes=[
            pltpu.VMEM((part, nocc), BF16),
            pltpu.VMEM((META, LANES), jnp.float32),
            pltpu.SemaphoreType.DMA,
        ],
        compiler_params=params,
        cost_estimate=cost(0, 4 * part * nocc),
    )(pair_codes[None], counts[None], coeff)
    end = on_end()
    near = lax.ppermute(packed, "blk", PAIRS)
    m3 = lax.ppermute(packed, "blk", MIDDLE)
    m2 = lax.ppermute(after(near, inear), "blk", MIDDLE)
    e2 = lax.ppermute(after(m3, im3), "blk", OUTWARD)
    e3 = lax.ppermute(m2, "blk", OUTWARD)
    swap = lambda x, k: lax.ppermute(x, "aux", flip(k))
    n0 = jnp.stack([near, jnp.where(end, e2, m3)])
    n2 = swap(n0, 2)
    f0 = after(jnp.where(end, e3, m2), im2, ie2)
    f2 = swap(f0, 2)
    n1, n3 = swap(n0, 1), swap(n2, 1)
    f1, f3 = swap(f0, 1), swap(f2, 1)
    second, last = n0[1, top:, :slots], f0[top:, :slots]
    notes = jnp.stack(
        [packed[top:, :slots], n0[0, top:, :slots], jnp.where(end, second, last), jnp.where(end, last, second)]
    ).astype(jnp.int32)
    live = jnp.arange(cap)[None, None, :] < notes[:, 8, :4, None]
    codes = jnp.where(live.reshape(4, slots), notes[:, 0], -1)

    full, overlap = pl.pallas_call(
        overlap_kernel,
        out_shape=(sds((nbf, nocc), BF16), sds((nbf, nbf), BF16)),
        in_specs=[vmem] * 9,
        out_specs=(vmem, vmem),
        compiler_params=params,
        cost_estimate=cost(2 * nbf * nbf * nocc, nbf * (nbf + 2 * nocc) * 2),
    )(coeff, n0, n1, n2, n3, f0, f1, f2, f3)

    mine, p1, p2, p3 = pl.pallas_call(
        exchange_kernel,
        out_shape=(sds((part, nocc), jnp.float32),) + (sds((part, nocc), BF16),) * 3,
        in_specs=[smem] + [vmem] * 8,
        out_specs=(vmem,) * 4,
        scratch_shapes=[pltpu.VMEM((nbf, nbf), BF16), pltpu.VMEM((rows, nocc), jnp.float32)],
        compiler_params=params,
        cost_estimate=cost(2 * rows * nbf * (2 * nbf + nocc), nbf * (2 * nbf + nocc) * 2),
    )(codes, ints, inear, im2, im3, ie2, ie3, overlap, full)
    got = [lax.ppermute(p, "aux", flip(k)) for k, p in ((2, p2), (3, p3), (1, p1))]
    return mine + got[0].astype(jnp.float32) + got[1].astype(jnp.float32) + got[2].astype(jnp.float32)


def local(integrals, pair_codes, counts, coeff):
    if lax.axis_size("blk") == 4 and lax.axis_size("aux") == 4:
        return local_line(integrals, pair_codes, counts, coeff)
    return local_long(integrals, pair_codes, counts, coeff)


def solution(mesh):
    in_specs = (
        P(("grp", "blk"), "aux", None, None),
        P(("grp", "blk")),
        P(("grp", "blk")),
        P(("grp", "blk"), None),
    )
    out_specs = P(("grp", "blk", "aux"), None)
    return jax.shard_map(local, mesh=mesh, in_specs=in_specs, out_specs=out_specs, check_vma=False)
```

```python
import functools

import jax
import jax.numpy as jnp
from jax import lax
from jax.experimental import pallas as pl
from jax.experimental.pallas import tpu as pltpu
from jax.sharding import PartitionSpec as P

BF16 = jnp.bfloat16
META = 16


def transform_slots(ints, columns, blocks):
    slots, paux, width, _ = ints.shape
    nocc = blocks.shape[2]

    def one_group(inputs):
        group_ints, group_cols = inputs
        chosen = blocks[group_cols]
        return jnp.einsum(
            "spml,sli->spmi", group_ints, chosen, preferred_element_type=jnp.float32
        ).astype(BF16)

    grouped = lax.map(
        one_group, (ints.reshape(slots // 8, 8, paux, width, width), columns.reshape(slots // 8, 8))
    )
    return grouped.reshape(slots, paux, width, nocc)


def local_long(integrals, pair_codes, counts, coeff):
    slots, paux, width, _ = integrals.shape
    nocc = coeff.shape[1]
    nblk = lax.axis_size("blk")
    per_dev = coeff.shape[0] // width
    cap = slots // nblk
    alive = (jnp.arange(cap)[None, :] < counts[:, None]).reshape(slots)
    masked = integrals * alive.astype(BF16)[:, None, None, None]
    local_blocks = coeff.reshape(per_dev, width, nocc)
    half = transform_slots(masked, pair_codes % per_dev, local_blocks)
    half_in, rows_in = (
        lax.all_to_all(half, "blk", split_axis=0, concat_axis=0, tiled=True),
        lax.all_to_all(pair_codes // per_dev, "blk", split_axis=0, concat_axis=0, tiled=True),
    )
    selector = (rows_in[:, None] == jnp.arange(per_dev, dtype=jnp.int32)[None, :]).astype(BF16)
    fitted = jnp.einsum("sk,spmi->pkmi", selector, half_in, preferred_element_type=jnp.float32)
    fitted = fitted.astype(BF16).reshape(paux, per_dev * width, nocc)
    partial_value = jnp.einsum(
        "nj,pni->pji", coeff, fitted, preferred_element_type=jnp.float32
    ).astype(BF16)
    occupied = lax.psum(partial_value.astype(jnp.float32).astype(BF16), "blk")
    return lax.psum_scatter(
        jnp.einsum("pnj,pji->ni", fitted, occupied, preferred_element_type=jnp.float32).astype(BF16),
        "aux",
        scatter_dimension=0,
        tiled=True,
    ).astype(jnp.float32)


LANES = 128


def after(x, *others):
    return lax.optimization_barrier((x, *others))[0]


def swap(x, axis, k):
    return lax.ppermute(x, axis, [(i, i ^ k) for i in range(4)])


def pack_kernel(codes, counts, coeff, out, quarter, note, sem):
    part, nocc = quarter.shape
    a = lax.axis_index("aux")
    copy = pltpu.make_async_copy(
        coeff.at[pl.ds(pl.multiple_of(a * part, part), part)], quarter, sem
    )
    copy.start()
    note[...] = jnp.zeros_like(note)
    note[0:1, : codes.shape[1]] = codes[...].astype(jnp.float32)
    note[8:9, : counts.shape[1]] = counts[...].astype(jnp.float32)
    top = nocc // LANES * part
    out[top : top + META, :] = note[...].astype(BF16)
    copy.wait()
    for c in range(nocc // LANES):
        out[c * part : (c + 1) * part, :] = quarter[:, c * LANES : (c + 1) * LANES]


def overlap_kernel(own, early, late, early2, late2, early13, late13, coeff_out, overlap_out):
    z, a = lax.axis_index("blk"), lax.axis_index("aux")
    rows, nocc = own.shape
    part = rows // 4
    coeff_out[pl.ds(pl.multiple_of(z * rows, rows), rows), :] = own[...]
    sources = (
        (0, early.at[0], late, early.at[1]),
        (1, early13.at[0], late13.at[0], early13.at[1]),
        (2, early2.at[0], late2, early2.at[1]),
        (3, early13.at[2], late13.at[1], early13.at[3]),
    )
    for j, *refs in sources:
        for k, ref in enumerate(refs, 1):
            at = pl.ds(pl.multiple_of((z ^ k) * rows + (a ^ j) * part, part), part)
            for c in range(nocc // LANES):
                coeff_out[at, c * LANES : (c + 1) * LANES] = ref[c * part : (c + 1) * part, :]
    total = coeff_out.shape[0]
    for at in range(0, total, rows):
        overlap_out[at : at + rows, :] = lax.dot_general(
            coeff_out[at : at + rows, :],
            coeff_out[...],
            (((1,), (1,)), ((), ())),
            preferred_element_type=jnp.float32,
        ).astype(BF16)


def exchange_kernel(
    notes, i0, i1, i2, i3, overlap, coeff, mine, p1, p2, p3, dense, total
):
    z, a = lax.axis_index("blk"), lax.axis_index("aux")
    slots, width, _ = i0.shape
    rows = mine.shape[0] * 4
    cap = slots // 4
    dense[...] = jnp.zeros_like(dense)

    def place(ref, k):
        for s in range(slots):
            code = notes[k, 0, s]

            @pl.when(s % cap < notes[k, 1, s // cap])
            def _():
                row = (s // cap) * rows + (code // 2) * width
                col = (z ^ k) * rows + (code % 2) * width
                dense[
                    pl.ds(pl.multiple_of(row, width), width),
                    pl.ds(pl.multiple_of(col, width), width),
                ] = ref[s]

    for k, ref in enumerate((i0, i1, i2, i3)):
        place(ref, k)

    f32 = jnp.float32
    here = dense[pl.ds(pl.multiple_of(z * rows, rows), rows), :]
    left = jnp.dot(here, overlap[...], preferred_element_type=f32).astype(BF16)
    left = jnp.dot(left, dense[...], preferred_element_type=f32).astype(BF16)
    total[...] = jnp.dot(left, coeff[...], preferred_element_type=f32)
    part = mine.shape[0]
    mine[...] = total[pl.ds(pl.multiple_of(a * part, part), part), :]
    for j, out in enumerate((p1, p2, p3), 1):
        out[...] = total[pl.ds(pl.multiple_of((a ^ j) * part, part), part), :].astype(BF16)


def local_line(integrals, pair_codes, counts, coeff):
    slots, _, width, _ = integrals.shape
    rows, nocc = coeff.shape
    part = rows // 4
    nbf = rows * 4
    sds = jax.ShapeDtypeStruct
    vmem = pl.BlockSpec(memory_space=pltpu.VMEM)
    smem = pl.BlockSpec(memory_space=pltpu.SMEM)
    params = pltpu.CompilerParams(vmem_limit_bytes=48 * 2**20)
    cost = lambda flops, size: pl.CostEstimate(
        flops=flops, bytes_accessed=size, transcendentals=0
    )

    ints = integrals.reshape(slots, width, width)
    i3 = swap(ints, "blk", 3)
    i1 = swap(ints, "blk", 1)
    i2 = swap(i3, "blk", 1)

    top = nocc // LANES * part
    packed = pl.pallas_call(
        pack_kernel,
        out_shape=sds((top + META, LANES), BF16),
        in_specs=[vmem, vmem, pl.BlockSpec(memory_space=pltpu.HBM)],
        out_specs=vmem,
        scratch_shapes=[
            pltpu.VMEM((part, nocc), BF16),
            pltpu.VMEM((META, LANES), jnp.float32),
            pltpu.SemaphoreType.DMA,
        ],
        compiler_params=params,
        cost_estimate=cost(0, 4 * part * nocc),
    )(pair_codes[None], counts[None], coeff)
    c3 = swap(packed, "blk", 3)
    c1 = swap(packed, "blk", 1)
    c2 = swap(after(c3, i1), "blk", 1)
    early = after(jnp.stack([c1, c3]), i3)
    early2 = swap(early, "aux", 2)
    late2 = swap(c2, "aux", 2)
    early13 = swap(jnp.concatenate([early, early2]), "aux", 1)
    late13 = swap(after(jnp.stack([c2, late2]), i2), "aux", 1)
    notes = jnp.stack([c[top::8, :slots] for c in (packed, c1, c2, c3)]).astype(jnp.int32)

    full, overlap = pl.pallas_call(
        overlap_kernel,
        out_shape=(sds((nbf, nocc), BF16), sds((nbf, nbf), BF16)),
        in_specs=[vmem] * 7,
        out_specs=(vmem, vmem),
        compiler_params=params,
        cost_estimate=cost(2 * nbf * nbf * nocc, nbf * (nbf + 2 * nocc) * 2),
    )(coeff, early, c2, early2, late2, early13, late13)

    mine, p1, p2, p3 = pl.pallas_call(
        exchange_kernel,
        out_shape=(sds((part, nocc), jnp.float32),) + (sds((part, nocc), BF16),) * 3,
        in_specs=[smem] + [vmem] * 6,
        out_specs=(vmem,) * 4,
        scratch_shapes=[pltpu.VMEM((nbf, nbf), BF16), pltpu.VMEM((rows, nocc), jnp.float32)],
        compiler_params=params,
        cost_estimate=cost(2 * rows * nbf * (2 * nbf + nocc), nbf * (2 * nbf + nocc) * 2),
    )(notes, ints, i1, i2, i3, overlap, full)
    got = [swap(p, "aux", k) for k, p in ((2, p2), (3, p3), (1, p1))]
    return mine + got[0].astype(jnp.float32) + got[1].astype(jnp.float32) + got[2].astype(jnp.float32)


def local(integrals, pair_codes, counts, coeff):
    if lax.axis_size("blk") == 4 and lax.axis_size("aux") == 4:
        return local_line(integrals, pair_codes, counts, coeff)
    return local_long(integrals, pair_codes, counts, coeff)


def solution(mesh):
    in_specs = (
        P(("grp", "blk"), "aux", None, None),
        P(("grp", "blk")),
        P(("grp", "blk")),
        P(("grp", "blk"), None),
    )
    out_specs = P(("grp", "blk", "aux"), None)
    return jax.shard_map(local, mesh=mesh, in_specs=in_specs, out_specs=out_specs, check_vma=False)
```

```python
import functools

import jax
import jax.numpy as jnp
from jax import lax
from jax.experimental import pallas as pl
from jax.experimental.pallas import tpu as pltpu
from jax.sharding import PartitionSpec as P

BF16 = jnp.bfloat16
META = 16


def transform_slots(ints, columns, blocks):
    slots, paux, width, _ = ints.shape
    nocc = blocks.shape[2]

    def one_group(inputs):
        group_ints, group_cols = inputs
        chosen = blocks[group_cols]
        return jnp.einsum(
            "spml,sli->spmi", group_ints, chosen, preferred_element_type=jnp.float32
        ).astype(BF16)

    grouped = lax.map(
        one_group, (ints.reshape(slots // 8, 8, paux, width, width), columns.reshape(slots // 8, 8))
    )
    return grouped.reshape(slots, paux, width, nocc)


def local_long(integrals, pair_codes, counts, coeff):
    slots, paux, width, _ = integrals.shape
    nocc = coeff.shape[1]
    nblk = lax.axis_size("blk")
    per_dev = coeff.shape[0] // width
    cap = slots // nblk
    alive = (jnp.arange(cap)[None, :] < counts[:, None]).reshape(slots)
    masked = integrals * alive.astype(BF16)[:, None, None, None]
    local_blocks = coeff.reshape(per_dev, width, nocc)
    half = transform_slots(masked, pair_codes % per_dev, local_blocks)
    half_in, rows_in = (
        lax.all_to_all(half, "blk", split_axis=0, concat_axis=0, tiled=True),
        lax.all_to_all(pair_codes // per_dev, "blk", split_axis=0, concat_axis=0, tiled=True),
    )
    selector = (rows_in[:, None] == jnp.arange(per_dev, dtype=jnp.int32)[None, :]).astype(BF16)
    fitted = jnp.einsum("sk,spmi->pkmi", selector, half_in, preferred_element_type=jnp.float32)
    fitted = fitted.astype(BF16).reshape(paux, per_dev * width, nocc)
    partial_value = jnp.einsum(
        "nj,pni->pji", coeff, fitted, preferred_element_type=jnp.float32
    ).astype(BF16)
    occupied = lax.psum(partial_value.astype(jnp.float32).astype(BF16), "blk")
    return lax.psum_scatter(
        jnp.einsum("pnj,pji->ni", fitted, occupied, preferred_element_type=jnp.float32).astype(BF16),
        "aux",
        scatter_dimension=0,
        tiled=True,
    ).astype(jnp.float32)


LANES = 128


def after(x, *others):
    return lax.optimization_barrier((x, *others))[0]


def swap(x, axis, k):
    return lax.ppermute(x, axis, [(i, i ^ k) for i in range(4)])


def gray(k):
    return k ^ (k >> 1)


def pack_kernel(codes, counts, coeff, ints, out, first, second, quarter, note, sems):
    part, nocc = quarter.shape
    half = first.shape[0]
    z, a = lax.axis_index("blk"), lax.axis_index("aux")
    copies = (
        pltpu.make_async_copy(
            coeff.at[pl.ds(pl.multiple_of(a * part, part), part)], quarter, sems.at[0]
        ),
        pltpu.make_async_copy(ints.at[pl.ds((1 - z // 2) * half, half)], first, sems.at[1]),
        pltpu.make_async_copy(ints.at[pl.ds(z // 2 * half, half)], second, sems.at[2]),
    )
    for copy in copies:
        copy.start()
    note[...] = jnp.zeros_like(note)
    note[0:1, : codes.shape[1]] = codes[...].astype(jnp.float32)
    note[8:9, : counts.shape[1]] = counts[...].astype(jnp.float32)
    top = nocc // LANES * part
    out[top : top + META, :] = note[...].astype(BF16)
    copies[0].wait()
    for c in range(nocc // LANES):
        out[c * part : (c + 1) * part, :] = quarter[:, c * LANES : (c + 1) * LANES]
    copies[1].wait()
    copies[2].wait()


def gather_quarters(coeff, own, early, late, early2, late2, early13, late13):
    a = lax.axis_index("aux")
    rows, nocc = own.shape
    part = rows // 4
    coeff[:rows, :] = own[...]
    sources = (
        (0, early.at[0], late, early.at[1]),
        (1, early13.at[0], late13.at[0], early13.at[1]),
        (2, early2.at[0], late2, early2.at[1]),
        (3, early13.at[2], late13.at[1], early13.at[3]),
    )
    for j, *refs in sources:
        for k, ref in enumerate(refs, 1):
            at = pl.ds(pl.multiple_of(gray(k) * rows + (a ^ j) * part, part), part)
            for c in range(nocc // LANES):
                coeff[at, c * LANES : (c + 1) * LANES] = ref[c * part : (c + 1) * part, :]


def place(dense, ref, notes, k, side, top, left, rows, cap):
    z = lax.axis_index("blk")
    width = ref.shape[1]
    for s in range(ref.shape[0]):
        target = s // cap if side is None else (z // 2 ^ side) * 2 + s // cap
        code = notes[k, 0, target * cap + s % cap]

        @pl.when(s % cap < notes[k, 1, target])
        def _():
            row = gray(target ^ z) * rows + code // 2 * width - top
            col = left + code % 2 * width
            dense[
                pl.ds(pl.multiple_of(row, width), width),
                pl.ds(pl.multiple_of(col, width), width),
            ] = ref[s]


def dot(x, y):
    return jnp.dot(x, y, preferred_element_type=jnp.float32)


def most_kernel(notes, i0, i1, i3a, i3b, i2a, own, *refs):
    *quarters, left_out, part_out, coeff_out, total_out, coeff, dense, dense2 = refs
    rows = total_out.shape[0]
    cap = i0.shape[0] // 4
    three, two = 3 * rows, 2 * rows
    dense[...] = jnp.zeros_like(dense)
    dense2[...] = jnp.zeros_like(dense2)
    place(dense, i0, notes, 0, None, 0, 0, rows, cap)
    place(dense, i1, notes, 1, None, 0, rows, rows, cap)
    place(dense, i3a, notes, 3, 0, 0, two, rows, cap)
    place(dense, i3b, notes, 3, 1, 0, two, rows, cap)
    place(dense2, i2a, notes, 2, 0, 0, 0, rows, cap)
    gather_quarters(coeff, own, *quarters)
    coeff_out[...] = coeff[three:, :]
    fitted = dot(dense[:rows, :], coeff[:three, :]) + dot(dense2[:rows, :], coeff[three:, :])
    left = lax.dot_general(
        fitted.astype(BF16), coeff[...], (((1,), (1,)), ((), ())), preferred_element_type=jnp.float32
    ).astype(BF16)
    left_out[...] = left[:, two:]
    part_out[...] = dot(left[:, :two], dense2[...])
    total_out[...] = dot(dot(left, dense[...]).astype(BF16), coeff[:three, :])


def last_kernel(notes, i2b, left, part, total, coeff, mine, p1, p2, p3, dense2, whole):
    a = lax.axis_index("aux")
    rows = total.shape[0]
    dense2[...] = jnp.zeros_like(dense2)
    place(dense2, i2b, notes, 2, 1, 2 * rows, 0, rows, i2b.shape[0] // 2)
    last = (part[...] + dot(left[...], dense2[...])).astype(BF16)
    whole[...] = total[...] + dot(last, coeff[...])
    size = mine.shape[0]
    mine[...] = whole[pl.ds(pl.multiple_of(a * size, size), size), :]
    for j, out in enumerate((p1, p2, p3), 1):
        out[...] = whole[pl.ds(pl.multiple_of((a ^ j) * size, size), size), :].astype(BF16)


def local_line(integrals, pair_codes, counts, coeff):
    slots, _, width, _ = integrals.shape
    rows, nocc = coeff.shape
    part = rows // 4
    nbf = rows * 4
    sds = jax.ShapeDtypeStruct
    vmem = pl.BlockSpec(memory_space=pltpu.VMEM)
    smem = pl.BlockSpec(memory_space=pltpu.SMEM)
    params = pltpu.CompilerParams(vmem_limit_bytes=48 * 2**20)
    cost = lambda flops, size: pl.CostEstimate(
        flops=flops, bytes_accessed=size, transcendentals=0
    )

    ints = integrals.reshape(slots, width, width)
    half = slots // 2
    any_ = pl.BlockSpec(memory_space=pl.ANY)
    top = nocc // LANES * part
    packed, ia, ib = pl.pallas_call(
        pack_kernel,
        out_shape=(sds((top + META, LANES), BF16),) + (sds((half, width, width), BF16),) * 2,
        in_specs=[vmem, vmem, any_, any_],
        out_specs=(vmem, any_, any_),
        scratch_shapes=[
            pltpu.VMEM((part, nocc), BF16),
            pltpu.VMEM((META, LANES), jnp.float32),
            pltpu.SemaphoreType.DMA((3,)),
        ],
        compiler_params=pltpu.CompilerParams(vmem_limit_bytes=60 * 2**20),
        cost_estimate=cost(0, 4 * part * nocc + 4 * slots * width * width),
    )(pair_codes[None], counts[None], coeff, ints)

    i1 = swap(ints, "blk", 1)
    c3 = swap(packed, "blk", 3)
    c1 = swap(packed, "blk", 1)
    i3a = swap(ia, "blk", 3)
    i3b = swap(ib, "blk", 3)
    i2a = swap(i3a, "blk", 1)
    i2b = swap(i3b, "blk", 1)
    c2 = swap(after(c3, i1), "blk", 1)
    early = after(jnp.stack([c1, c3]), i1, i3a)
    early2 = swap(early, "aux", 2)
    late2 = swap(c2, "aux", 2)
    early13 = swap(after(jnp.concatenate([early, early2]), i3b, i2a), "aux", 1)
    late13 = swap(jnp.stack([c2, late2]), "aux", 1)
    notes = jnp.stack([c[top::8, :slots] for c in (packed, c1, c2, c3)]).astype(jnp.int32)

    left, some, coeff2, total = pl.pallas_call(
        most_kernel,
        out_shape=(
            sds((rows, 2 * rows), BF16),
            sds((rows, rows), jnp.float32),
            sds((rows, nocc), BF16),
            sds((rows, nocc), jnp.float32),
        ),
        in_specs=[smem] + [vmem] * 12,
        out_specs=(vmem,) * 4,
        scratch_shapes=[
            pltpu.VMEM((nbf, nocc), BF16),
            pltpu.VMEM((nbf, 3 * rows), BF16),
            pltpu.VMEM((2 * rows, rows), BF16),
        ],
        compiler_params=params,
        cost_estimate=cost(2 * rows * nbf * (3 * nocc + rows), nbf * nocc * 4),
    )(notes, ints, i1, i3a, i3b, i2a, coeff, early, c2, early2, late2, early13, late13)
    mine, p1, p2, p3 = pl.pallas_call(
        last_kernel,
        out_shape=(sds((part, nocc), jnp.float32),) + (sds((part, nocc), BF16),) * 3,
        in_specs=[smem] + [vmem] * 5,
        out_specs=(vmem,) * 4,
        scratch_shapes=[pltpu.VMEM((2 * rows, rows), BF16), pltpu.VMEM((rows, nocc), jnp.float32)],
        compiler_params=params,
        cost_estimate=cost(2 * rows * rows * (2 * rows + nocc), rows * nocc * 8),
    )(notes, i2b, left, some, total, coeff2)
    got = [swap(p, "aux", k) for k, p in ((2, p2), (3, p3), (1, p1))]
    return mine + got[0].astype(jnp.float32) + got[1].astype(jnp.float32) + got[2].astype(jnp.float32)


def local(integrals, pair_codes, counts, coeff):
    if lax.axis_size("blk") == 4 and lax.axis_size("aux") == 4:
        return local_line(integrals, pair_codes, counts, coeff)
    return local_long(integrals, pair_codes, counts, coeff)


def solution(mesh):
    in_specs = (
        P(("grp", "blk"), "aux", None, None),
        P(("grp", "blk")),
        P(("grp", "blk")),
        P(("grp", "blk"), None),
    )
    out_specs = P(("grp", "blk", "aux"), None)
    return jax.shard_map(local, mesh=mesh, in_specs=in_specs, out_specs=out_specs, check_vma=False)
```

```python
import functools

import jax
import jax.numpy as jnp
from jax import lax
from jax.experimental import pallas as pl
from jax.experimental.pallas import tpu as pltpu
from jax.sharding import PartitionSpec as P

BF16 = jnp.bfloat16
META = 16


def transform_slots(ints, columns, blocks):
    slots, paux, width, _ = ints.shape
    nocc = blocks.shape[2]

    def one_group(inputs):
        group_ints, group_cols = inputs
        chosen = blocks[group_cols]
        return jnp.einsum(
            "spml,sli->spmi", group_ints, chosen, preferred_element_type=jnp.float32
        ).astype(BF16)

    grouped = lax.map(
        one_group, (ints.reshape(slots // 8, 8, paux, width, width), columns.reshape(slots // 8, 8))
    )
    return grouped.reshape(slots, paux, width, nocc)


def local_long(integrals, pair_codes, counts, coeff):
    slots, paux, width, _ = integrals.shape
    nocc = coeff.shape[1]
    nblk = lax.axis_size("blk")
    per_dev = coeff.shape[0] // width
    cap = slots // nblk
    alive = (jnp.arange(cap)[None, :] < counts[:, None]).reshape(slots)
    masked = integrals * alive.astype(BF16)[:, None, None, None]
    local_blocks = coeff.reshape(per_dev, width, nocc)
    half = transform_slots(masked, pair_codes % per_dev, local_blocks)
    half_in, rows_in = (
        lax.all_to_all(half, "blk", split_axis=0, concat_axis=0, tiled=True),
        lax.all_to_all(pair_codes // per_dev, "blk", split_axis=0, concat_axis=0, tiled=True),
    )
    selector = (rows_in[:, None] == jnp.arange(per_dev, dtype=jnp.int32)[None, :]).astype(BF16)
    fitted = jnp.einsum("sk,spmi->pkmi", selector, half_in, preferred_element_type=jnp.float32)
    fitted = fitted.astype(BF16).reshape(paux, per_dev * width, nocc)
    partial_value = jnp.einsum(
        "nj,pni->pji", coeff, fitted, preferred_element_type=jnp.float32
    ).astype(BF16)
    occupied = lax.psum(partial_value.astype(jnp.float32).astype(BF16), "blk")
    return lax.psum_scatter(
        jnp.einsum("pnj,pji->ni", fitted, occupied, preferred_element_type=jnp.float32).astype(BF16),
        "aux",
        scatter_dimension=0,
        tiled=True,
    ).astype(jnp.float32)


LANES = 128


def after(x, *others):
    return lax.optimization_barrier((x, *others))[0]


def swap(x, axis, k):
    return lax.ppermute(x, axis, [(i, i ^ k) for i in range(4)])


def gray(k):
    return k ^ (k >> 1)


def pack_kernel(codes, counts, coeff, out, quarter, note, sem):
    part, nocc = quarter.shape
    a = lax.axis_index("aux")
    copy = pltpu.make_async_copy(
        coeff.at[pl.ds(pl.multiple_of(a * part, part), part)], quarter, sem
    )
    copy.start()
    note[...] = jnp.zeros_like(note)
    note[0:1, : codes.shape[1]] = codes[...].astype(jnp.float32)
    note[8:9, : counts.shape[1]] = counts[...].astype(jnp.float32)
    top = nocc // LANES * part
    out[top : top + META, :] = note[...].astype(BF16)
    copy.wait()
    for c in range(nocc // LANES):
        out[c * part : (c + 1) * part, :] = quarter[:, c * LANES : (c + 1) * LANES]


def gather_quarters(coeff, own, early, late, early2, late2, early13, late13):
    a = lax.axis_index("aux")
    rows, nocc = own.shape
    part = rows // 4
    coeff[:rows, :] = own[...]
    sources = (
        (0, early.at[0], late, early.at[1]),
        (1, early13.at[0], late13.at[0], early13.at[1]),
        (2, early2.at[0], late2, early2.at[1]),
        (3, early13.at[2], late13.at[1], early13.at[3]),
    )
    for j, *refs in sources:
        for k, ref in enumerate(refs, 1):
            at = pl.ds(pl.multiple_of(gray(k) * rows + (a ^ j) * part, part), part)
            for c in range(nocc // LANES):
                coeff[at, c * LANES : (c + 1) * LANES] = ref[c * part : (c + 1) * part, :]


def place(dense, ref, notes, k, rows):
    z = lax.axis_index("blk")
    slots, width, _ = ref.shape
    cap = slots // 4
    for s in range(slots):
        target = s // cap
        code = notes[k, 0, s]

        @pl.when(s % cap < notes[k, 1, target])
        def _():
            row = gray(target ^ z) * rows + code // 2 * width
            col = gray(k) * rows + code % 2 * width
            dense[
                pl.ds(pl.multiple_of(row, width), width),
                pl.ds(pl.multiple_of(col, width), width),
            ] = ref[s]


def dot(x, y):
    return jnp.dot(x, y, preferred_element_type=jnp.float32)


def exchange_kernel(notes, i0, i1, i2, i3, own, *refs):
    *quarters, mine, p1, p2, p3, coeff, dense, total = refs
    a = lax.axis_index("aux")
    rows = own.shape[0]
    dense[...] = jnp.zeros_like(dense)
    for k, ref in enumerate((i0, i1, i2, i3)):
        place(dense, ref, notes, k, rows)
    gather_quarters(coeff, own, *quarters)
    fitted = dot(dense[:rows, :], coeff[...]).astype(BF16)
    left = lax.dot_general(
        fitted, coeff[...], (((1,), (1,)), ((), ())), preferred_element_type=jnp.float32
    ).astype(BF16)
    total[...] = dot(dot(left, dense[...]).astype(BF16), coeff[...])
    size = mine.shape[0]
    mine[...] = total[pl.ds(pl.multiple_of(a * size, size), size), :]
    for j, out in enumerate((p1, p2, p3), 1):
        out[...] = total[pl.ds(pl.multiple_of((a ^ j) * size, size), size), :].astype(BF16)


def local_line(integrals, pair_codes, counts, coeff):
    slots, _, width, _ = integrals.shape
    rows, nocc = coeff.shape
    part = rows // 4
    nbf = rows * 4
    sds = jax.ShapeDtypeStruct
    vmem = pl.BlockSpec(memory_space=pltpu.VMEM)
    smem = pl.BlockSpec(memory_space=pltpu.SMEM)
    params = pltpu.CompilerParams(vmem_limit_bytes=48 * 2**20)
    cost = lambda flops, size: pl.CostEstimate(
        flops=flops, bytes_accessed=size, transcendentals=0
    )

    ints = integrals.reshape(slots, width, width)
    top = nocc // LANES * part
    packed = pl.pallas_call(
        pack_kernel,
        out_shape=sds((top + META, LANES), BF16),
        in_specs=[vmem, vmem, pl.BlockSpec(memory_space=pl.ANY)],
        out_specs=vmem,
        scratch_shapes=[
            pltpu.VMEM((part, nocc), BF16),
            pltpu.VMEM((META, LANES), jnp.float32),
            pltpu.SemaphoreType.DMA,
        ],
        compiler_params=pltpu.CompilerParams(vmem_limit_bytes=60 * 2**20),
        cost_estimate=cost(0, 4 * part * nocc),
    )(pair_codes[None], counts[None], coeff)

    i3 = swap(ints, "blk", 3)
    i1 = swap(ints, "blk", 1)
    i2 = swap(i3, "blk", 1)
    c3 = swap(packed, "blk", 3)
    c1 = swap(packed, "blk", 1)
    c2 = swap(after(c3, i3, i1), "blk", 1)
    early = after(jnp.stack([c1, c3]), i3, i1)
    early2 = swap(early, "aux", 2)
    late2 = swap(c2, "aux", 2)
    early13 = swap(jnp.concatenate([early, early2]), "aux", 1)
    late13 = swap(after(jnp.stack([c2, late2]), i2), "aux", 1)
    notes = jnp.stack([c[top::8, :slots] for c in (packed, c1, c2, c3)]).astype(jnp.int32)

    mine, p1, p2, p3 = pl.pallas_call(
        exchange_kernel,
        out_shape=(sds((part, nocc), jnp.float32),) + (sds((part, nocc), BF16),) * 3,
        in_specs=[smem] + [vmem] * 11,
        out_specs=(vmem,) * 4,
        scratch_shapes=[
            pltpu.VMEM((nbf, nocc), BF16),
            pltpu.VMEM((nbf, nbf), BF16),
            pltpu.VMEM((rows, nocc), jnp.float32),
        ],
        compiler_params=params,
        cost_estimate=cost(2 * rows * nbf * (3 * nocc + nbf), nbf * nocc * 4),
    )(notes, ints, i1, i2, i3, coeff, early, c2, early2, late2, early13, late13)
    got = [swap(p, "aux", k) for k, p in ((2, p2), (3, p3), (1, p1))]
    return mine + got[0].astype(jnp.float32) + got[1].astype(jnp.float32) + got[2].astype(jnp.float32)


def local(integrals, pair_codes, counts, coeff):
    if lax.axis_size("blk") == 4 and lax.axis_size("aux") == 4:
        return local_line(integrals, pair_codes, counts, coeff)
    return local_long(integrals, pair_codes, counts, coeff)


def solution(mesh):
    in_specs = (
        P(("grp", "blk"), "aux", None, None),
        P(("grp", "blk")),
        P(("grp", "blk")),
        P(("grp", "blk"), None),
    )
    out_specs = P(("grp", "blk", "aux"), None)
    return jax.shard_map(local, mesh=mesh, in_specs=in_specs, out_specs=out_specs, check_vma=False)
```

```python
import functools

import jax
import jax.numpy as jnp
from jax import lax
from jax.experimental import pallas as pl
from jax.experimental.pallas import tpu as pltpu
from jax.sharding import PartitionSpec as P

BF16 = jnp.bfloat16
META = 16


def transform_slots(ints, columns, blocks):
    slots, paux, width, _ = ints.shape
    nocc = blocks.shape[2]

    def one_group(inputs):
        group_ints, group_cols = inputs
        chosen = blocks[group_cols]
        return jnp.einsum(
            "spml,sli->spmi", group_ints, chosen, preferred_element_type=jnp.float32
        ).astype(BF16)

    grouped = lax.map(
        one_group, (ints.reshape(slots // 8, 8, paux, width, width), columns.reshape(slots // 8, 8))
    )
    return grouped.reshape(slots, paux, width, nocc)


def local_long(integrals, pair_codes, counts, coeff):
    slots, paux, width, _ = integrals.shape
    nocc = coeff.shape[1]
    nblk = lax.axis_size("blk")
    per_dev = coeff.shape[0] // width
    cap = slots // nblk
    alive = (jnp.arange(cap)[None, :] < counts[:, None]).reshape(slots)
    masked = integrals * alive.astype(BF16)[:, None, None, None]
    local_blocks = coeff.reshape(per_dev, width, nocc)
    half = transform_slots(masked, pair_codes % per_dev, local_blocks)
    half_in, rows_in = (
        lax.all_to_all(half, "blk", split_axis=0, concat_axis=0, tiled=True),
        lax.all_to_all(pair_codes // per_dev, "blk", split_axis=0, concat_axis=0, tiled=True),
    )
    selector = (rows_in[:, None] == jnp.arange(per_dev, dtype=jnp.int32)[None, :]).astype(BF16)
    fitted = jnp.einsum("sk,spmi->pkmi", selector, half_in, preferred_element_type=jnp.float32)
    fitted = fitted.astype(BF16).reshape(paux, per_dev * width, nocc)
    partial_value = jnp.einsum(
        "nj,pni->pji", coeff, fitted, preferred_element_type=jnp.float32
    ).astype(BF16)
    occupied = lax.psum(partial_value.astype(jnp.float32).astype(BF16), "blk")
    return lax.psum_scatter(
        jnp.einsum("pnj,pji->ni", fitted, occupied, preferred_element_type=jnp.float32).astype(BF16),
        "aux",
        scatter_dimension=0,
        tiled=True,
    ).astype(jnp.float32)


LANES = 128


def after(x, *others):
    return lax.optimization_barrier((x, *others))[0]


def swap(x, axis, k):
    return lax.ppermute(x, axis, [(i, i ^ k) for i in range(4)])


def gray(k):
    return k ^ (k >> 1)


def pack_kernel(codes, counts, coeff, out, quarter, note, sem):
    part, nocc = quarter.shape
    a = lax.axis_index("aux")
    copy = pltpu.make_async_copy(
        coeff.at[pl.ds(pl.multiple_of(a * part, part), part)], quarter, sem
    )
    copy.start()
    note[...] = jnp.zeros_like(note)
    note[0:1, : codes.shape[1]] = codes[...].astype(jnp.float32)
    note[8:9, : counts.shape[1]] = counts[...].astype(jnp.float32)
    top = nocc // LANES * part
    out[top : top + META, :] = note[...].astype(BF16)
    copy.wait()
    for c in range(nocc // LANES):
        out[c * part : (c + 1) * part, :] = quarter[:, c * LANES : (c + 1) * LANES]


def stage_kernel(c1, c3, early, onward):
    early[0] = c1[...]
    early[1] = c3[...]
    onward[...] = c3[...]


def copy_kernel(x, y):
    y[...] = x[...]


def gather_quarters(coeff, own, early, late, early2, late2, early13, late13):
    a = lax.axis_index("aux")
    rows, nocc = own.shape
    part = rows // 4
    coeff[:rows, :] = own[...]
    sources = (
        (0, early.at[0], late, early.at[1]),
        (1, early13.at[0], late13.at[0], early13.at[1]),
        (2, early2.at[0], late2, early2.at[1]),
        (3, early13.at[2], late13.at[1], early13.at[3]),
    )
    for j, *refs in sources:
        for k, ref in enumerate(refs, 1):
            at = pl.ds(pl.multiple_of(gray(k) * rows + (a ^ j) * part, part), part)
            for c in range(nocc // LANES):
                coeff[at, c * LANES : (c + 1) * LANES] = ref[c * part : (c + 1) * part, :]


def place(dense, ref, notes, k, left, rows):
    z = lax.axis_index("blk")
    slots, width, _ = ref.shape
    cap = slots // 4
    for s in range(slots):
        target = s // cap
        code = notes[k, 0, s]

        @pl.when(s % cap < notes[k, 1, target])
        def _():
            row = gray(target ^ z) * rows + code // 2 * width
            col = left + code % 2 * width
            dense[
                pl.ds(pl.multiple_of(row, width), width),
                pl.ds(pl.multiple_of(col, width), width),
            ] = ref[s]


def dot(x, y):
    return jnp.dot(x, y, preferred_element_type=jnp.float32)


def dot_t(x, y):
    return lax.dot_general(x, y, (((1,), (1,)), ((), ())), preferred_element_type=jnp.float32)


def first_kernel(notes, i0, i1, i3, own, *refs):
    *quarters, dense, coeff, left, overlap = refs
    rows = own.shape[0]
    dense[...] = jnp.zeros_like(dense)
    place(dense, i0, notes, 0, 0, rows)
    place(dense, i1, notes, 1, rows, rows)
    place(dense, i3, notes, 3, 2 * rows, rows)
    gather_quarters(coeff, own, *quarters)
    fitted = dot(dense[:rows, :], coeff[: 3 * rows, :]).astype(BF16)
    left[...] = dot_t(fitted, coeff[...])
    overlap[...] = dot_t(coeff[3 * rows :, :], coeff[...]).astype(BF16)


def last_kernel(notes, i2, dense, coeff, left, overlap, mine, p1, p2, p3, dense2, total):
    a = lax.axis_index("aux")
    rows = left.shape[0]
    dense2[...] = jnp.zeros_like(dense2)
    place(dense2, i2, notes, 2, 0, rows)
    whole = (left[...] + dot(dense2[:rows, :], overlap[...])).astype(BF16)
    total[...] = dot(dot(whole, dense[...]).astype(BF16), coeff[: 3 * rows, :]) + dot(
        dot(whole, dense2[...]).astype(BF16), coeff[3 * rows :, :]
    )
    size = mine.shape[0]
    mine[...] = total[pl.ds(pl.multiple_of(a * size, size), size), :]
    for j, out in enumerate((p1, p2, p3), 1):
        out[...] = total[pl.ds(pl.multiple_of((a ^ j) * size, size), size), :].astype(BF16)


def local_line(integrals, pair_codes, counts, coeff):
    slots, _, width, _ = integrals.shape
    rows, nocc = coeff.shape
    part = rows // 4
    nbf = rows * 4
    sds = jax.ShapeDtypeStruct
    vmem = pl.BlockSpec(memory_space=pltpu.VMEM)
    smem = pl.BlockSpec(memory_space=pltpu.SMEM)
    params = pltpu.CompilerParams(vmem_limit_bytes=20 * 2**20)
    cost = lambda flops, size: pl.CostEstimate(
        flops=flops, bytes_accessed=size, transcendentals=0
    )

    ahead = cost(4 * 10**10, nbf * nocc * 4)
    ints = integrals.reshape(slots, width, width)
    top = nocc // LANES * part
    packed = pl.pallas_call(
        pack_kernel,
        out_shape=sds((top + META, LANES), BF16),
        in_specs=[vmem, vmem, pl.BlockSpec(memory_space=pl.ANY)],
        out_specs=vmem,
        scratch_shapes=[
            pltpu.VMEM((part, nocc), BF16),
            pltpu.VMEM((META, LANES), jnp.float32),
            pltpu.SemaphoreType.DMA,
        ],
        compiler_params=pltpu.CompilerParams(vmem_limit_bytes=60 * 2**20),
        cost_estimate=cost(0, 4 * part * nocc),
    )(pair_codes[None], counts[None], coeff)

    stage = pl.pallas_call(
        stage_kernel,
        out_shape=(sds((2, top + META, LANES), BF16), sds((top + META, LANES), BF16)),
        in_specs=[vmem, vmem],
        out_specs=(vmem, vmem),
        compiler_params=params,
        cost_estimate=ahead,
    )
    stage2 = pl.pallas_call(
        copy_kernel,
        out_shape=(sds((top + META, LANES), BF16),),
        in_specs=[vmem],
        out_specs=(vmem,),
        compiler_params=params,
        cost_estimate=ahead,
    )
    c3 = swap(packed, "blk", 3)
    c1 = swap(packed, "blk", 1)
    i3 = swap(ints, "blk", 3)
    i1 = swap(ints, "blk", 1)
    early, onward = stage(c1, c3)
    c2 = swap(onward, "blk", 1)
    early2 = swap(early, "aux", 2)
    i2 = swap(i3, "blk", 1)
    late, = stage2(after(c2, i3, i1))
    late2 = swap(late, "aux", 2)
    early13 = swap(jnp.concatenate([early, early2]), "aux", 1)
    late13 = swap(jnp.stack([late, late2]), "aux", 1)
    notes = jnp.stack([c[top::8, :slots] for c in (packed, c1, c2, c3)]).astype(jnp.int32)

    dense, full, left, overlap = pl.pallas_call(
        first_kernel,
        out_shape=(
            sds((nbf, 3 * rows), BF16),
            sds((nbf, nocc), BF16),
            sds((rows, nbf), jnp.float32),
            sds((rows, nbf), BF16),
        ),
        in_specs=[smem] + [vmem] * 10,
        out_specs=(vmem,) * 4,
        compiler_params=params,
    )(notes, ints, i1, i3, coeff, early, late, early2, late2, early13, late13)
    mine, p1, p2, p3 = pl.pallas_call(
        last_kernel,
        out_shape=(sds((part, nocc), jnp.float32),) + (sds((part, nocc), BF16),) * 3,
        in_specs=[smem] + [vmem] * 5,
        out_specs=(vmem,) * 4,
        scratch_shapes=[pltpu.VMEM((nbf, rows), BF16), pltpu.VMEM((rows, nocc), jnp.float32)],
        compiler_params=params,
        cost_estimate=cost(2 * rows * nbf * (rows + nbf + nocc), nbf * nocc * 8),
    )(notes, i2, dense, full, left, overlap)
    got = [swap(p, "aux", k) for k, p in ((2, p2), (3, p3), (1, p1))]
    return mine + got[0].astype(jnp.float32) + got[1].astype(jnp.float32) + got[2].astype(jnp.float32)


def local(integrals, pair_codes, counts, coeff):
    if lax.axis_size("blk") == 4 and lax.axis_size("aux") == 4:
        return local_line(integrals, pair_codes, counts, coeff)
    return local_long(integrals, pair_codes, counts, coeff)


def solution(mesh):
    in_specs = (
        P(("grp", "blk"), "aux", None, None),
        P(("grp", "blk")),
        P(("grp", "blk")),
        P(("grp", "blk"), None),
    )
    out_specs = P(("grp", "blk", "aux"), None)
    return jax.shard_map(local, mesh=mesh, in_specs=in_specs, out_specs=out_specs, check_vma=False)
```

```python
import functools

import jax
import jax.numpy as jnp
from jax import lax
from jax.experimental import pallas as pl
from jax.experimental.pallas import tpu as pltpu
from jax.sharding import PartitionSpec as P

BF16 = jnp.bfloat16
META = 16


def transform_slots(ints, columns, blocks):
    slots, paux, width, _ = ints.shape
    nocc = blocks.shape[2]

    def one_group(inputs):
        group_ints, group_cols = inputs
        chosen = blocks[group_cols]
        return jnp.einsum(
            "spml,sli->spmi", group_ints, chosen, preferred_element_type=jnp.float32
        ).astype(BF16)

    grouped = lax.map(
        one_group, (ints.reshape(slots // 8, 8, paux, width, width), columns.reshape(slots // 8, 8))
    )
    return grouped.reshape(slots, paux, width, nocc)


def local_long(integrals, pair_codes, counts, coeff):
    slots, paux, width, _ = integrals.shape
    nocc = coeff.shape[1]
    nblk = lax.axis_size("blk")
    per_dev = coeff.shape[0] // width
    cap = slots // nblk
    alive = (jnp.arange(cap)[None, :] < counts[:, None]).reshape(slots)
    masked = integrals * alive.astype(BF16)[:, None, None, None]
    local_blocks = coeff.reshape(per_dev, width, nocc)
    half = transform_slots(masked, pair_codes % per_dev, local_blocks)
    half_in, rows_in = (
        lax.all_to_all(half, "blk", split_axis=0, concat_axis=0, tiled=True),
        lax.all_to_all(pair_codes // per_dev, "blk", split_axis=0, concat_axis=0, tiled=True),
    )
    selector = (rows_in[:, None] == jnp.arange(per_dev, dtype=jnp.int32)[None, :]).astype(BF16)
    fitted = jnp.einsum("sk,spmi->pkmi", selector, half_in, preferred_element_type=jnp.float32)
    fitted = fitted.astype(BF16).reshape(paux, per_dev * width, nocc)
    partial_value = jnp.einsum(
        "nj,pni->pji", coeff, fitted, preferred_element_type=jnp.float32
    ).astype(BF16)
    occupied = lax.psum(partial_value.astype(jnp.float32).astype(BF16), "blk")
    return lax.psum_scatter(
        jnp.einsum("pnj,pji->ni", fitted, occupied, preferred_element_type=jnp.float32).astype(BF16),
        "aux",
        scatter_dimension=0,
        tiled=True,
    ).astype(jnp.float32)


LANES = 128


def after(x, *others):
    return lax.optimization_barrier((x, *others))[0]


def swap(x, axis, k):
    return lax.ppermute(x, axis, [(i, i ^ k) for i in range(4)])


def gray(k):
    return k ^ (k >> 1)


def pack_kernel(codes, counts, coeff, out, quarter, note, sem):
    part, nocc = quarter.shape
    a = lax.axis_index("aux")
    copy = pltpu.make_async_copy(
        coeff.at[pl.ds(pl.multiple_of(a * part, part), part)], quarter, sem
    )
    copy.start()
    note[...] = jnp.zeros_like(note)
    note[0:1, : codes.shape[1]] = codes[...].astype(jnp.float32)
    note[8:9, : counts.shape[1]] = counts[...].astype(jnp.float32)
    top = nocc // LANES * part
    out[top : top + META, :] = note[...].astype(BF16)
    copy.wait()
    for c in range(nocc // LANES):
        out[c * part : (c + 1) * part, :] = quarter[:, c * LANES : (c + 1) * LANES]


def gather_quarters(coeff, at_k, refs):
    a = lax.axis_index("aux")
    part = (refs[0].shape[0] - META) * LANES // coeff.shape[1]
    for j, ref in enumerate(refs):
        at = pl.ds(pl.multiple_of(at_k * 4 * part + (a ^ j) * part, part), part)
        for c in range(coeff.shape[1] // LANES):
            coeff[at, c * LANES : (c + 1) * LANES] = ref[c * part : (c + 1) * part, :]


def place(dense, ref, notes, k, left, rows):
    z = lax.axis_index("blk")
    slots, width, _ = ref.shape
    cap = slots // 4
    for s in range(slots):
        target = s // cap
        code = notes[k, 0, s]

        @pl.when(s % cap < notes[k, 1, target])
        def _():
            row = gray(target ^ z) * rows + code // 2 * width
            col = left + code % 2 * width
            dense[
                pl.ds(pl.multiple_of(row, width), width),
                pl.ds(pl.multiple_of(col, width), width),
            ] = ref[s]


def dot(x, y):
    return jnp.dot(x, y, preferred_element_type=jnp.float32)


def dot_t(x, y):
    return lax.dot_general(x, y, (((1,), (1,)), ((), ())), preferred_element_type=jnp.float32)


def first_kernel(notes, i0, i1, i2, i3, own, early, early2, early13, dense, coeff, fitted):
    rows = own.shape[0]
    dense[...] = jnp.zeros_like(dense)
    for k, ref in enumerate((i0, i1, i2, i3)):
        place(dense, ref, notes, k, gray(k) * rows, rows)
    coeff[:rows, :] = own[...]
    for i, k in enumerate((1, 3)):
        gather_quarters(coeff, gray(k), (early.at[i], early13.at[i], early2.at[i], early13.at[2 + i]))
    fitted[...] = dot(dense[:rows, : 3 * rows], coeff[...])


def last_kernel(dense, coeff, fitted, late, late2, late13, mine, p1, p2, p3, last, total):
    a = lax.axis_index("aux")
    rows = fitted.shape[0]
    three = 3 * rows
    gather_quarters(last, 0, (late, late13.at[0], late2, late13.at[1]))
    whole = (fitted[...] + dot(dense[:rows, three:], last[...])).astype(BF16)
    left, left2 = dot_t(whole, coeff[...]).astype(BF16), dot_t(whole, last[...]).astype(BF16)
    both = (dot(left, dense[:three, :]) + dot(left2, dense[three:, :])).astype(BF16)
    total[...] = dot(both[:, :three], coeff[...]) + dot(both[:, three:], last[...])
    size = mine.shape[0]
    mine[...] = total[pl.ds(pl.multiple_of(a * size, size), size), :]
    for j, out in enumerate((p1, p2, p3), 1):
        out[...] = total[pl.ds(pl.multiple_of((a ^ j) * size, size), size), :].astype(BF16)


def local_line(integrals, pair_codes, counts, coeff):
    slots, _, width, _ = integrals.shape
    rows, nocc = coeff.shape
    part = rows // 4
    nbf = rows * 4
    sds = jax.ShapeDtypeStruct
    vmem = pl.BlockSpec(memory_space=pltpu.VMEM)
    smem = pl.BlockSpec(memory_space=pltpu.SMEM)
    params = pltpu.CompilerParams(vmem_limit_bytes=20 * 2**20)
    cost = lambda flops, size: pl.CostEstimate(
        flops=flops, bytes_accessed=size, transcendentals=0
    )

    ints = integrals.reshape(slots, width, width)
    top = nocc // LANES * part
    packed = pl.pallas_call(
        pack_kernel,
        out_shape=sds((top + META, LANES), BF16),
        in_specs=[vmem, vmem, pl.BlockSpec(memory_space=pl.ANY)],
        out_specs=vmem,
        scratch_shapes=[
            pltpu.VMEM((part, nocc), BF16),
            pltpu.VMEM((META, LANES), jnp.float32),
            pltpu.SemaphoreType.DMA,
        ],
        compiler_params=pltpu.CompilerParams(vmem_limit_bytes=60 * 2**20),
        cost_estimate=cost(0, 4 * part * nocc),
    )(pair_codes[None], counts[None], coeff)

    i3 = swap(ints, "blk", 3)
    i1 = swap(ints, "blk", 1)
    c3 = swap(packed, "blk", 3)
    c1 = swap(packed, "blk", 1)
    c2 = swap(after(c3, i3), "blk", 1)
    i2 = swap(i3, "blk", 1)
    early = jnp.stack([c1, c3])
    early2 = swap(early, "aux", 2)
    late2 = swap(after(c2, i1), "aux", 2)
    early13 = swap(after(jnp.concatenate([early, early2]), late2), "aux", 1)
    late13 = swap(after(jnp.stack([c2, late2]), i2), "aux", 1)
    notes = jnp.stack([c[top::8, :slots] for c in (packed, c1, c2, c3)]).astype(jnp.int32)

    dense, full, fitted = pl.pallas_call(
        first_kernel,
        out_shape=(
            sds((nbf, nbf), BF16),
            sds((3 * rows, nocc), BF16),
            sds((rows, nocc), jnp.float32),
        ),
        in_specs=[smem] + [vmem] * 8,
        out_specs=(vmem,) * 3,
        compiler_params=params,
        cost_estimate=cost(6 * rows * rows * nocc, nbf * nbf * 2),
    )(notes, ints, i1, i2, i3, coeff, early, early2, early13)
    mine, p1, p2, p3 = pl.pallas_call(
        last_kernel,
        out_shape=(sds((part, nocc), jnp.float32),) + (sds((part, nocc), BF16),) * 3,
        in_specs=[vmem] * 6,
        out_specs=(vmem,) * 4,
        scratch_shapes=[pltpu.VMEM((rows, nocc), BF16), pltpu.VMEM((rows, nocc), jnp.float32)],
        compiler_params=params,
        cost_estimate=cost(2 * rows * nbf * (2 * nocc + nbf), nbf * nocc * 8),
    )(dense, full, fitted, c2, late2, late13)
    got = [swap(p, "aux", k) for k, p in ((2, p2), (3, p3), (1, p1))]
    return mine + got[0].astype(jnp.float32) + got[1].astype(jnp.float32) + got[2].astype(jnp.float32)


def local(integrals, pair_codes, counts, coeff):
    if lax.axis_size("blk") == 4 and lax.axis_size("aux") == 4:
        return local_line(integrals, pair_codes, counts, coeff)
    return local_long(integrals, pair_codes, counts, coeff)


def solution(mesh):
    in_specs = (
        P(("grp", "blk"), "aux", None, None),
        P(("grp", "blk")),
        P(("grp", "blk")),
        P(("grp", "blk"), None),
    )
    out_specs = P(("grp", "blk", "aux"), None)
    return jax.shard_map(local, mesh=mesh, in_specs=in_specs, out_specs=out_specs, check_vma=False)
```

```python
import functools

import jax
import jax.numpy as jnp
from jax import lax
from jax.experimental import pallas as pl
from jax.experimental.pallas import tpu as pltpu
from jax.sharding import PartitionSpec as P

BF16 = jnp.bfloat16
META = 16


def transform_slots(ints, columns, blocks):
    slots, paux, width, _ = ints.shape
    nocc = blocks.shape[2]

    def one_group(inputs):
        group_ints, group_cols = inputs
        chosen = blocks[group_cols]
        return jnp.einsum(
            "spml,sli->spmi", group_ints, chosen, preferred_element_type=jnp.float32
        ).astype(BF16)

    grouped = lax.map(
        one_group, (ints.reshape(slots // 8, 8, paux, width, width), columns.reshape(slots // 8, 8))
    )
    return grouped.reshape(slots, paux, width, nocc)


def local_long(integrals, pair_codes, counts, coeff):
    slots, paux, width, _ = integrals.shape
    nocc = coeff.shape[1]
    nblk = lax.axis_size("blk")
    per_dev = coeff.shape[0] // width
    cap = slots // nblk
    alive = (jnp.arange(cap)[None, :] < counts[:, None]).reshape(slots)
    masked = integrals * alive.astype(BF16)[:, None, None, None]
    local_blocks = coeff.reshape(per_dev, width, nocc)
    half = transform_slots(masked, pair_codes % per_dev, local_blocks)
    half_in, rows_in = (
        lax.all_to_all(half, "blk", split_axis=0, concat_axis=0, tiled=True),
        lax.all_to_all(pair_codes // per_dev, "blk", split_axis=0, concat_axis=0, tiled=True),
    )
    selector = (rows_in[:, None] == jnp.arange(per_dev, dtype=jnp.int32)[None, :]).astype(BF16)
    fitted = jnp.einsum("sk,spmi->pkmi", selector, half_in, preferred_element_type=jnp.float32)
    fitted = fitted.astype(BF16).reshape(paux, per_dev * width, nocc)
    partial_value = jnp.einsum(
        "nj,pni->pji", coeff, fitted, preferred_element_type=jnp.float32
    ).astype(BF16)
    occupied = lax.psum(partial_value.astype(jnp.float32).astype(BF16), "blk")
    return lax.psum_scatter(
        jnp.einsum("pnj,pji->ni", fitted, occupied, preferred_element_type=jnp.float32).astype(BF16),
        "aux",
        scatter_dimension=0,
        tiled=True,
    ).astype(jnp.float32)


LANES = 128


def after(x, *others):
    return lax.optimization_barrier((x, *others))[0]


def swap(x, axis, k):
    return lax.ppermute(x, axis, [(i, i ^ k) for i in range(4)])


def gray(k):
    return k ^ (k >> 1)


def pack_kernel(codes, counts, coeff, out, quarter, note, code, count, sems):
    part, nocc = quarter.shape
    a = lax.axis_index("aux")
    copies = (
        pltpu.make_async_copy(
            coeff.at[pl.ds(pl.multiple_of(a * part, part), part)], quarter, sems.at[0]
        ),
        pltpu.make_async_copy(codes, code, sems.at[1]),
        pltpu.make_async_copy(counts, count, sems.at[2]),
    )
    for copy in copies:
        copy.start()
    note[...] = jnp.zeros_like(note)
    for copy in copies:
        copy.wait()
    note[0:1, : code.shape[1]] = code[...].astype(jnp.float32)
    note[8:9, : count.shape[1]] = count[...].astype(jnp.float32)
    top = nocc // LANES * part
    out[top : top + META, :] = note[...].astype(BF16)
    for c in range(nocc // LANES):
        out[c * part : (c + 1) * part, :] = quarter[:, c * LANES : (c + 1) * LANES]


def gather_quarters(coeff, at_k, refs):
    a = lax.axis_index("aux")
    part = (refs[0].shape[0] - META) * LANES // coeff.shape[1]
    for j, ref in enumerate(refs):
        at = pl.ds(pl.multiple_of(at_k * 4 * part + (a ^ j) * part, part), part)
        for c in range(coeff.shape[1] // LANES):
            coeff[at, c * LANES : (c + 1) * LANES] = ref[c * part : (c + 1) * part, :]


def place(dense, ref, notes, k, left, rows):
    z = lax.axis_index("blk")
    slots, width, _ = ref.shape
    cap = slots // 4
    for s in range(slots):
        target = s // cap
        code = notes[k, 0, s]

        @pl.when(s % cap < notes[k, 1, target])
        def _():
            row = gray(target ^ z) * rows + code // 2 * width
            col = left + code % 2 * width
            dense[
                pl.ds(pl.multiple_of(row, width), width),
                pl.ds(pl.multiple_of(col, width), width),
            ] = ref[s]


def dot(x, y):
    return jnp.dot(x, y, preferred_element_type=jnp.float32)


def dot_t(x, y):
    return lax.dot_general(x, y, (((1,), (1,)), ((), ())), preferred_element_type=jnp.float32)


def first_kernel(notes, i0, i1, i3, own, early, early2, early13, dense, coeff, fitted):
    rows = own.shape[0]
    dense[...] = jnp.zeros_like(dense)
    for k, ref in ((0, i0), (1, i1), (3, i3)):
        place(dense, ref, notes, k, gray(k) * rows, rows)
    coeff[:rows, :] = own[...]
    for i, k in enumerate((1, 3)):
        gather_quarters(coeff, gray(k), (early.at[i], early13.at[i], early2.at[i], early13.at[2 + i]))
    fitted[...] = dot(dense[:rows, :], coeff[...])


def chain(fitted, dense, dense2, coeff, coeff2):
    three = coeff.shape[0]
    left, left2 = dot_t(fitted, coeff[...]).astype(BF16), dot_t(fitted, coeff2[...]).astype(BF16)
    most = dot(left, dense[:three, :]) + dot(left2, dense[three:, :])
    last = dot(left, dense2[:three, :]) + dot(left2, dense2[three:, :])
    return dot(most.astype(BF16), coeff[...]) + dot(last.astype(BF16), coeff2[...])


def far_kernel(notes, i2, dense, coeff, early_fitted, late, late2, late13, p2, p3, dense2, coeff2, fitted, total):
    a = lax.axis_index("aux")
    rows = coeff2.shape[0]
    dense2[...] = jnp.zeros_like(dense2)
    place(dense2, i2, notes, 2, 0, rows)
    gather_quarters(coeff2, 0, (late, late13.at[0], late2, late13.at[1]))
    total[...] = early_fitted[...] + dot(dense2[:rows, :], coeff2[...])
    half, part = rows // 2, rows // 4
    fitted[...] = total[pl.ds(pl.multiple_of(a // 2 * half, half), half), :].astype(BF16)
    far = total[pl.ds(pl.multiple_of((1 - a // 2) * half, half), half), :].astype(BF16)
    total[:half, :] = chain(far, dense, dense2, coeff, coeff2)
    for j, out in ((2, p2), (3, p3)):
        out[...] = total[pl.ds(pl.multiple_of((a ^ j) % 2 * part, part), part), :].astype(BF16)


def near_kernel(fitted, dense, dense2, coeff, coeff2, mine, p1, total):
    a = lax.axis_index("aux")
    part = mine.shape[0]
    total[...] = chain(fitted[...], dense, dense2, coeff, coeff2)
    mine[...] = total[pl.ds(pl.multiple_of(a % 2 * part, part), part), :]
    p1[...] = total[pl.ds(pl.multiple_of((a ^ 1) % 2 * part, part), part), :].astype(BF16)


def local_line(integrals, pair_codes, counts, coeff):
    slots, _, width, _ = integrals.shape
    rows, nocc = coeff.shape
    part = rows // 4
    nbf = rows * 4
    sds = jax.ShapeDtypeStruct
    vmem = pl.BlockSpec(memory_space=pltpu.VMEM)
    smem = pl.BlockSpec(memory_space=pltpu.SMEM)
    params = pltpu.CompilerParams(vmem_limit_bytes=20 * 2**20)
    cost = lambda flops, size: pl.CostEstimate(
        flops=flops, bytes_accessed=size, transcendentals=0
    )

    ints = integrals.reshape(slots, width, width)
    top = nocc // LANES * part
    packed = pl.pallas_call(
        pack_kernel,
        out_shape=sds((top + META, LANES), BF16),
        in_specs=[pl.BlockSpec(memory_space=pl.ANY)] * 3,
        out_specs=vmem,
        scratch_shapes=[
            pltpu.VMEM((part, nocc), BF16),
            pltpu.VMEM((META, LANES), jnp.float32),
            pltpu.VMEM((1, slots), jnp.int32),
            pltpu.VMEM((1, counts.shape[0]), jnp.int32),
            pltpu.SemaphoreType.DMA((3,)),
        ],
        compiler_params=pltpu.CompilerParams(vmem_limit_bytes=60 * 2**20),
        cost_estimate=cost(0, 4 * part * nocc),
    )(pair_codes[None], counts[None], coeff)

    i3 = swap(ints, "blk", 3)
    i1 = swap(ints, "blk", 1)
    c3 = swap(packed, "blk", 3)
    c1 = swap(packed, "blk", 1)
    c2 = swap(after(c3, i3, i1), "blk", 1)
    i2 = swap(i3, "blk", 1)
    early = after(jnp.stack([c1, c3]), i3)
    early2 = swap(early, "aux", 2)
    late2 = swap(c2, "aux", 2)
    early13 = swap(after(jnp.concatenate([early, early2]), c2), "aux", 1)
    notes = jnp.stack([c[top::8, :slots] for c in (packed, c1, c2, c3)]).astype(jnp.int32)
    dense, full, fitted = pl.pallas_call(
        first_kernel,
        out_shape=(
            sds((nbf, 3 * rows), BF16),
            sds((3 * rows, nocc), BF16),
            sds((rows, nocc), jnp.float32),
        ),
        in_specs=[smem] + [vmem] * 7,
        out_specs=(vmem,) * 3,
        compiler_params=params,
    )(notes, ints, i1, i3, coeff, early, early2, early13)
    late13 = swap(after(jnp.stack([c2, late2]), i2, notes), "aux", 1)
    half = rows // 2
    p2, p3, dense2, coeff2, near = pl.pallas_call(
        far_kernel,
        out_shape=(sds((part, nocc), BF16),) * 2
        + (sds((nbf, rows), BF16), sds((rows, nocc), BF16), sds((half, nocc), BF16)),
        in_specs=[smem] + [vmem] * 7,
        out_specs=(vmem,) * 5,
        scratch_shapes=[pltpu.VMEM((rows, nocc), jnp.float32)],
        compiler_params=params,
        cost_estimate=cost(2 * half * nbf * (2 * nocc + nbf), nbf * nocc * 8),
    )(notes, i2, dense, full, fitted, c2, late2, late13)
    mine, p1 = pl.pallas_call(
        near_kernel,
        out_shape=(sds((part, nocc), jnp.float32), sds((part, nocc), BF16)),
        in_specs=[vmem] * 5,
        out_specs=(vmem,) * 2,
        scratch_shapes=[pltpu.VMEM((half, nocc), jnp.float32)],
        compiler_params=params,
        cost_estimate=cost(2 * half * nbf * (2 * nocc + nbf), nbf * nocc * 8),
    )(near, dense, dense2, full, coeff2)
    got2, got3, got1 = swap(p2, "aux", 2), swap(p3, "aux", 3), swap(p1, "aux", 1)
    others = after(got2.astype(jnp.float32) + got3.astype(jnp.float32), mine)
    return mine + got1.astype(jnp.float32) + others


def local(integrals, pair_codes, counts, coeff):
    if lax.axis_size("blk") == 4 and lax.axis_size("aux") == 4:
        return local_line(integrals, pair_codes, counts, coeff)
    return local_long(integrals, pair_codes, counts, coeff)


def solution(mesh):
    in_specs = (
        P(("grp", "blk"), "aux", None, None),
        P(("grp", "blk")),
        P(("grp", "blk")),
        P(("grp", "blk"), None),
    )
    out_specs = P(("grp", "blk", "aux"), None)
    return jax.shard_map(local, mesh=mesh, in_specs=in_specs, out_specs=out_specs, check_vma=False)
```

```python
import functools

import jax
import jax.numpy as jnp
from jax import lax
from jax.experimental import pallas as pl
from jax.experimental.pallas import tpu as pltpu
from jax.sharding import PartitionSpec as P

BF16 = jnp.bfloat16
META = 16


def transform_slots(ints, columns, blocks):
    slots, paux, width, _ = ints.shape
    nocc = blocks.shape[2]

    def one_group(inputs):
        group_ints, group_cols = inputs
        chosen = blocks[group_cols]
        return jnp.einsum(
            "spml,sli->spmi", group_ints, chosen, preferred_element_type=jnp.float32
        ).astype(BF16)

    grouped = lax.map(
        one_group, (ints.reshape(slots // 8, 8, paux, width, width), columns.reshape(slots // 8, 8))
    )
    return grouped.reshape(slots, paux, width, nocc)


def local_long(integrals, pair_codes, counts, coeff):
    slots, paux, width, _ = integrals.shape
    nocc = coeff.shape[1]
    nblk = lax.axis_size("blk")
    per_dev = coeff.shape[0] // width
    cap = slots // nblk
    alive = (jnp.arange(cap)[None, :] < counts[:, None]).reshape(slots)
    masked = integrals * alive.astype(BF16)[:, None, None, None]
    local_blocks = coeff.reshape(per_dev, width, nocc)
    half = transform_slots(masked, pair_codes % per_dev, local_blocks)
    half_in, rows_in = (
        lax.all_to_all(half, "blk", split_axis=0, concat_axis=0, tiled=True),
        lax.all_to_all(pair_codes // per_dev, "blk", split_axis=0, concat_axis=0, tiled=True),
    )
    selector = (rows_in[:, None] == jnp.arange(per_dev, dtype=jnp.int32)[None, :]).astype(BF16)
    fitted = jnp.einsum("sk,spmi->pkmi", selector, half_in, preferred_element_type=jnp.float32)
    fitted = fitted.astype(BF16).reshape(paux, per_dev * width, nocc)
    partial_value = jnp.einsum(
        "nj,pni->pji", coeff, fitted, preferred_element_type=jnp.float32
    ).astype(BF16)
    occupied = lax.psum(partial_value.astype(jnp.float32).astype(BF16), "blk")
    return lax.psum_scatter(
        jnp.einsum("pnj,pji->ni", fitted, occupied, preferred_element_type=jnp.float32).astype(BF16),
        "aux",
        scatter_dimension=0,
        tiled=True,
    ).astype(jnp.float32)


LANES = 128


def after(x, *others):
    return lax.optimization_barrier((x, *others))[0]


def swap(x, axis, k):
    return lax.ppermute(x, axis, [(i, i ^ k) for i in range(4)])


def gray(k):
    return k ^ (k >> 1)


def pack_kernel(codes, counts, coeff, out, quarter, note, code, count, sems):
    part, nocc = quarter.shape
    a = lax.axis_index("aux")
    copies = (
        pltpu.make_async_copy(
            coeff.at[pl.ds(pl.multiple_of(a * part, part), part)], quarter, sems.at[0]
        ),
        pltpu.make_async_copy(codes, code, sems.at[1]),
        pltpu.make_async_copy(counts, count, sems.at[2]),
    )
    for copy in copies:
        copy.start()
    note[...] = jnp.zeros_like(note)
    for copy in copies:
        copy.wait()
    note[0:1, : code.shape[1]] = code[...].astype(jnp.float32)
    note[8:9, : count.shape[1]] = count[...].astype(jnp.float32)
    top = nocc // LANES * part
    out[top : top + META, :] = note[...].astype(BF16)
    for c in range(nocc // LANES):
        out[c * part : (c + 1) * part, :] = quarter[:, c * LANES : (c + 1) * LANES]


def stage_kernel(c1, c3, early, onward):
    early[0] = c1[...]
    early[1] = c3[...]
    onward[...] = c3[...]


def copy_kernel(x, y):
    y[...] = x[...]


def gather_quarters(coeff, at_k, refs):
    a = lax.axis_index("aux")
    part = (refs[0].shape[0] - META) * LANES // coeff.shape[1]
    for j, ref in enumerate(refs):
        at = pl.ds(pl.multiple_of(at_k * 4 * part + (a ^ j) * part, part), part)
        for c in range(coeff.shape[1] // LANES):
            coeff[at, c * LANES : (c + 1) * LANES] = ref[c * part : (c + 1) * part, :]


def place(dense, ref, notes, k, left, rows):
    z = lax.axis_index("blk")
    slots, width, _ = ref.shape
    cap = slots // 4
    for s in range(slots):
        target = s // cap
        code = notes[k, 0, s]

        @pl.when(s % cap < notes[k, 1, target])
        def _():
            row = gray(target ^ z) * rows + code // 2 * width
            col = left + code % 2 * width
            dense[
                pl.ds(pl.multiple_of(row, width), width),
                pl.ds(pl.multiple_of(col, width), width),
            ] = ref[s]


def dot(x, y):
    return jnp.dot(x, y, preferred_element_type=jnp.float32)


def dot_t(x, y):
    return lax.dot_general(x, y, (((1,), (1,)), ((), ())), preferred_element_type=jnp.float32)


def first_kernel(notes, i0, i1, i3, own, *refs):
    early, late, early2, late2, early13, late13, dense, coeff, left, overlap = refs
    rows = own.shape[0]
    three = 3 * rows
    dense[...] = jnp.zeros_like(dense)
    for k, ref in ((0, i0), (1, i1), (3, i3)):
        place(dense, ref, notes, k, gray(k) * rows, rows)
    coeff[:rows, :] = own[...]
    for i, k in enumerate((1, 3)):
        gather_quarters(coeff, gray(k), (early.at[i], early13.at[i], early2.at[i], early13.at[2 + i]))
    gather_quarters(coeff, gray(2), (late, late13.at[0], late2, late13.at[1]))
    fitted = dot(dense[:rows, :], coeff[:three, :]).astype(BF16)
    left[...] = dot_t(fitted, coeff[...])
    overlap[...] = dot_t(coeff[three:, :], coeff[...]).astype(BF16)


def chain(left, dense, dense2, coeff):
    three = dense.shape[1]
    most, last = dot(left, dense[...]).astype(BF16), dot(left, dense2[...]).astype(BF16)
    return dot(most, coeff[:three, :]) + dot(last, coeff[three:, :])


def far_kernel(notes, i2, dense, coeff, left, overlap, p2, p3, dense2, total):
    a = lax.axis_index("aux")
    rows = left.shape[0]
    half, part = rows // 2, rows // 4
    dense2[...] = jnp.zeros_like(dense2)
    place(dense2, i2, notes, 2, 0, rows)
    far = pl.ds(pl.multiple_of((1 - a // 2) * half, half), half)
    whole = left[far, :] + dot(dense2[far, :], overlap[...])
    total[...] = chain(whole.astype(BF16), dense, dense2, coeff)
    for j, out in ((2, p2), (3, p3)):
        out[...] = total[pl.ds(pl.multiple_of((a ^ j) % 2 * part, part), part), :].astype(BF16)


def near_kernel(dense2, dense, coeff, left, overlap, mine, p1, total):
    a = lax.axis_index("aux")
    part = mine.shape[0]
    near = pl.ds(pl.multiple_of(a // 2 * 2 * part, 2 * part), 2 * part)
    whole = left[near, :] + dot(dense2[near, :], overlap[...])
    total[...] = chain(whole.astype(BF16), dense, dense2, coeff)
    mine[...] = total[pl.ds(pl.multiple_of(a % 2 * part, part), part), :]
    p1[...] = total[pl.ds(pl.multiple_of((a ^ 1) % 2 * part, part), part), :].astype(BF16)


def local_line(integrals, pair_codes, counts, coeff):
    slots, _, width, _ = integrals.shape
    rows, nocc = coeff.shape
    part = rows // 4
    nbf = rows * 4
    sds = jax.ShapeDtypeStruct
    vmem = pl.BlockSpec(memory_space=pltpu.VMEM)
    smem = pl.BlockSpec(memory_space=pltpu.SMEM)
    params = pltpu.CompilerParams(vmem_limit_bytes=20 * 2**20)
    cost = lambda flops, size: pl.CostEstimate(
        flops=flops, bytes_accessed=size, transcendentals=0
    )

    ints = integrals.reshape(slots, width, width)
    top = nocc // LANES * part
    packed = pl.pallas_call(
        pack_kernel,
        out_shape=sds((top + META, LANES), BF16),
        in_specs=[pl.BlockSpec(memory_space=pl.ANY)] * 3,
        out_specs=vmem,
        scratch_shapes=[
            pltpu.VMEM((part, nocc), BF16),
            pltpu.VMEM((META, LANES), jnp.float32),
            pltpu.VMEM((1, slots), jnp.int32),
            pltpu.VMEM((1, counts.shape[0]), jnp.int32),
            pltpu.SemaphoreType.DMA((3,)),
        ],
        compiler_params=pltpu.CompilerParams(vmem_limit_bytes=60 * 2**20),
        cost_estimate=cost(0, 4 * part * nocc),
    )(pair_codes[None], counts[None], coeff)

    ahead = cost(4 * 10**10, nbf * nocc * 4)
    quarter = sds((top + META, LANES), BF16)
    stage = pl.pallas_call(
        stage_kernel,
        out_shape=(sds((2, top + META, LANES), BF16), quarter),
        in_specs=[vmem, vmem],
        out_specs=(vmem, vmem),
        compiler_params=params,
        cost_estimate=ahead,
    )
    hold = pl.pallas_call(
        copy_kernel,
        out_shape=quarter,
        in_specs=[vmem],
        out_specs=vmem,
        compiler_params=params,
        cost_estimate=ahead,
    )
    c3 = swap(packed, "blk", 3)
    c1 = swap(packed, "blk", 1)
    i1 = swap(ints, "blk", 1)
    early, onward = stage(c1, c3)
    c2 = swap(onward, "blk", 1)
    early2 = swap(early, "aux", 2)
    i3 = swap(after(ints, onward), "blk", 3)
    i2 = swap(i3, "blk", 1)
    late = hold(after(c2, i1))
    late2 = swap(late, "aux", 2)
    early13 = swap(jnp.concatenate([early, early2]), "aux", 1)
    late13 = swap(jnp.stack([late, late2]), "aux", 1)
    notes = jnp.stack([c[top::8, :slots] for c in (packed, c1, late, c3)]).astype(jnp.int32)

    dense, full, left, overlap = pl.pallas_call(
        first_kernel,
        out_shape=(
            sds((nbf, 3 * rows), BF16),
            sds((nbf, nocc), BF16),
            sds((rows, nbf), jnp.float32),
            sds((rows, nbf), BF16),
        ),
        in_specs=[smem] + [vmem] * 10,
        out_specs=(vmem,) * 4,
        compiler_params=params,
    )(notes, ints, i1, i3, coeff, early, late, early2, late2, early13, late13)
    half = rows // 2
    p2, p3, dense2 = pl.pallas_call(
        far_kernel,
        out_shape=(sds((part, nocc), BF16),) * 2 + (sds((nbf, rows), BF16),),
        in_specs=[smem] + [vmem] * 5,
        out_specs=(vmem,) * 3,
        scratch_shapes=[pltpu.VMEM((half, nocc), jnp.float32)],
        compiler_params=params,
        cost_estimate=cost(2 * half * nbf * (rows + nbf + nocc), nbf * nocc * 8),
    )(notes, i2, dense, full, left, overlap)
    mine, p1 = pl.pallas_call(
        near_kernel,
        out_shape=(sds((part, nocc), jnp.float32), sds((part, nocc), BF16)),
        in_specs=[vmem] * 5,
        out_specs=(vmem,) * 2,
        scratch_shapes=[pltpu.VMEM((half, nocc), jnp.float32)],
        compiler_params=params,
        cost_estimate=cost(2 * half * nbf * (rows + nbf + nocc), nbf * nocc * 8),
    )(dense2, dense, full, left, overlap)
    got2, got3, got1 = swap(p2, "aux", 2), swap(p3, "aux", 3), swap(p1, "aux", 1)
    others = after(got2.astype(jnp.float32) + got3.astype(jnp.float32), mine)
    return mine + got1.astype(jnp.float32) + others


def local(integrals, pair_codes, counts, coeff):
    if lax.axis_size("blk") == 4 and lax.axis_size("aux") == 4:
        return local_line(integrals, pair_codes, counts, coeff)
    return local_long(integrals, pair_codes, counts, coeff)


def solution(mesh):
    in_specs = (
        P(("grp", "blk"), "aux", None, None),
        P(("grp", "blk")),
        P(("grp", "blk")),
        P(("grp", "blk"), None),
    )
    out_specs = P(("grp", "blk", "aux"), None)
    return jax.shard_map(local, mesh=mesh, in_specs=in_specs, out_specs=out_specs, check_vma=False)
```

```python
import functools

import jax
import jax.numpy as jnp
from jax import lax
from jax.experimental import pallas as pl
from jax.experimental.pallas import tpu as pltpu
from jax.sharding import PartitionSpec as P

BF16 = jnp.bfloat16
META = 16


def transform_slots(ints, columns, blocks):
    slots, paux, width, _ = ints.shape
    nocc = blocks.shape[2]

    def one_group(inputs):
        group_ints, group_cols = inputs
        chosen = blocks[group_cols]
        return jnp.einsum(
            "spml,sli->spmi", group_ints, chosen, preferred_element_type=jnp.float32
        ).astype(BF16)

    grouped = lax.map(
        one_group, (ints.reshape(slots // 8, 8, paux, width, width), columns.reshape(slots // 8, 8))
    )
    return grouped.reshape(slots, paux, width, nocc)


def local_long(integrals, pair_codes, counts, coeff):
    slots, paux, width, _ = integrals.shape
    nocc = coeff.shape[1]
    nblk = lax.axis_size("blk")
    per_dev = coeff.shape[0] // width
    cap = slots // nblk
    alive = (jnp.arange(cap)[None, :] < counts[:, None]).reshape(slots)
    masked = integrals * alive.astype(BF16)[:, None, None, None]
    local_blocks = coeff.reshape(per_dev, width, nocc)
    half = transform_slots(masked, pair_codes % per_dev, local_blocks)
    half_in, rows_in = (
        lax.all_to_all(half, "blk", split_axis=0, concat_axis=0, tiled=True),
        lax.all_to_all(pair_codes // per_dev, "blk", split_axis=0, concat_axis=0, tiled=True),
    )
    selector = (rows_in[:, None] == jnp.arange(per_dev, dtype=jnp.int32)[None, :]).astype(BF16)
    fitted = jnp.einsum("sk,spmi->pkmi", selector, half_in, preferred_element_type=jnp.float32)
    fitted = fitted.astype(BF16).reshape(paux, per_dev * width, nocc)
    partial_value = jnp.einsum(
        "nj,pni->pji", coeff, fitted, preferred_element_type=jnp.float32
    ).astype(BF16)
    occupied = lax.psum(partial_value.astype(jnp.float32).astype(BF16), "blk")
    return lax.psum_scatter(
        jnp.einsum("pnj,pji->ni", fitted, occupied, preferred_element_type=jnp.float32).astype(BF16),
        "aux",
        scatter_dimension=0,
        tiled=True,
    ).astype(jnp.float32)


LANES = 128


def after(x, *others):
    return lax.optimization_barrier((x, *others))[0]


def swap(x, axis, k):
    return lax.ppermute(x, axis, [(i, i ^ k) for i in range(4)])


def gray(k):
    return k ^ (k >> 1)


def pack_kernel(codes, counts, coeff, out, quarter, note, code, count, sems):
    part, nocc = quarter.shape
    a = lax.axis_index("aux")
    copies = (
        pltpu.make_async_copy(
            coeff.at[pl.ds(pl.multiple_of(a * part, part), part)], quarter, sems.at[0]
        ),
        pltpu.make_async_copy(codes, code, sems.at[1]),
        pltpu.make_async_copy(counts, count, sems.at[2]),
    )
    for copy in copies:
        copy.start()
    note[...] = jnp.zeros_like(note)
    for copy in copies:
        copy.wait()
    note[0:1, : code.shape[1]] = code[...].astype(jnp.float32)
    note[8:9, : count.shape[1]] = count[...].astype(jnp.float32)
    top = nocc // LANES * part
    out[top : top + META, :] = note[...].astype(BF16)
    for c in range(nocc // LANES):
        out[c * part : (c + 1) * part, :] = quarter[:, c * LANES : (c + 1) * LANES]


def stack_kernel(x, y, both):
    both[0] = x[...]
    both[1] = y[...]


def copy_kernel(x, y):
    y[...] = x[...]


def gather_quarters(coeff, at_k, refs):
    a = lax.axis_index("aux")
    part = (refs[0].shape[0] - META) * LANES // coeff.shape[1]
    for j, ref in enumerate(refs):
        at = pl.ds(pl.multiple_of(at_k * 4 * part + (a ^ j) * part, part), part)
        for c in range(coeff.shape[1] // LANES):
            coeff[at, c * LANES : (c + 1) * LANES] = ref[c * part : (c + 1) * part, :]


def place(dense, ref, notes, k, left, rows):
    z = lax.axis_index("blk")
    slots, width, _ = ref.shape
    cap = slots // 4
    for s in range(slots):
        target = s // cap
        code = notes[k, 0, s]

        @pl.when(s % cap < notes[k, 1, target])
        def _():
            row = gray(target ^ z) * rows + code // 2 * width
            col = left + code % 2 * width
            dense[
                pl.ds(pl.multiple_of(row, width), width),
                pl.ds(pl.multiple_of(col, width), width),
            ] = ref[s]


def dot(x, y):
    return jnp.dot(x, y, preferred_element_type=jnp.float32)


def dot_t(x, y):
    return lax.dot_general(x, y, (((1,), (1,)), ((), ())), preferred_element_type=jnp.float32)


def first_kernel(notes, i0, i1, i3, own, *refs):
    early, late, early2, late2, early13, late13, dense, coeff, left, overlap = refs
    rows = own.shape[0]
    three = 3 * rows
    dense[...] = jnp.zeros_like(dense)
    for k, ref in ((0, i0), (1, i1), (3, i3)):
        place(dense, ref, notes, k, gray(k) * rows, rows)
    coeff[:rows, :] = own[...]
    for i, k in enumerate((1, 3)):
        gather_quarters(coeff, gray(k), (early.at[i], early13.at[i], early2.at[i], early13.at[2 + i]))
    gather_quarters(coeff, gray(2), (late, late13.at[0], late2, late13.at[1]))
    fitted = dot(dense[:rows, :], coeff[:three, :]).astype(BF16)
    left[...] = dot_t(fitted, coeff[...])
    overlap[...] = dot_t(coeff[three:, :], coeff[...]).astype(BF16)


def chain(left, dense, dense2, coeff):
    three = dense.shape[1]
    most, last = dot(left, dense[...]).astype(BF16), dot(left, dense2[...]).astype(BF16)
    return dot(most, coeff[:three, :]) + dot(last, coeff[three:, :])


def far_kernel(notes, i2, dense, coeff, left, overlap, p2, p3, dense2, total):
    a = lax.axis_index("aux")
    rows = left.shape[0]
    half, part = rows // 2, rows // 4
    dense2[...] = jnp.zeros_like(dense2)
    place(dense2, i2, notes, 2, 0, rows)
    far = pl.ds(pl.multiple_of((1 - a // 2) * half, half), half)
    whole = left[far, :] + dot(dense2[far, :], overlap[...])
    total[...] = chain(whole.astype(BF16), dense, dense2, coeff)
    for j, out in ((2, p2), (3, p3)):
        out[...] = total[pl.ds(pl.multiple_of((a ^ j) % 2 * part, part), part), :].astype(BF16)


def near_kernel(dense2, dense, coeff, left, overlap, mine, p1, total):
    a = lax.axis_index("aux")
    part = mine.shape[0]
    near = pl.ds(pl.multiple_of(a // 2 * 2 * part, 2 * part), 2 * part)
    whole = left[near, :] + dot(dense2[near, :], overlap[...])
    total[...] = chain(whole.astype(BF16), dense, dense2, coeff)
    mine[...] = total[pl.ds(pl.multiple_of(a % 2 * part, part), part), :]
    p1[...] = total[pl.ds(pl.multiple_of((a ^ 1) % 2 * part, part), part), :].astype(BF16)


def local_line(integrals, pair_codes, counts, coeff):
    slots, _, width, _ = integrals.shape
    rows, nocc = coeff.shape
    part = rows // 4
    nbf = rows * 4
    sds = jax.ShapeDtypeStruct
    vmem = pl.BlockSpec(memory_space=pltpu.VMEM)
    smem = pl.BlockSpec(memory_space=pltpu.SMEM)
    params = pltpu.CompilerParams(vmem_limit_bytes=20 * 2**20)
    cost = lambda flops, size: pl.CostEstimate(
        flops=flops, bytes_accessed=size, transcendentals=0
    )

    ints = integrals.reshape(slots, width, width)
    top = nocc // LANES * part
    packed = pl.pallas_call(
        pack_kernel,
        out_shape=sds((top + META, LANES), BF16),
        in_specs=[pl.BlockSpec(memory_space=pl.ANY)] * 3,
        out_specs=vmem,
        scratch_shapes=[
            pltpu.VMEM((part, nocc), BF16),
            pltpu.VMEM((META, LANES), jnp.float32),
            pltpu.VMEM((1, slots), jnp.int32),
            pltpu.VMEM((1, counts.shape[0]), jnp.int32),
            pltpu.SemaphoreType.DMA((3,)),
        ],
        compiler_params=pltpu.CompilerParams(vmem_limit_bytes=60 * 2**20),
        cost_estimate=cost(0, 4 * part * nocc),
    )(pair_codes[None], counts[None], coeff)

    ahead = cost(4 * 10**10, nbf * nocc * 4)
    quarter = sds((top + META, LANES), BF16)
    stack = pl.pallas_call(
        stack_kernel,
        out_shape=sds((2, top + META, LANES), BF16),
        in_specs=[vmem, vmem],
        out_specs=vmem,
        compiler_params=params,
        cost_estimate=ahead,
    )
    hold = pl.pallas_call(
        copy_kernel,
        out_shape=quarter,
        in_specs=[vmem],
        out_specs=vmem,
        compiler_params=params,
        cost_estimate=ahead,
    )
    c3 = swap(packed, "blk", 3)
    c1 = swap(packed, "blk", 1)
    i1 = swap(ints, "blk", 1)
    onward = hold(c3)
    c2 = swap(onward, "blk", 1)
    i3 = swap(after(ints, onward), "blk", 3)
    early = stack(c1, after(onward, i1))
    early2 = swap(early, "aux", 2)
    i2 = swap(i3, "blk", 1)
    late = hold(after(c2, i1))
    late2 = swap(late, "aux", 2)
    early13 = swap(jnp.concatenate([early, early2]), "aux", 1)
    late13 = swap(jnp.stack([late, late2]), "aux", 1)
    notes = jnp.stack([c[top::8, :slots] for c in (packed, c1, late, c3)]).astype(jnp.int32)

    dense, full, left, overlap = pl.pallas_call(
        first_kernel,
        out_shape=(
            sds((nbf, 3 * rows), BF16),
            sds((nbf, nocc), BF16),
            sds((rows, nbf), jnp.float32),
            sds((rows, nbf), BF16),
        ),
        in_specs=[smem] + [vmem] * 10,
        out_specs=(vmem,) * 4,
        compiler_params=params,
    )(notes, ints, i1, i3, coeff, early, late, early2, late2, early13, late13)
    half = rows // 2
    p2, p3, dense2 = pl.pallas_call(
        far_kernel,
        out_shape=(sds((part, nocc), BF16),) * 2 + (sds((nbf, rows), BF16),),
        in_specs=[smem] + [vmem] * 5,
        out_specs=(vmem,) * 3,
        scratch_shapes=[pltpu.VMEM((half, nocc), jnp.float32)],
        compiler_params=params,
        cost_estimate=cost(2 * half * nbf * (rows + nbf + nocc), nbf * nocc * 8),
    )(notes, i2, dense, full, left, overlap)
    mine, p1 = pl.pallas_call(
        near_kernel,
        out_shape=(sds((part, nocc), jnp.float32), sds((part, nocc), BF16)),
        in_specs=[vmem] * 5,
        out_specs=(vmem,) * 2,
        scratch_shapes=[pltpu.VMEM((half, nocc), jnp.float32)],
        compiler_params=params,
        cost_estimate=cost(2 * half * nbf * (rows + nbf + nocc), nbf * nocc * 8),
    )(dense2, dense, full, left, overlap)
    got2, got3, got1 = swap(p2, "aux", 2), swap(p3, "aux", 3), swap(p1, "aux", 1)
    others = after(got2.astype(jnp.float32) + got3.astype(jnp.float32), mine)
    return mine + got1.astype(jnp.float32) + others


def local(integrals, pair_codes, counts, coeff):
    if lax.axis_size("blk") == 4 and lax.axis_size("aux") == 4:
        return local_line(integrals, pair_codes, counts, coeff)
    return local_long(integrals, pair_codes, counts, coeff)


def solution(mesh):
    in_specs = (
        P(("grp", "blk"), "aux", None, None),
        P(("grp", "blk")),
        P(("grp", "blk")),
        P(("grp", "blk"), None),
    )
    out_specs = P(("grp", "blk", "aux"), None)
    return jax.shard_map(local, mesh=mesh, in_specs=in_specs, out_specs=out_specs, check_vma=False)
```

```python
import functools

import jax
import jax.numpy as jnp
from jax import lax
from jax.experimental import pallas as pl
from jax.experimental.pallas import tpu as pltpu
from jax.sharding import PartitionSpec as P

BF16 = jnp.bfloat16
META = 16


def transform_slots(ints, columns, blocks):
    slots, paux, width, _ = ints.shape
    nocc = blocks.shape[2]

    def one_group(inputs):
        group_ints, group_cols = inputs
        chosen = blocks[group_cols]
        return jnp.einsum(
            "spml,sli->spmi", group_ints, chosen, preferred_element_type=jnp.float32
        ).astype(BF16)

    grouped = lax.map(
        one_group, (ints.reshape(slots // 8, 8, paux, width, width), columns.reshape(slots // 8, 8))
    )
    return grouped.reshape(slots, paux, width, nocc)


def local_long(integrals, pair_codes, counts, coeff):
    slots, paux, width, _ = integrals.shape
    nocc = coeff.shape[1]
    nblk = lax.axis_size("blk")
    per_dev = coeff.shape[0] // width
    cap = slots // nblk
    alive = (jnp.arange(cap)[None, :] < counts[:, None]).reshape(slots)
    masked = integrals * alive.astype(BF16)[:, None, None, None]
    local_blocks = coeff.reshape(per_dev, width, nocc)
    half = transform_slots(masked, pair_codes % per_dev, local_blocks)
    half_in, rows_in = (
        lax.all_to_all(half, "blk", split_axis=0, concat_axis=0, tiled=True),
        lax.all_to_all(pair_codes // per_dev, "blk", split_axis=0, concat_axis=0, tiled=True),
    )
    selector = (rows_in[:, None] == jnp.arange(per_dev, dtype=jnp.int32)[None, :]).astype(BF16)
    fitted = jnp.einsum("sk,spmi->pkmi", selector, half_in, preferred_element_type=jnp.float32)
    fitted = fitted.astype(BF16).reshape(paux, per_dev * width, nocc)
    partial_value = jnp.einsum(
        "nj,pni->pji", coeff, fitted, preferred_element_type=jnp.float32
    ).astype(BF16)
    occupied = lax.psum(partial_value.astype(jnp.float32).astype(BF16), "blk")
    return lax.psum_scatter(
        jnp.einsum("pnj,pji->ni", fitted, occupied, preferred_element_type=jnp.float32).astype(BF16),
        "aux",
        scatter_dimension=0,
        tiled=True,
    ).astype(jnp.float32)


LANES = 128


def after(x, *others):
    return lax.optimization_barrier((x, *others))[0]


def swap(x, axis, k):
    return lax.ppermute(x, axis, [(i, i ^ k) for i in range(4)])


def gray(k):
    return k ^ (k >> 1)


def pack_kernel(codes, counts, coeff, out, quarter, note, code, count, sems):
    part, nocc = quarter.shape
    a = lax.axis_index("aux")
    copies = (
        pltpu.make_async_copy(
            coeff.at[pl.ds(pl.multiple_of(a * part, part), part)], quarter, sems.at[0]
        ),
        pltpu.make_async_copy(codes, code, sems.at[1]),
        pltpu.make_async_copy(counts, count, sems.at[2]),
    )
    for copy in copies:
        copy.start()
    note[...] = jnp.zeros_like(note)
    for copy in copies:
        copy.wait()
    note[0:1, : code.shape[1]] = code[...].astype(jnp.float32)
    note[8:9, : count.shape[1]] = count[...].astype(jnp.float32)
    top = nocc // LANES * part
    out[top : top + META, :] = note[...].astype(BF16)
    for c in range(nocc // LANES):
        out[c * part : (c + 1) * part, :] = quarter[:, c * LANES : (c + 1) * LANES]


def stack_kernel(x, y, both):
    both[0] = x[...]
    both[1] = y[...]


def copy_kernel(x, y):
    y[...] = x[...]


def gather_quarters(coeff, at_k, refs):
    a = lax.axis_index("aux")
    part = (refs[0].shape[0] - META) * LANES // coeff.shape[1]
    for j, ref in enumerate(refs):
        at = pl.ds(pl.multiple_of(at_k * 4 * part + (a ^ j) * part, part), part)
        for c in range(coeff.shape[1] // LANES):
            coeff[at, c * LANES : (c + 1) * LANES] = ref[c * part : (c + 1) * part, :]


def place(dense, ref, notes, k, left, rows):
    z = lax.axis_index("blk")
    slots, width, _ = ref.shape
    cap = slots // 4
    for s in range(slots):
        target = s // cap
        code = notes[k, 0, s]

        @pl.when(s % cap < notes[k, 1, target])
        def _():
            row = gray(target ^ z) * rows + code // 2 * width
            col = left + code % 2 * width
            dense[
                pl.ds(pl.multiple_of(row, width), width),
                pl.ds(pl.multiple_of(col, width), width),
            ] = ref[s]


def dot(x, y):
    return jnp.dot(x, y, preferred_element_type=jnp.float32)


def dot_t(x, y):
    return lax.dot_general(x, y, (((1,), (1,)), ((), ())), preferred_element_type=jnp.float32)


def early_kernel(notes, i0, i1, own, early, late, early2, late2, early13, late13, dense, coeff, overlap):
    rows = own.shape[0]
    dense[...] = jnp.zeros_like(dense)
    place(dense, i0, notes, 0, 0, rows)
    place(dense, i1, notes, 1, rows, rows)
    coeff[:rows, :] = own[...]
    for i, k in enumerate((1, 3)):
        gather_quarters(coeff, gray(k), (early.at[i], early13.at[i], early2.at[i], early13.at[2 + i]))
    gather_quarters(coeff, gray(2), (late, late13.at[0], late2, late13.at[1]))
    overlap[...] = dot_t(coeff[3 * rows :, :], coeff[...]).astype(BF16)


def first_kernel(notes, i3, dense, coeff, overlap, left, ahead, total, dense3, fitted):
    rows = overlap.shape[0]
    two, three = 2 * rows, 3 * rows
    dense3[...] = jnp.zeros_like(dense3)
    place(dense3, i3, notes, 3, 0, rows)
    for at in range(0, 4 * rows, rows):
        part = pl.ds(at, rows)
        fitted[part, :] = (
            dot(dense[part, :], coeff[:two, :]) + dot(dense3[part, :], coeff[two:three, :])
        ).astype(BF16)
    left[...] = dot_t(fitted[:rows, :], coeff[...])
    total[...] = dot(left[...].astype(BF16), fitted[...])
    ahead[...] = dot(overlap[...], fitted[...]).astype(BF16)


def last_kernel(notes, i2, coeff, left, overlap, ahead, early_total, mine, p1, p2, p3, dense2, total):
    a = lax.axis_index("aux")
    rows = left.shape[0]
    dense2[...] = jnp.zeros_like(dense2)
    place(dense2, i2, notes, 2, 0, rows)
    here = dense2[:rows, :]
    whole = (left[...] + dot(here, overlap[...])).astype(BF16)
    last = dot(whole, dense2[...]).astype(BF16)
    total[...] = early_total[...] + dot(here, ahead[...]) + dot(last, coeff[3 * rows :, :])
    size = mine.shape[0]
    mine[...] = total[pl.ds(pl.multiple_of(a * size, size), size), :]
    for j, out in enumerate((p1, p2, p3), 1):
        out[...] = total[pl.ds(pl.multiple_of((a ^ j) * size, size), size), :].astype(BF16)


def local_line(integrals, pair_codes, counts, coeff):
    slots, _, width, _ = integrals.shape
    rows, nocc = coeff.shape
    part = rows // 4
    nbf = rows * 4
    sds = jax.ShapeDtypeStruct
    vmem = pl.BlockSpec(memory_space=pltpu.VMEM)
    smem = pl.BlockSpec(memory_space=pltpu.SMEM)
    params = pltpu.CompilerParams(vmem_limit_bytes=20 * 2**20)
    cost = lambda flops, size: pl.CostEstimate(
        flops=flops, bytes_accessed=size, transcendentals=0
    )

    ints = integrals.reshape(slots, width, width)
    top = nocc // LANES * part
    packed = pl.pallas_call(
        pack_kernel,
        out_shape=sds((top + META, LANES), BF16),
        in_specs=[pl.BlockSpec(memory_space=pl.ANY)] * 3,
        out_specs=vmem,
        scratch_shapes=[
            pltpu.VMEM((part, nocc), BF16),
            pltpu.VMEM((META, LANES), jnp.float32),
            pltpu.VMEM((1, slots), jnp.int32),
            pltpu.VMEM((1, counts.shape[0]), jnp.int32),
            pltpu.SemaphoreType.DMA((3,)),
        ],
        compiler_params=pltpu.CompilerParams(vmem_limit_bytes=60 * 2**20),
        cost_estimate=cost(0, 4 * part * nocc),
    )(pair_codes[None], counts[None], coeff)

    ahead = cost(4 * 10**10, nbf * nocc * 4)
    quarter = sds((top + META, LANES), BF16)
    stack = pl.pallas_call(
        stack_kernel,
        out_shape=sds((2, top + META, LANES), BF16),
        in_specs=[vmem, vmem],
        out_specs=vmem,
        compiler_params=params,
        cost_estimate=ahead,
    )
    hold = pl.pallas_call(
        copy_kernel,
        out_shape=quarter,
        in_specs=[vmem],
        out_specs=vmem,
        compiler_params=params,
        cost_estimate=ahead,
    )
    c3 = swap(packed, "blk", 3)
    c1 = swap(packed, "blk", 1)
    i1 = swap(ints, "blk", 1)
    onward = hold(c3)
    c2 = swap(onward, "blk", 1)
    early = stack(c1, c3)
    early2 = swap(early, "aux", 2)
    i3 = swap(after(ints, onward), "blk", 3)
    late = hold(after(c2, i1))
    late2 = swap(late, "aux", 2)
    early13 = swap(jnp.concatenate([early, early2]), "aux", 1)
    notes = jnp.stack([c[top::8, :slots] for c in (packed, c1, late, c3)]).astype(jnp.int32)
    late13 = swap(after(jnp.stack([late, late2]), notes), "aux", 1)

    f32 = jnp.float32
    dense, full, overlap = pl.pallas_call(
        early_kernel,
        out_shape=(sds((nbf, 2 * rows), BF16), sds((nbf, nocc), BF16), sds((rows, nbf), BF16)),
        in_specs=[smem] + [vmem] * 9,
        out_specs=(vmem,) * 3,
        compiler_params=params,
    )(notes, ints, i1, coeff, early, late, early2, late2, early13, late13)
    i2 = swap(after(i3, overlap), "blk", 1)
    left, ahead2, total = pl.pallas_call(
        first_kernel,
        out_shape=(sds((rows, nbf), f32), sds((rows, nocc), BF16), sds((rows, nocc), f32)),
        in_specs=[smem] + [vmem] * 4,
        out_specs=(vmem,) * 3,
        scratch_shapes=[pltpu.VMEM((nbf, rows), BF16), pltpu.VMEM((nbf, nocc), BF16)],
        compiler_params=params,
    )(notes, i3, dense, full, overlap)
    mine, p1, p2, p3 = pl.pallas_call(
        last_kernel,
        out_shape=(sds((part, nocc), f32),) + (sds((part, nocc), BF16),) * 3,
        in_specs=[smem] + [vmem] * 6,
        out_specs=(vmem,) * 4,
        scratch_shapes=[pltpu.VMEM((nbf, rows), BF16), pltpu.VMEM((rows, nocc), f32)],
        compiler_params=params,
        cost_estimate=cost(2 * rows * rows * (2 * nbf + 2 * nocc), nbf * nocc * 4),
    )(notes, i2, full, left, overlap, ahead2, total)
    got = [swap(p, "aux", k) for k, p in ((2, p2), (3, p3), (1, p1))]
    return mine + got[0].astype(f32) + got[1].astype(f32) + got[2].astype(f32)


def local(integrals, pair_codes, counts, coeff):
    if lax.axis_size("blk") == 4 and lax.axis_size("aux") == 4:
        return local_line(integrals, pair_codes, counts, coeff)
    return local_long(integrals, pair_codes, counts, coeff)


def solution(mesh):
    in_specs = (
        P(("grp", "blk"), "aux", None, None),
        P(("grp", "blk")),
        P(("grp", "blk")),
        P(("grp", "blk"), None),
    )
    out_specs = P(("grp", "blk", "aux"), None)
    return jax.shard_map(local, mesh=mesh, in_specs=in_specs, out_specs=out_specs, check_vma=False)
```

```python
import functools

import jax
import jax.numpy as jnp
from jax import lax
from jax.experimental import pallas as pl
from jax.experimental.pallas import tpu as pltpu
from jax.sharding import PartitionSpec as P

BF16 = jnp.bfloat16
META = 16


def transform_slots(ints, columns, blocks):
    slots, paux, width, _ = ints.shape
    nocc = blocks.shape[2]

    def one_group(inputs):
        group_ints, group_cols = inputs
        chosen = blocks[group_cols]
        return jnp.einsum(
            "spml,sli->spmi", group_ints, chosen, preferred_element_type=jnp.float32
        ).astype(BF16)

    grouped = lax.map(
        one_group, (ints.reshape(slots // 8, 8, paux, width, width), columns.reshape(slots // 8, 8))
    )
    return grouped.reshape(slots, paux, width, nocc)


def local_long(integrals, pair_codes, counts, coeff):
    slots, paux, width, _ = integrals.shape
    nocc = coeff.shape[1]
    nblk = lax.axis_size("blk")
    per_dev = coeff.shape[0] // width
    cap = slots // nblk
    alive = (jnp.arange(cap)[None, :] < counts[:, None]).reshape(slots)
    masked = integrals * alive.astype(BF16)[:, None, None, None]
    local_blocks = coeff.reshape(per_dev, width, nocc)
    half = transform_slots(masked, pair_codes % per_dev, local_blocks)
    half_in, rows_in = (
        lax.all_to_all(half, "blk", split_axis=0, concat_axis=0, tiled=True),
        lax.all_to_all(pair_codes // per_dev, "blk", split_axis=0, concat_axis=0, tiled=True),
    )
    selector = (rows_in[:, None] == jnp.arange(per_dev, dtype=jnp.int32)[None, :]).astype(BF16)
    fitted = jnp.einsum("sk,spmi->pkmi", selector, half_in, preferred_element_type=jnp.float32)
    fitted = fitted.astype(BF16).reshape(paux, per_dev * width, nocc)
    partial_value = jnp.einsum(
        "nj,pni->pji", coeff, fitted, preferred_element_type=jnp.float32
    ).astype(BF16)
    occupied = lax.psum(partial_value.astype(jnp.float32).astype(BF16), "blk")
    return lax.psum_scatter(
        jnp.einsum("pnj,pji->ni", fitted, occupied, preferred_element_type=jnp.float32).astype(BF16),
        "aux",
        scatter_dimension=0,
        tiled=True,
    ).astype(jnp.float32)


LANES = 128


def after(x, *others):
    return lax.optimization_barrier((x, *others))[0]


def swap(x, axis, k):
    return lax.ppermute(x, axis, [(i, i ^ k) for i in range(4)])


def gray(k):
    return k ^ (k >> 1)


def pack_kernel(codes, counts, coeff, out, quarter, note, code, count, sems):
    part, nocc = quarter.shape
    a = lax.axis_index("aux")
    copies = (
        pltpu.make_async_copy(
            coeff.at[pl.ds(pl.multiple_of(a * part, part), part)], quarter, sems.at[0]
        ),
        pltpu.make_async_copy(codes, code, sems.at[1]),
        pltpu.make_async_copy(counts, count, sems.at[2]),
    )
    for copy in copies:
        copy.start()
    note[...] = jnp.zeros_like(note)
    for copy in copies:
        copy.wait()
    note[0:1, : code.shape[1]] = code[...].astype(jnp.float32)
    note[8:9, : count.shape[1]] = count[...].astype(jnp.float32)
    top = nocc // LANES * part
    out[top : top + META, :] = note[...].astype(BF16)
    for c in range(nocc // LANES):
        out[c * part : (c + 1) * part, :] = quarter[:, c * LANES : (c + 1) * LANES]


def stack_kernel(x, y, both):
    both[0] = x[...]
    both[1] = y[...]


def copy_kernel(x, y):
    y[...] = x[...]


def gather_quarters(coeff, at_k, refs):
    a = lax.axis_index("aux")
    part = (refs[0].shape[0] - META) * LANES // coeff.shape[1]
    for j, ref in enumerate(refs):
        at = pl.ds(pl.multiple_of(at_k * 4 * part + (a ^ j) * part, part), part)
        for c in range(coeff.shape[1] // LANES):
            coeff[at, c * LANES : (c + 1) * LANES] = ref[c * part : (c + 1) * part, :]


def place(dense, ref, notes, k, left, rows):
    z = lax.axis_index("blk")
    slots, width, _ = ref.shape
    cap = slots // 4
    for s in range(slots):
        target = s // cap
        code = notes[k, 0, s]

        @pl.when(s % cap < notes[k, 1, target])
        def _():
            row = gray(target ^ z) * rows + code // 2 * width
            col = left + code % 2 * width
            dense[
                pl.ds(pl.multiple_of(row, width), width),
                pl.ds(pl.multiple_of(col, width), width),
            ] = ref[s]


def dot(x, y):
    return jnp.dot(x, y, preferred_element_type=jnp.float32)


def dot_t(x, y):
    return lax.dot_general(x, y, (((1,), (1,)), ((), ())), preferred_element_type=jnp.float32)


def first_kernel(notes, i0, i1, i3, own, *refs):
    early, late, early2, late2, early13, late13, dense, coeff, left, overlap = refs
    rows = own.shape[0]
    three = 3 * rows
    dense[...] = jnp.zeros_like(dense)
    for k, ref in ((0, i0), (1, i1), (3, i3)):
        place(dense, ref, notes, k, gray(k) * rows, rows)
    coeff[:rows, :] = own[...]
    for i, k in enumerate((1, 3)):
        gather_quarters(coeff, gray(k), (early.at[i], early13.at[i], early2.at[i], early13.at[2 + i]))
    gather_quarters(coeff, gray(2), (late, late13.at[0], late2, late13.at[1]))
    fitted = dot(dense[:rows, :], coeff[:three, :]).astype(BF16)
    left[...] = dot_t(fitted, coeff[...])
    overlap[...] = dot_t(coeff[three:, :], coeff[...]).astype(BF16)


def chain(left, dense, dense2, coeff):
    three = dense.shape[1]
    most, last = dot(left, dense[...]).astype(BF16), dot(left, dense2[...]).astype(BF16)
    return dot(most, coeff[:three, :]) + dot(last, coeff[three:, :])


def far_kernel(notes, i2, dense, coeff, left, overlap, p2, p3, dense2, total):
    a = lax.axis_index("aux")
    rows = left.shape[0]
    half, part = rows // 2, rows // 4
    dense2[...] = jnp.zeros_like(dense2)
    place(dense2, i2, notes, 2, 0, rows)
    far = pl.ds(pl.multiple_of((1 - a // 2) * half, half), half)
    whole = left[far, :] + dot(dense2[far, :], overlap[...])
    total[...] = chain(whole.astype(BF16), dense, dense2, coeff)
    for j, out in ((2, p2), (3, p3)):
        out[...] = total[pl.ds(pl.multiple_of((a ^ j) % 2 * part, part), part), :].astype(BF16)


def near_kernel(dense2, dense, coeff, left, overlap, mine, p1, total):
    a = lax.axis_index("aux")
    part = mine.shape[0]
    near = pl.ds(pl.multiple_of(a // 2 * 2 * part, 2 * part), 2 * part)
    whole = left[near, :] + dot(dense2[near, :], overlap[...])
    total[...] = chain(whole.astype(BF16), dense, dense2, coeff)
    mine[...] = total[pl.ds(pl.multiple_of(a % 2 * part, part), part), :]
    p1[...] = total[pl.ds(pl.multiple_of((a ^ 1) % 2 * part, part), part), :].astype(BF16)


def local_line(integrals, pair_codes, counts, coeff):
    slots, _, width, _ = integrals.shape
    rows, nocc = coeff.shape
    part = rows // 4
    nbf = rows * 4
    sds = jax.ShapeDtypeStruct
    vmem = pl.BlockSpec(memory_space=pltpu.VMEM)
    smem = pl.BlockSpec(memory_space=pltpu.SMEM)
    params = pltpu.CompilerParams(vmem_limit_bytes=20 * 2**20)
    cost = lambda flops, size: pl.CostEstimate(
        flops=flops, bytes_accessed=size, transcendentals=0
    )

    ints = integrals.reshape(slots, width, width)
    top = nocc // LANES * part
    packed = pl.pallas_call(
        pack_kernel,
        out_shape=sds((top + META, LANES), BF16),
        in_specs=[pl.BlockSpec(memory_space=pl.ANY)] * 3,
        out_specs=vmem,
        scratch_shapes=[
            pltpu.VMEM((part, nocc), BF16),
            pltpu.VMEM((META, LANES), jnp.float32),
            pltpu.VMEM((1, slots), jnp.int32),
            pltpu.VMEM((1, counts.shape[0]), jnp.int32),
            pltpu.SemaphoreType.DMA((3,)),
        ],
        compiler_params=pltpu.CompilerParams(vmem_limit_bytes=60 * 2**20),
        cost_estimate=cost(0, 4 * part * nocc),
    )(pair_codes[None], counts[None], coeff)

    ahead = cost(4 * 10**10, nbf * nocc * 4)
    quarter = sds((top + META, LANES), BF16)
    stack = pl.pallas_call(
        stack_kernel,
        out_shape=sds((2, top + META, LANES), BF16),
        in_specs=[vmem, vmem],
        out_specs=vmem,
        compiler_params=params,
        cost_estimate=ahead,
    )
    hold = pl.pallas_call(
        copy_kernel,
        out_shape=quarter,
        in_specs=[vmem],
        out_specs=vmem,
        compiler_params=params,
        cost_estimate=ahead,
    )
    c3 = swap(packed, "blk", 3)
    c1 = swap(packed, "blk", 1)
    onward = hold(c3)
    c2 = swap(onward, "blk", 1)
    early = stack(c1, c3)
    early2 = swap(early, "aux", 2)
    later = after(ints, early)
    i3 = swap(later, "blk", 3)
    i1 = swap(later, "blk", 1)
    late = hold(c2)
    late2 = swap(late, "aux", 2)
    early13 = swap(jnp.concatenate([early, early2]), "aux", 1)
    notes = jnp.stack([c[top::8, :slots] for c in (packed, c1, late, c3)]).astype(jnp.int32)
    late13 = swap(after(jnp.stack([late, late2]), notes), "aux", 1)

    i2 = swap(after(i3, late13, i1), "blk", 1)
    dense, full, left, overlap = pl.pallas_call(
        first_kernel,
        out_shape=(
            sds((nbf, 3 * rows), BF16),
            sds((nbf, nocc), BF16),
            sds((rows, nbf), jnp.float32),
            sds((rows, nbf), BF16),
        ),
        in_specs=[smem] + [vmem] * 10,
        out_specs=(vmem,) * 4,
        compiler_params=params,
    )(notes, ints, i1, i3, coeff, early, late, early2, late2, early13, late13)
    half = rows // 2
    p2, p3, dense2 = pl.pallas_call(
        far_kernel,
        out_shape=(sds((part, nocc), BF16),) * 2 + (sds((nbf, rows), BF16),),
        in_specs=[smem] + [vmem] * 5,
        out_specs=(vmem,) * 3,
        scratch_shapes=[pltpu.VMEM((half, nocc), jnp.float32)],
        compiler_params=params,
        cost_estimate=cost(2 * half * nbf * (rows + nbf + nocc), nbf * nocc * 8),
    )(notes, i2, dense, full, left, overlap)
    mine, p1 = pl.pallas_call(
        near_kernel,
        out_shape=(sds((part, nocc), jnp.float32), sds((part, nocc), BF16)),
        in_specs=[vmem] * 5,
        out_specs=(vmem,) * 2,
        scratch_shapes=[pltpu.VMEM((half, nocc), jnp.float32)],
        compiler_params=params,
        cost_estimate=cost(2 * half * nbf * (rows + nbf + nocc), nbf * nocc * 8),
    )(dense2, dense, full, left, overlap)
    got2, got3, got1 = swap(p2, "aux", 2), swap(p3, "aux", 3), swap(p1, "aux", 1)
    others = after(got2.astype(jnp.float32) + got3.astype(jnp.float32), mine)
    return mine + got1.astype(jnp.float32) + others


def local(integrals, pair_codes, counts, coeff):
    if lax.axis_size("blk") == 4 and lax.axis_size("aux") == 4:
        return local_line(integrals, pair_codes, counts, coeff)
    return local_long(integrals, pair_codes, counts, coeff)


def solution(mesh):
    in_specs = (
        P(("grp", "blk"), "aux", None, None),
        P(("grp", "blk")),
        P(("grp", "blk")),
        P(("grp", "blk"), None),
    )
    out_specs = P(("grp", "blk", "aux"), None)
    return jax.shard_map(local, mesh=mesh, in_specs=in_specs, out_specs=out_specs, check_vma=False)
```

```python
import functools

import jax
import jax.numpy as jnp
from jax import lax
from jax.experimental import pallas as pl
from jax.experimental.pallas import tpu as pltpu
from jax.sharding import PartitionSpec as P

BF16 = jnp.bfloat16
META = 16


def transform_slots(ints, columns, blocks):
    slots, paux, width, _ = ints.shape
    nocc = blocks.shape[2]

    def one_group(inputs):
        group_ints, group_cols = inputs
        chosen = blocks[group_cols]
        return jnp.einsum(
            "spml,sli->spmi", group_ints, chosen, preferred_element_type=jnp.float32
        ).astype(BF16)

    grouped = lax.map(
        one_group, (ints.reshape(slots // 8, 8, paux, width, width), columns.reshape(slots // 8, 8))
    )
    return grouped.reshape(slots, paux, width, nocc)


def local_long(integrals, pair_codes, counts, coeff):
    slots, paux, width, _ = integrals.shape
    nocc = coeff.shape[1]
    nblk = lax.axis_size("blk")
    per_dev = coeff.shape[0] // width
    cap = slots // nblk
    alive = (jnp.arange(cap)[None, :] < counts[:, None]).reshape(slots)
    masked = integrals * alive.astype(BF16)[:, None, None, None]
    local_blocks = coeff.reshape(per_dev, width, nocc)
    half = transform_slots(masked, pair_codes % per_dev, local_blocks)
    half_in, rows_in = (
        lax.all_to_all(half, "blk", split_axis=0, concat_axis=0, tiled=True),
        lax.all_to_all(pair_codes // per_dev, "blk", split_axis=0, concat_axis=0, tiled=True),
    )
    selector = (rows_in[:, None] == jnp.arange(per_dev, dtype=jnp.int32)[None, :]).astype(BF16)
    fitted = jnp.einsum("sk,spmi->pkmi", selector, half_in, preferred_element_type=jnp.float32)
    fitted = fitted.astype(BF16).reshape(paux, per_dev * width, nocc)
    partial_value = jnp.einsum(
        "nj,pni->pji", coeff, fitted, preferred_element_type=jnp.float32
    ).astype(BF16)
    occupied = lax.psum(partial_value.astype(jnp.float32).astype(BF16), "blk")
    return lax.psum_scatter(
        jnp.einsum("pnj,pji->ni", fitted, occupied, preferred_element_type=jnp.float32).astype(BF16),
        "aux",
        scatter_dimension=0,
        tiled=True,
    ).astype(jnp.float32)


LANES = 128


def after(x, *others):
    return lax.optimization_barrier((x, *others))[0]


def swap(x, axis, k):
    return lax.ppermute(x, axis, [(i, i ^ k) for i in range(4)])


def gray(k):
    return k ^ (k >> 1)


def pack_kernel(codes, counts, coeff, out, quarter, note, code, count, sems):
    part, nocc = quarter.shape
    a = lax.axis_index("aux")
    copies = (
        pltpu.make_async_copy(
            coeff.at[pl.ds(pl.multiple_of(a * part, part), part)], quarter, sems.at[0]
        ),
        pltpu.make_async_copy(codes, code, sems.at[1]),
        pltpu.make_async_copy(counts, count, sems.at[2]),
    )
    for copy in copies:
        copy.start()
    note[...] = jnp.zeros_like(note)
    for copy in copies:
        copy.wait()
    note[0:1, : code.shape[1]] = code[...].astype(jnp.float32)
    note[8:9, : count.shape[1]] = count[...].astype(jnp.float32)
    top = nocc // LANES * part
    out[top : top + META, :] = note[...].astype(BF16)
    for c in range(nocc // LANES):
        out[c * part : (c + 1) * part, :] = quarter[:, c * LANES : (c + 1) * LANES]


def stack_kernel(x, y, both):
    both[0] = x[...]
    both[1] = y[...]


def copy_kernel(x, y):
    y[...] = x[...]


def gather_quarters(coeff, at_k, refs):
    a = lax.axis_index("aux")
    part = (refs[0].shape[0] - META) * LANES // coeff.shape[1]
    for j, ref in enumerate(refs):
        at = pl.ds(pl.multiple_of(at_k * 4 * part + (a ^ j) * part, part), part)
        for c in range(coeff.shape[1] // LANES):
            coeff[at, c * LANES : (c + 1) * LANES] = ref[c * part : (c + 1) * part, :]


def place(dense, ref, notes, k, left, rows):
    z = lax.axis_index("blk")
    slots, width, _ = ref.shape
    cap = slots // 4
    for s in range(slots):
        target = s // cap
        code = notes[k, 0, s]

        @pl.when(s % cap < notes[k, 1, target])
        def _():
            row = gray(target ^ z) * rows + code // 2 * width
            col = left + code % 2 * width
            dense[
                pl.ds(pl.multiple_of(row, width), width),
                pl.ds(pl.multiple_of(col, width), width),
            ] = ref[s]


def dot(x, y):
    return jnp.dot(x, y, preferred_element_type=jnp.float32)


def dot_t(x, y):
    return lax.dot_general(x, y, (((1,), (1,)), ((), ())), preferred_element_type=jnp.float32)


def first_kernel(notes, i0, i1, i3, own, *refs):
    early, late, early2, late2, early13, late13, dense, coeff, left, overlap = refs
    rows = own.shape[0]
    three = 3 * rows
    dense[...] = jnp.zeros_like(dense)
    for k, ref in ((0, i0), (1, i1), (3, i3)):
        place(dense, ref, notes, k, gray(k) * rows, rows)
    coeff[:rows, :] = own[...]
    for i, k in enumerate((1, 3)):
        gather_quarters(coeff, gray(k), (early.at[i], early13.at[i], early2.at[i], early13.at[2 + i]))
    gather_quarters(coeff, gray(2), (late, late13.at[0], late2, late13.at[1]))
    fitted = dot(dense[:rows, :], coeff[:three, :]).astype(BF16)
    left[...] = dot_t(fitted, coeff[...])
    overlap[...] = dot_t(coeff[three:, :], coeff[...]).astype(BF16)


def chain(left, dense, dense2, coeff):
    three = dense.shape[1]
    most, last = dot(left, dense[...]).astype(BF16), dot(left, dense2[...]).astype(BF16)
    return dot(most, coeff[:three, :]) + dot(last, coeff[three:, :])


def far_kernel(notes, i2, dense, coeff, left, overlap, p2, p3, dense2, total):
    a = lax.axis_index("aux")
    rows = left.shape[0]
    half, part = rows // 2, rows // 4
    dense2[...] = jnp.zeros_like(dense2)
    place(dense2, i2, notes, 2, 0, rows)
    far = pl.ds(pl.multiple_of((1 - a // 2) * half, half), half)
    whole = left[far, :] + dot(dense2[far, :], overlap[...])
    total[...] = chain(whole.astype(BF16), dense, dense2, coeff)
    for j, out in ((2, p2), (3, p3)):
        out[...] = total[pl.ds(pl.multiple_of((a ^ j) % 2 * part, part), part), :].astype(BF16)


def near_kernel(dense2, dense, coeff, left, overlap, mine, p1, total):
    a = lax.axis_index("aux")
    part = mine.shape[0]
    near = pl.ds(pl.multiple_of(a // 2 * 2 * part, 2 * part), 2 * part)
    whole = left[near, :] + dot(dense2[near, :], overlap[...])
    total[...] = chain(whole.astype(BF16), dense, dense2, coeff)
    mine[...] = total[pl.ds(pl.multiple_of(a % 2 * part, part), part), :]
    p1[...] = total[pl.ds(pl.multiple_of((a ^ 1) % 2 * part, part), part), :].astype(BF16)


def local_line(integrals, pair_codes, counts, coeff):
    slots, _, width, _ = integrals.shape
    rows, nocc = coeff.shape
    part = rows // 4
    nbf = rows * 4
    sds = jax.ShapeDtypeStruct
    vmem = pl.BlockSpec(memory_space=pltpu.VMEM)
    smem = pl.BlockSpec(memory_space=pltpu.SMEM)
    params = pltpu.CompilerParams(vmem_limit_bytes=20 * 2**20)
    cost = lambda flops, size: pl.CostEstimate(
        flops=flops, bytes_accessed=size, transcendentals=0
    )

    ints = integrals.reshape(slots, width, width)
    top = nocc // LANES * part
    packed = pl.pallas_call(
        pack_kernel,
        out_shape=sds((top + META, LANES), BF16),
        in_specs=[pl.BlockSpec(memory_space=pl.ANY)] * 3,
        out_specs=vmem,
        scratch_shapes=[
            pltpu.VMEM((part, nocc), BF16),
            pltpu.VMEM((META, LANES), jnp.float32),
            pltpu.VMEM((1, slots), jnp.int32),
            pltpu.VMEM((1, counts.shape[0]), jnp.int32),
            pltpu.SemaphoreType.DMA((3,)),
        ],
        compiler_params=pltpu.CompilerParams(vmem_limit_bytes=60 * 2**20),
        cost_estimate=cost(0, 4 * part * nocc),
    )(pair_codes[None], counts[None], coeff)

    ahead = cost(4 * 10**10, nbf * nocc * 4)
    quarter = sds((top + META, LANES), BF16)
    stack = pl.pallas_call(
        stack_kernel,
        out_shape=sds((2, top + META, LANES), BF16),
        in_specs=[vmem, vmem],
        out_specs=vmem,
        compiler_params=params,
        cost_estimate=ahead,
    )
    hold = pl.pallas_call(
        copy_kernel,
        out_shape=quarter,
        in_specs=[vmem],
        out_specs=vmem,
        compiler_params=params,
        cost_estimate=ahead,
    )
    c3 = swap(packed, "blk", 3)
    c1 = swap(packed, "blk", 1)
    onward = hold(c3)
    c2 = swap(onward, "blk", 1)
    later = after(ints, onward)
    i3 = swap(later, "blk", 3)
    i1 = swap(later, "blk", 1)
    late = hold(c2)
    early = stack(c1, after(c3, late))
    early2 = swap(early, "aux", 2)
    late2 = swap(late, "aux", 2)
    notes = jnp.stack([c[top::8, :slots] for c in (packed, c1, late, c3)]).astype(jnp.int32)
    late13 = swap(after(jnp.stack([late, late2]), notes), "aux", 1)
    early13 = swap(jnp.concatenate([early, early2]), "aux", 1)
    i2 = swap(after(i3, late13, i1), "blk", 1)

    dense, full, left, overlap = pl.pallas_call(
        first_kernel,
        out_shape=(
            sds((nbf, 3 * rows), BF16),
            sds((nbf, nocc), BF16),
            sds((rows, nbf), jnp.float32),
            sds((rows, nbf), BF16),
        ),
        in_specs=[smem] + [vmem] * 10,
        out_specs=(vmem,) * 4,
        compiler_params=params,
    )(notes, ints, i1, i3, coeff, early, late, early2, late2, early13, late13)
    half = rows // 2
    p2, p3, dense2 = pl.pallas_call(
        far_kernel,
        out_shape=(sds((part, nocc), BF16),) * 2 + (sds((nbf, rows), BF16),),
        in_specs=[smem] + [vmem] * 5,
        out_specs=(vmem,) * 3,
        scratch_shapes=[pltpu.VMEM((half, nocc), jnp.float32)],
        compiler_params=params,
        cost_estimate=cost(2 * half * nbf * (rows + nbf + nocc), nbf * nocc * 8),
    )(notes, i2, dense, full, left, overlap)
    mine, p1 = pl.pallas_call(
        near_kernel,
        out_shape=(sds((part, nocc), jnp.float32), sds((part, nocc), BF16)),
        in_specs=[vmem] * 5,
        out_specs=(vmem,) * 2,
        scratch_shapes=[pltpu.VMEM((half, nocc), jnp.float32)],
        compiler_params=params,
        cost_estimate=cost(2 * half * nbf * (rows + nbf + nocc), nbf * nocc * 8),
    )(dense2, dense, full, left, overlap)
    got2, got3, got1 = swap(p2, "aux", 2), swap(p3, "aux", 3), swap(p1, "aux", 1)
    others = after(got2.astype(jnp.float32) + got3.astype(jnp.float32), mine)
    return mine + got1.astype(jnp.float32) + others


def local(integrals, pair_codes, counts, coeff):
    if lax.axis_size("blk") == 4 and lax.axis_size("aux") == 4:
        return local_line(integrals, pair_codes, counts, coeff)
    return local_long(integrals, pair_codes, counts, coeff)


def solution(mesh):
    in_specs = (
        P(("grp", "blk"), "aux", None, None),
        P(("grp", "blk")),
        P(("grp", "blk")),
        P(("grp", "blk"), None),
    )
    out_specs = P(("grp", "blk", "aux"), None)
    return jax.shard_map(local, mesh=mesh, in_specs=in_specs, out_specs=out_specs, check_vma=False)
```

```python
import functools

import jax
import jax.numpy as jnp
from jax import lax
from jax.experimental import pallas as pl
from jax.experimental.pallas import tpu as pltpu
from jax.sharding import PartitionSpec as P

BF16 = jnp.bfloat16
META = 16


def transform_slots(ints, columns, blocks):
    slots, paux, width, _ = ints.shape
    nocc = blocks.shape[2]

    def one_group(inputs):
        group_ints, group_cols = inputs
        chosen = blocks[group_cols]
        return jnp.einsum(
            "spml,sli->spmi", group_ints, chosen, preferred_element_type=jnp.float32
        ).astype(BF16)

    grouped = lax.map(
        one_group, (ints.reshape(slots // 8, 8, paux, width, width), columns.reshape(slots // 8, 8))
    )
    return grouped.reshape(slots, paux, width, nocc)


def local_long(integrals, pair_codes, counts, coeff):
    slots, paux, width, _ = integrals.shape
    nocc = coeff.shape[1]
    nblk = lax.axis_size("blk")
    per_dev = coeff.shape[0] // width
    cap = slots // nblk
    alive = (jnp.arange(cap)[None, :] < counts[:, None]).reshape(slots)
    masked = integrals * alive.astype(BF16)[:, None, None, None]
    local_blocks = coeff.reshape(per_dev, width, nocc)
    half = transform_slots(masked, pair_codes % per_dev, local_blocks)
    half_in, rows_in = (
        lax.all_to_all(half, "blk", split_axis=0, concat_axis=0, tiled=True),
        lax.all_to_all(pair_codes // per_dev, "blk", split_axis=0, concat_axis=0, tiled=True),
    )
    selector = (rows_in[:, None] == jnp.arange(per_dev, dtype=jnp.int32)[None, :]).astype(BF16)
    fitted = jnp.einsum("sk,spmi->pkmi", selector, half_in, preferred_element_type=jnp.float32)
    fitted = fitted.astype(BF16).reshape(paux, per_dev * width, nocc)
    partial_value = jnp.einsum(
        "nj,pni->pji", coeff, fitted, preferred_element_type=jnp.float32
    ).astype(BF16)
    occupied = lax.psum(partial_value.astype(jnp.float32).astype(BF16), "blk")
    return lax.psum_scatter(
        jnp.einsum("pnj,pji->ni", fitted, occupied, preferred_element_type=jnp.float32).astype(BF16),
        "aux",
        scatter_dimension=0,
        tiled=True,
    ).astype(jnp.float32)


LANES = 128


def after(x, *others):
    return lax.optimization_barrier((x, *others))[0]


def swap(x, axis, k):
    return lax.ppermute(x, axis, [(i, i ^ k) for i in range(4)])


def gray(k):
    return k ^ (k >> 1)


def middle(x):
    return lax.ppermute(x, "blk", [(1, 2), (2, 1)])


def pack_kernel(codes, counts, coeff, out, quarter, note, code, count, sems):
    part, nocc = quarter.shape
    a = lax.axis_index("aux")
    copies = (
        pltpu.make_async_copy(
            coeff.at[pl.ds(pl.multiple_of(a * part, part), part)], quarter, sems.at[0]
        ),
        pltpu.make_async_copy(codes, code, sems.at[1]),
        pltpu.make_async_copy(counts, count, sems.at[2]),
    )
    for copy in copies:
        copy.start()
    note[...] = jnp.zeros_like(note)
    for copy in copies:
        copy.wait()
    note[0:1, : code.shape[1]] = code[...].astype(jnp.float32)
    note[8:9, : count.shape[1]] = count[...].astype(jnp.float32)
    top = nocc // LANES * part
    out[top : top + META, :] = note[...].astype(BF16)
    for c in range(nocc // LANES):
        out[c * part : (c + 1) * part, :] = quarter[:, c * LANES : (c + 1) * LANES]


def stack_kernel(x, y, both):
    both[0] = x[...]
    both[1] = y[...]


def copy_kernel(x, y):
    y[...] = x[...]


def gather_quarters(coeff, at_k, refs):
    a = lax.axis_index("aux")
    part = (refs[0].shape[0] - META) * LANES // coeff.shape[1]
    for j, ref in enumerate(refs):
        at = pl.ds(pl.multiple_of(at_k * 4 * part + (a ^ j) * part, part), part)
        for c in range(coeff.shape[1] // LANES):
            coeff[at, c * LANES : (c + 1) * LANES] = ref[c * part : (c + 1) * part, :]


def place(dense, ref, notes, k, left, rows):
    z = lax.axis_index("blk")
    slots, width, _ = ref.shape
    cap = slots // 4
    for s in range(slots):
        target = s // cap
        code = notes[k, 0, s]

        @pl.when(s % cap < notes[k, 1, target])
        def _():
            row = gray(target ^ z) * rows + code // 2 * width
            col = left + code % 2 * width
            dense[
                pl.ds(pl.multiple_of(row, width), width),
                pl.ds(pl.multiple_of(col, width), width),
            ] = ref[s]


def dot(x, y):
    return jnp.dot(x, y, preferred_element_type=jnp.float32)


def dot_t(x, y):
    return lax.dot_general(x, y, (((1,), (1,)), ((), ())), preferred_element_type=jnp.float32)


def first_kernel(notes, i0, i1, i3, own, *refs):
    early, late, early2, late2, early13, late13, dense, coeff, left, overlap = refs
    rows = own.shape[0]
    three = 3 * rows
    dense[...] = jnp.zeros_like(dense)
    for k, ref in ((0, i0), (1, i1), (3, i3)):
        place(dense, ref, notes, k, gray(k) * rows, rows)
    coeff[:rows, :] = own[...]
    for i, k in enumerate((1, 3)):
        gather_quarters(coeff, gray(k), (early.at[i], early13.at[i], early2.at[i], early13.at[2 + i]))
    gather_quarters(coeff, gray(2), (late, late13.at[0], late2, late13.at[1]))
    fitted = dot(dense[: 2 * rows, :], coeff[:three, :]).astype(BF16)
    left[...] = dot_t(fitted, coeff[...])
    overlap[...] = dot_t(coeff[three:, :], coeff[...]).astype(BF16)


def chain(left, dense, dense2, coeff):
    three = dense.shape[1]
    most, last = dot(left, dense[...]).astype(BF16), dot(left, dense2[...]).astype(BF16)
    return dot(most, coeff[:three, :]) + dot(last, coeff[three:, :])


def cut(total, mine, p1, p2, p3):
    a = lax.axis_index("aux")
    size = mine.shape[0]
    mine[...] = total[pl.ds(pl.multiple_of(a * size, size), size), :]
    for j, out in enumerate((p1, p2, p3), 1):
        out[...] = total[pl.ds(pl.multiple_of((a ^ j) * size, size), size), :].astype(BF16)


def end_kernel(notes, i2, dense, coeff, left, overlap, mine, p1, p2, p3, dense2, total):
    rows = total.shape[0]
    dense2[...] = jnp.zeros_like(dense2)
    place(dense2, i2, notes, 2, 0, rows)
    whole = left[rows:, :] + dot(dense2[rows : 2 * rows, :], overlap[...])
    total[...] = chain(whole.astype(BF16), dense, dense2, coeff)
    cut(total, mine, p1, p2, p3)


def own_kernel(dense2, dense, coeff, left, overlap, mine, p1, p2, p3, total):
    rows = total.shape[0]
    whole = left[:rows, :] + dot(dense2[:rows, :], overlap[...])
    total[...] = chain(whole.astype(BF16), dense, dense2, coeff)
    cut(total, mine, p1, p2, p3)


def local_line(integrals, pair_codes, counts, coeff):
    slots, _, width, _ = integrals.shape
    rows, nocc = coeff.shape
    part = rows // 4
    nbf = rows * 4
    sds = jax.ShapeDtypeStruct
    vmem = pl.BlockSpec(memory_space=pltpu.VMEM)
    smem = pl.BlockSpec(memory_space=pltpu.SMEM)
    params = pltpu.CompilerParams(vmem_limit_bytes=20 * 2**20)
    cost = lambda flops, size: pl.CostEstimate(
        flops=flops, bytes_accessed=size, transcendentals=0
    )

    ints = integrals.reshape(slots, width, width)
    top = nocc // LANES * part
    packed = pl.pallas_call(
        pack_kernel,
        out_shape=sds((top + META, LANES), BF16),
        in_specs=[pl.BlockSpec(memory_space=pl.ANY)] * 3,
        out_specs=vmem,
        scratch_shapes=[
            pltpu.VMEM((part, nocc), BF16),
            pltpu.VMEM((META, LANES), jnp.float32),
            pltpu.VMEM((1, slots), jnp.int32),
            pltpu.VMEM((1, counts.shape[0]), jnp.int32),
            pltpu.SemaphoreType.DMA((3,)),
        ],
        compiler_params=pltpu.CompilerParams(vmem_limit_bytes=60 * 2**20),
        cost_estimate=cost(0, 4 * part * nocc),
    )(pair_codes[None], counts[None], coeff)

    ahead = cost(4 * 10**10, nbf * nocc * 4)
    quarter = sds((top + META, LANES), BF16)
    stack = pl.pallas_call(
        stack_kernel,
        out_shape=sds((2, top + META, LANES), BF16),
        in_specs=[vmem, vmem],
        out_specs=vmem,
        compiler_params=params,
        cost_estimate=ahead,
    )
    hold = pl.pallas_call(
        copy_kernel,
        out_shape=quarter,
        in_specs=[vmem],
        out_specs=vmem,
        compiler_params=params,
        cost_estimate=ahead,
    )
    f32 = jnp.float32
    c1 = swap(packed, "blk", 1)
    c3 = middle(packed)
    i1 = swap(ints, "blk", 1)
    onward = hold(c1)
    c2 = middle(onward)
    early = stack(c1, c3)
    early2 = swap(early, "aux", 2)
    i3 = middle(after(ints, onward))
    i2 = middle(i1)
    late = hold(after(c2, i1))
    late2 = swap(late, "aux", 2)
    early13 = swap(jnp.concatenate([early, early2]), "aux", 1)
    notes = jnp.stack([c[top::8, :slots] for c in (packed, c1, late, c3)]).astype(jnp.int32)
    late13 = swap(after(jnp.stack([late, late2]), notes), "aux", 1)

    dense, full, left, overlap = pl.pallas_call(
        first_kernel,
        out_shape=(
            sds((nbf, 3 * rows), BF16),
            sds((nbf, nocc), BF16),
            sds((2 * rows, nbf), f32),
            sds((rows, nbf), BF16),
        ),
        in_specs=[smem] + [vmem] * 10,
        out_specs=(vmem,) * 4,
        compiler_params=params,
    )(notes, ints, i1, i3, coeff, early, late, early2, late2, early13, late13)
    pieces = (sds((part, nocc), f32),) + (sds((part, nocc), BF16),) * 3
    estimate = cost(2 * rows * nbf * (rows + nbf + nocc), nbf * nocc * 8)
    *end_parts, dense2 = pl.pallas_call(
        end_kernel,
        out_shape=pieces + (sds((nbf, rows), BF16),),
        in_specs=[smem] + [vmem] * 5,
        out_specs=(vmem,) * 5,
        scratch_shapes=[pltpu.VMEM((rows, nocc), f32)],
        compiler_params=params,
        cost_estimate=estimate,
    )(notes, i2, dense, full, left, overlap)
    own_parts = pl.pallas_call(
        own_kernel,
        out_shape=pieces,
        in_specs=[vmem] * 5,
        out_specs=(vmem,) * 4,
        scratch_shapes=[pltpu.VMEM((rows, nocc), f32)],
        compiler_params=params,
        cost_estimate=estimate,
    )(dense2, dense, full, left, overlap)

    def summed(mine, p1, p2, p3):
        got = [swap(p, "aux", k) for k, p in ((2, p2), (3, p3), (1, p1))]
        return mine + got[0].astype(f32) + got[1].astype(f32) + got[2].astype(f32)

    back = swap(summed(*end_parts).astype(BF16), "blk", 1)
    z = lax.axis_index("blk")
    return jnp.where((z == 0) | (z == 3), back.astype(f32), summed(*own_parts))


def local(integrals, pair_codes, counts, coeff):
    if lax.axis_size("blk") == 4 and lax.axis_size("aux") == 4:
        return local_line(integrals, pair_codes, counts, coeff)
    return local_long(integrals, pair_codes, counts, coeff)


def solution(mesh):
    in_specs = (
        P(("grp", "blk"), "aux", None, None),
        P(("grp", "blk")),
        P(("grp", "blk")),
        P(("grp", "blk"), None),
    )
    out_specs = P(("grp", "blk", "aux"), None)
    return jax.shard_map(local, mesh=mesh, in_specs=in_specs, out_specs=out_specs, check_vma=False)
```

```python
import functools

import jax
import jax.numpy as jnp
from jax import lax
from jax.experimental import pallas as pl
from jax.experimental.pallas import tpu as pltpu
from jax.sharding import PartitionSpec as P

BF16 = jnp.bfloat16
META = 16


def transform_slots(ints, columns, blocks):
    slots, paux, width, _ = ints.shape
    nocc = blocks.shape[2]

    def one_group(inputs):
        group_ints, group_cols = inputs
        chosen = blocks[group_cols]
        return jnp.einsum(
            "spml,sli->spmi", group_ints, chosen, preferred_element_type=jnp.float32
        ).astype(BF16)

    grouped = lax.map(
        one_group, (ints.reshape(slots // 8, 8, paux, width, width), columns.reshape(slots // 8, 8))
    )
    return grouped.reshape(slots, paux, width, nocc)


def local_long(integrals, pair_codes, counts, coeff):
    slots, paux, width, _ = integrals.shape
    nocc = coeff.shape[1]
    nblk = lax.axis_size("blk")
    per_dev = coeff.shape[0] // width
    cap = slots // nblk
    alive = (jnp.arange(cap)[None, :] < counts[:, None]).reshape(slots)
    masked = integrals * alive.astype(BF16)[:, None, None, None]
    local_blocks = coeff.reshape(per_dev, width, nocc)
    half = transform_slots(masked, pair_codes % per_dev, local_blocks)
    half_in, rows_in = (
        lax.all_to_all(half, "blk", split_axis=0, concat_axis=0, tiled=True),
        lax.all_to_all(pair_codes // per_dev, "blk", split_axis=0, concat_axis=0, tiled=True),
    )
    selector = (rows_in[:, None] == jnp.arange(per_dev, dtype=jnp.int32)[None, :]).astype(BF16)
    fitted = jnp.einsum("sk,spmi->pkmi", selector, half_in, preferred_element_type=jnp.float32)
    fitted = fitted.astype(BF16).reshape(paux, per_dev * width, nocc)
    partial_value = jnp.einsum(
        "nj,pni->pji", coeff, fitted, preferred_element_type=jnp.float32
    ).astype(BF16)
    occupied = lax.psum(partial_value.astype(jnp.float32).astype(BF16), "blk")
    return lax.psum_scatter(
        jnp.einsum("pnj,pji->ni", fitted, occupied, preferred_element_type=jnp.float32).astype(BF16),
        "aux",
        scatter_dimension=0,
        tiled=True,
    ).astype(jnp.float32)


LANES = 128


def after(x, *others):
    return lax.optimization_barrier((x, *others))[0]


def swap(x, axis, k):
    return lax.ppermute(x, axis, [(i, i ^ k) for i in range(4)])


def gray(k):
    return k ^ (k >> 1)


def middle(x):
    return lax.ppermute(x, "blk", [(1, 2), (2, 1)])


def pack_kernel(codes, counts, coeff, out, quarter, note, code, count, sems):
    part, nocc = quarter.shape
    a = lax.axis_index("aux")
    copies = (
        pltpu.make_async_copy(
            coeff.at[pl.ds(pl.multiple_of(a * part, part), part)], quarter, sems.at[0]
        ),
        pltpu.make_async_copy(codes, code, sems.at[1]),
        pltpu.make_async_copy(counts, count, sems.at[2]),
    )
    for copy in copies:
        copy.start()
    note[...] = jnp.zeros_like(note)
    for copy in copies:
        copy.wait()
    note[0:1, : code.shape[1]] = code[...].astype(jnp.float32)
    note[8:9, : count.shape[1]] = count[...].astype(jnp.float32)
    top = nocc // LANES * part
    out[top : top + META, :] = note[...].astype(BF16)
    for c in range(nocc // LANES):
        out[c * part : (c + 1) * part, :] = quarter[:, c * LANES : (c + 1) * LANES]


def stack_kernel(x, y, both):
    both[0] = x[...]
    both[1] = y[...]


def copy_kernel(x, y):
    y[...] = x[...]


def gather_quarters(coeff, at_k, refs):
    a = lax.axis_index("aux")
    part = (refs[0].shape[0] - META) * LANES // coeff.shape[1]
    for j, ref in enumerate(refs):
        at = pl.ds(pl.multiple_of(at_k * 4 * part + (a ^ j) * part, part), part)
        for c in range(coeff.shape[1] // LANES):
            coeff[at, c * LANES : (c + 1) * LANES] = ref[c * part : (c + 1) * part, :]


def place(dense, ref, notes, k, left, rows):
    z = lax.axis_index("blk")
    slots, width, _ = ref.shape
    cap = slots // 4
    for s in range(slots):
        target = s // cap
        code = notes[k, 0, s]

        @pl.when(s % cap < notes[k, 1, target])
        def _():
            row = gray(target ^ z) * rows + code // 2 * width
            col = left + code % 2 * width
            dense[
                pl.ds(pl.multiple_of(row, width), width),
                pl.ds(pl.multiple_of(col, width), width),
            ] = ref[s]


def dot(x, y):
    return jnp.dot(x, y, preferred_element_type=jnp.float32)


def dot_t(x, y):
    return lax.dot_general(x, y, (((1,), (1,)), ((), ())), preferred_element_type=jnp.float32)


def place_kernel(notes, i0, i1, dense):
    rows = dense.shape[1] // 2
    dense[...] = jnp.zeros_like(dense)
    place(dense, i0, notes, 0, 0, rows)
    place(dense, i1, notes, 1, rows, rows)


def fit(dense, dense3, coeff, first):
    two = dense.shape[1]
    rows = two // 2
    part = pl.ds(first, rows)
    fitted = dot(dense[part, :], coeff[:two, :]) + dot(dense3[part, :], coeff[two : two + rows, :])
    return dot_t(fitted.astype(BF16), coeff[...])


def first_kernel(notes, dense, i3, own, *refs):
    early, late, early2, late2, early13, late13, dense3, coeff, left, overlap = refs
    rows = own.shape[0]
    dense3[...] = jnp.zeros_like(dense3)
    place(dense3, i3, notes, 3, 0, rows)
    coeff[:rows, :] = own[...]
    for i, k in enumerate((1, 3)):
        gather_quarters(coeff, gray(k), (early.at[i], early13.at[i], early2.at[i], early13.at[2 + i]))
    gather_quarters(coeff, gray(2), (late, late13.at[0], late2, late13.at[1]))
    left[...] = fit(dense, dense3, coeff, rows)
    overlap[...] = dot_t(coeff[3 * rows :, :], coeff[...]).astype(BF16)


def chain(left, dense, dense3, dense2, coeff):
    at, total = 0, None
    for columns in (dense, dense3, dense2):
        width = columns.shape[1]
        term = dot(dot(left, columns[...]).astype(BF16), coeff[at : at + width, :])
        total = term if total is None else total + term
        at += width
    return total


def cut(total, mine, p1, p2, p3):
    a = lax.axis_index("aux")
    size = mine.shape[0]
    mine[...] = total[pl.ds(pl.multiple_of(a * size, size), size), :]
    for j, out in enumerate((p1, p2, p3), 1):
        out[...] = total[pl.ds(pl.multiple_of((a ^ j) * size, size), size), :].astype(BF16)


def end_kernel(notes, i2, dense, dense3, coeff, left, overlap, mine, p1, p2, p3, dense2, total):
    rows = total.shape[0]
    dense2[...] = jnp.zeros_like(dense2)
    place(dense2, i2, notes, 2, 0, rows)
    whole = left[...] + dot(dense2[rows : 2 * rows, :], overlap[...])
    total[...] = chain(whole.astype(BF16), dense, dense3, dense2, coeff)
    cut(total, mine, p1, p2, p3)


def own_kernel(dense, dense3, dense2, coeff, overlap, mine, p1, p2, p3, total):
    rows = total.shape[0]
    whole = fit(dense, dense3, coeff, 0) + dot(dense2[:rows, :], overlap[...])
    total[...] = chain(whole.astype(BF16), dense, dense3, dense2, coeff)
    cut(total, mine, p1, p2, p3)


def local_line(integrals, pair_codes, counts, coeff):
    slots, _, width, _ = integrals.shape
    rows, nocc = coeff.shape
    part = rows // 4
    nbf = rows * 4
    sds = jax.ShapeDtypeStruct
    vmem = pl.BlockSpec(memory_space=pltpu.VMEM)
    smem = pl.BlockSpec(memory_space=pltpu.SMEM)
    params = pltpu.CompilerParams(vmem_limit_bytes=20 * 2**20)
    cost = lambda flops, size: pl.CostEstimate(
        flops=flops, bytes_accessed=size, transcendentals=0
    )

    ints = integrals.reshape(slots, width, width)
    top = nocc // LANES * part
    packed = pl.pallas_call(
        pack_kernel,
        out_shape=sds((top + META, LANES), BF16),
        in_specs=[pl.BlockSpec(memory_space=pl.ANY)] * 3,
        out_specs=vmem,
        scratch_shapes=[
            pltpu.VMEM((part, nocc), BF16),
            pltpu.VMEM((META, LANES), jnp.float32),
            pltpu.VMEM((1, slots), jnp.int32),
            pltpu.VMEM((1, counts.shape[0]), jnp.int32),
            pltpu.SemaphoreType.DMA((3,)),
        ],
        compiler_params=pltpu.CompilerParams(vmem_limit_bytes=60 * 2**20),
        cost_estimate=cost(0, 4 * part * nocc),
    )(pair_codes[None], counts[None], coeff)

    ahead = cost(4 * 10**10, nbf * nocc * 4)
    quarter = sds((top + META, LANES), BF16)
    stack = pl.pallas_call(
        stack_kernel,
        out_shape=sds((2, top + META, LANES), BF16),
        in_specs=[vmem, vmem],
        out_specs=vmem,
        compiler_params=params,
        cost_estimate=ahead,
    )
    hold = pl.pallas_call(
        copy_kernel,
        out_shape=quarter,
        in_specs=[vmem],
        out_specs=vmem,
        compiler_params=params,
        cost_estimate=ahead,
    )
    f32 = jnp.float32
    c1 = swap(packed, "blk", 1)
    c3 = middle(packed)
    i1 = swap(ints, "blk", 1)
    onward = hold(c1)
    c2 = middle(onward)
    early = stack(c1, c3)
    early2 = swap(early, "aux", 2)
    i3 = middle(after(ints, onward))
    i2 = middle(i1)
    late = hold(after(c2, i1))
    late2 = swap(late, "aux", 2)
    early13 = swap(jnp.concatenate([early, early2]), "aux", 1)
    mine_late = after(packed, late)
    notes = jnp.stack([c[top::8, :slots] for c in (mine_late, c1, late, c3)]).astype(jnp.int32)
    dense = pl.pallas_call(
        place_kernel,
        out_shape=sds((nbf, 2 * rows), BF16),
        in_specs=[smem] + [vmem] * 2,
        out_specs=vmem,
        compiler_params=params,
    )(notes, ints, i1)
    late13 = swap(after(jnp.stack([late, late2]), dense), "aux", 1)
    dense3, full, left, overlap = pl.pallas_call(
        first_kernel,
        out_shape=(
            sds((nbf, rows), BF16),
            sds((nbf, nocc), BF16),
            sds((rows, nbf), f32),
            sds((rows, nbf), BF16),
        ),
        in_specs=[smem] + [vmem] * 9,
        out_specs=(vmem,) * 4,
        compiler_params=params,
    )(notes, dense, i3, coeff, early, late, early2, late2, early13, late13)
    pieces = (sds((part, nocc), f32),) + (sds((part, nocc), BF16),) * 3
    estimate = cost(2 * rows * nbf * (rows + nbf + nocc), nbf * nocc * 8)
    *end_parts, dense2 = pl.pallas_call(
        end_kernel,
        out_shape=pieces + (sds((nbf, rows), BF16),),
        in_specs=[smem] + [vmem] * 6,
        out_specs=(vmem,) * 5,
        scratch_shapes=[pltpu.VMEM((rows, nocc), f32)],
        compiler_params=params,
        cost_estimate=estimate,
    )(notes, i2, dense, dense3, full, left, overlap)
    own_parts = pl.pallas_call(
        own_kernel,
        out_shape=pieces,
        in_specs=[vmem] * 5,
        out_specs=(vmem,) * 4,
        scratch_shapes=[pltpu.VMEM((rows, nocc), f32)],
        compiler_params=params,
        cost_estimate=estimate,
    )(dense, dense3, dense2, full, overlap)

    def summed(mine, p1, p2, p3):
        got = [swap(p, "aux", k) for k, p in ((2, p2), (3, p3), (1, p1))]
        return mine + got[0].astype(f32) + got[1].astype(f32) + got[2].astype(f32)

    back = swap(summed(*end_parts).astype(BF16), "blk", 1)
    z = lax.axis_index("blk")
    return jnp.where((z == 0) | (z == 3), back.astype(f32), summed(*own_parts))


def local(integrals, pair_codes, counts, coeff):
    if lax.axis_size("blk") == 4 and lax.axis_size("aux") == 4:
        return local_line(integrals, pair_codes, counts, coeff)
    return local_long(integrals, pair_codes, counts, coeff)


def solution(mesh):
    in_specs = (
        P(("grp", "blk"), "aux", None, None),
        P(("grp", "blk")),
        P(("grp", "blk")),
        P(("grp", "blk"), None),
    )
    out_specs = P(("grp", "blk", "aux"), None)
    return jax.shard_map(local, mesh=mesh, in_specs=in_specs, out_specs=out_specs, check_vma=False)
```

```python
import functools

import jax
import jax.numpy as jnp
from jax import lax
from jax.experimental import pallas as pl
from jax.experimental.pallas import tpu as pltpu
from jax.sharding import PartitionSpec as P

BF16 = jnp.bfloat16
META = 16


def transform_slots(ints, columns, blocks):
    slots, paux, width, _ = ints.shape
    nocc = blocks.shape[2]

    def one_group(inputs):
        group_ints, group_cols = inputs
        chosen = blocks[group_cols]
        return jnp.einsum(
            "spml,sli->spmi", group_ints, chosen, preferred_element_type=jnp.float32
        ).astype(BF16)

    grouped = lax.map(
        one_group, (ints.reshape(slots // 8, 8, paux, width, width), columns.reshape(slots // 8, 8))
    )
    return grouped.reshape(slots, paux, width, nocc)


def local_long(integrals, pair_codes, counts, coeff):
    slots, paux, width, _ = integrals.shape
    nocc = coeff.shape[1]
    nblk = lax.axis_size("blk")
    per_dev = coeff.shape[0] // width
    cap = slots // nblk
    alive = (jnp.arange(cap)[None, :] < counts[:, None]).reshape(slots)
    masked = integrals * alive.astype(BF16)[:, None, None, None]
    local_blocks = coeff.reshape(per_dev, width, nocc)
    half = transform_slots(masked, pair_codes % per_dev, local_blocks)
    half_in, rows_in = (
        lax.all_to_all(half, "blk", split_axis=0, concat_axis=0, tiled=True),
        lax.all_to_all(pair_codes // per_dev, "blk", split_axis=0, concat_axis=0, tiled=True),
    )
    selector = (rows_in[:, None] == jnp.arange(per_dev, dtype=jnp.int32)[None, :]).astype(BF16)
    fitted = jnp.einsum("sk,spmi->pkmi", selector, half_in, preferred_element_type=jnp.float32)
    fitted = fitted.astype(BF16).reshape(paux, per_dev * width, nocc)
    partial_value = jnp.einsum(
        "nj,pni->pji", coeff, fitted, preferred_element_type=jnp.float32
    ).astype(BF16)
    occupied = lax.psum(partial_value.astype(jnp.float32).astype(BF16), "blk")
    return lax.psum_scatter(
        jnp.einsum("pnj,pji->ni", fitted, occupied, preferred_element_type=jnp.float32).astype(BF16),
        "aux",
        scatter_dimension=0,
        tiled=True,
    ).astype(jnp.float32)


LANES = 128


def after(x, *others):
    return lax.optimization_barrier((x, *others))[0]


def swap(x, axis, k):
    return lax.ppermute(x, axis, [(i, i ^ k) for i in range(4)])


def gray(k):
    return k ^ (k >> 1)


def middle(x):
    return lax.ppermute(x, "blk", [(1, 2), (2, 1)])


def pack_kernel(codes, counts, coeff, out, quarter, note, code, count, sems):
    part, nocc = quarter.shape
    a = lax.axis_index("aux")
    copies = (
        pltpu.make_async_copy(
            coeff.at[pl.ds(pl.multiple_of(a * part, part), part)], quarter, sems.at[0]
        ),
        pltpu.make_async_copy(codes, code, sems.at[1]),
        pltpu.make_async_copy(counts, count, sems.at[2]),
    )
    for copy in copies:
        copy.start()
    note[...] = jnp.zeros_like(note)
    for copy in copies:
        copy.wait()
    note[0:1, : code.shape[1]] = code[...].astype(jnp.float32)
    note[8:9, : count.shape[1]] = count[...].astype(jnp.float32)
    top = nocc // LANES * part
    out[top : top + META, :] = note[...].astype(BF16)
    for c in range(nocc // LANES):
        out[c * part : (c + 1) * part, :] = quarter[:, c * LANES : (c + 1) * LANES]


def stack_kernel(x, y, both):
    both[0] = x[...]
    both[1] = y[...]


def copy_kernel(x, y):
    y[...] = x[...]


def gather_quarters(coeff, at_k, refs):
    a = lax.axis_index("aux")
    part = (refs[0].shape[0] - META) * LANES // coeff.shape[1]
    for j, ref in enumerate(refs):
        at = pl.ds(pl.multiple_of(at_k * 4 * part + (a ^ j) * part, part), part)
        for c in range(coeff.shape[1] // LANES):
            coeff[at, c * LANES : (c + 1) * LANES] = ref[c * part : (c + 1) * part, :]


def place(dense, ref, codes, counts, k, left, rows):
    z = lax.axis_index("blk")
    slots, width, _ = ref.shape
    cap = slots // 4
    for s in range(slots):
        target = s // cap
        code = codes[s]

        @pl.when(s % cap < counts[target])
        def _():
            row = gray(target ^ z) * rows + code // 2 * width
            col = left + code % 2 * width
            dense[
                pl.ds(pl.multiple_of(row, width), width),
                pl.ds(pl.multiple_of(col, width), width),
            ] = ref[s]


def noted(notes, k):
    return notes.at[k - 1, 0], notes.at[k - 1, 1]


def dot(x, y):
    return jnp.dot(x, y, preferred_element_type=jnp.float32)


def dot_t(x, y):
    return lax.dot_general(x, y, (((1,), (1,)), ((), ())), preferred_element_type=jnp.float32)


def place_kernel(codes, counts, notes, i0, i1, dense):
    rows = dense.shape[1] // 2
    dense[...] = jnp.zeros_like(dense)
    place(dense, i0, codes, counts, 0, 0, rows)
    place(dense, i1, *noted(notes, 1), 1, rows, rows)


def fit(dense, dense3, coeff, first):
    two = dense.shape[1]
    rows = two // 2
    part = pl.ds(first, rows)
    fitted = dot(dense[part, :], coeff[:two, :]) + dot(dense3[part, :], coeff[two : two + rows, :])
    return dot_t(fitted.astype(BF16), coeff[...])


def first_kernel(notes, dense, i3, own, *refs):
    early, late, early2, late2, early13, late13, dense3, coeff, left, overlap = refs
    rows = own.shape[0]
    dense3[...] = jnp.zeros_like(dense3)
    place(dense3, i3, *noted(notes, 3), 3, 0, rows)
    coeff[:rows, :] = own[...]
    for i, k in enumerate((1, 3)):
        gather_quarters(coeff, gray(k), (early.at[i], early13.at[i], early2.at[i], early13.at[2 + i]))
    gather_quarters(coeff, gray(2), (late, late13.at[0], late2, late13.at[1]))
    left[...] = fit(dense, dense3, coeff, rows)
    overlap[...] = dot_t(coeff[3 * rows :, :], coeff[...]).astype(BF16)


def chain(left, dense, dense3, dense2, coeff):
    at, total = 0, None
    for columns in (dense, dense3, dense2):
        width = columns.shape[1]
        term = dot(dot(left, columns[...]).astype(BF16), coeff[at : at + width, :])
        total = term if total is None else total + term
        at += width
    return total


def cut(total, kept, given):
    a = lax.axis_index("aux")
    part = total.shape[0] // 4
    for i in (0, 2):
        at = pl.ds(i // 2 * part, part)
        kept[at, :] = total[pl.ds(pl.multiple_of((a ^ i) * part, part), part), :]
        given[at, :] = total[pl.ds(pl.multiple_of((a ^ i ^ 1) * part, part), part), :].astype(BF16)


def end_kernel(notes, i2, dense, dense3, coeff, left, overlap, kept, given, dense2, total):
    rows = total.shape[0]
    dense2[...] = jnp.zeros_like(dense2)
    place(dense2, i2, *noted(notes, 2), 2, 0, rows)
    whole = left[...] + dot(dense2[rows : 2 * rows, :], overlap[...])
    total[...] = chain(whole.astype(BF16), dense, dense3, dense2, coeff)
    cut(total, kept, given)


def own_kernel(dense, dense3, dense2, coeff, overlap, kept, given, total):
    rows = total.shape[0]
    whole = fit(dense, dense3, coeff, 0) + dot(dense2[:rows, :], overlap[...])
    total[...] = chain(whole.astype(BF16), dense, dense3, dense2, coeff)
    cut(total, kept, given)


def local_line(integrals, pair_codes, counts, coeff):
    slots, _, width, _ = integrals.shape
    rows, nocc = coeff.shape
    part = rows // 4
    nbf = rows * 4
    sds = jax.ShapeDtypeStruct
    vmem = pl.BlockSpec(memory_space=pltpu.VMEM)
    smem = pl.BlockSpec(memory_space=pltpu.SMEM)
    params = pltpu.CompilerParams(vmem_limit_bytes=20 * 2**20)
    cost = lambda flops, size: pl.CostEstimate(
        flops=flops, bytes_accessed=size, transcendentals=0
    )

    ints = integrals.reshape(slots, width, width)
    top = nocc // LANES * part
    packed = pl.pallas_call(
        pack_kernel,
        out_shape=sds((top + META, LANES), BF16),
        in_specs=[pl.BlockSpec(memory_space=pl.ANY)] * 3,
        out_specs=vmem,
        scratch_shapes=[
            pltpu.VMEM((part, nocc), BF16),
            pltpu.VMEM((META, LANES), jnp.float32),
            pltpu.VMEM((1, slots), jnp.int32),
            pltpu.VMEM((1, counts.shape[0]), jnp.int32),
            pltpu.SemaphoreType.DMA((3,)),
        ],
        compiler_params=pltpu.CompilerParams(vmem_limit_bytes=60 * 2**20),
        cost_estimate=cost(0, 4 * part * nocc),
    )(pair_codes[None], counts[None], coeff)

    ahead = cost(4 * 10**10, nbf * nocc * 4)
    quarter = sds((top + META, LANES), BF16)
    stack = pl.pallas_call(
        stack_kernel,
        out_shape=sds((2, top + META, LANES), BF16),
        in_specs=[vmem, vmem],
        out_specs=vmem,
        compiler_params=params,
        cost_estimate=ahead,
    )
    hold = pl.pallas_call(
        copy_kernel,
        out_shape=quarter,
        in_specs=[vmem],
        out_specs=vmem,
        compiler_params=params,
        cost_estimate=ahead,
    )
    f32 = jnp.float32
    c1 = swap(packed, "blk", 1)
    c3 = middle(packed)
    i1 = swap(ints, "blk", 1)
    onward = hold(c1)
    c2 = middle(onward)
    early = stack(c1, c3)
    early2 = swap(early, "aux", 2)
    i3 = middle(after(ints, onward))
    i2 = middle(i1)
    late = hold(after(c2, i1))
    late2 = swap(late, "aux", 2)
    early13 = swap(jnp.concatenate([early, early2]), "aux", 1)
    notes = jnp.stack([c[top::8, :slots] for c in (c1, late, c3)]).astype(jnp.int32)
    dense = pl.pallas_call(
        place_kernel,
        out_shape=sds((nbf, 2 * rows), BF16),
        in_specs=[smem] * 3 + [vmem] * 2,
        out_specs=vmem,
        compiler_params=params,
    )(pair_codes, counts, notes, ints, i1)
    late13 = swap(after(jnp.stack([late, late2]), dense), "aux", 1)
    dense3, full, left, overlap = pl.pallas_call(
        first_kernel,
        out_shape=(
            sds((nbf, rows), BF16),
            sds((nbf, nocc), BF16),
            sds((rows, nbf), f32),
            sds((rows, nbf), BF16),
        ),
        in_specs=[smem] + [vmem] * 9,
        out_specs=(vmem,) * 4,
        compiler_params=params,
    )(notes, dense, i3, coeff, early, late, early2, late2, early13, late13)
    pieces = (sds((2 * part, nocc), f32), sds((2 * part, nocc), BF16))
    estimate = cost(2 * rows * nbf * (rows + nbf + nocc), nbf * nocc * 8)
    *end_rows, dense2 = pl.pallas_call(
        end_kernel,
        out_shape=pieces + (sds((nbf, rows), BF16),),
        in_specs=[smem] + [vmem] * 6,
        out_specs=(vmem,) * 3,
        scratch_shapes=[pltpu.VMEM((rows, nocc), f32)],
        compiler_params=params,
        cost_estimate=estimate,
    )(notes, i2, dense, dense3, full, left, overlap)
    pair = lambda kept, given: kept + swap(given, "aux", 1).astype(f32)
    ends = pair(*end_rows)
    over = ends[part:].astype(BF16)
    own_rows = pl.pallas_call(
        own_kernel,
        out_shape=pieces,
        in_specs=[vmem] * 5,
        out_specs=(vmem,) * 2,
        scratch_shapes=[pltpu.VMEM((rows, nocc), f32)],
        compiler_params=params,
        cost_estimate=estimate,
    )(dense, dense3, after(dense2, over), full, overlap)

    owns = pair(*own_rows)
    ends = ends[:part] + swap(over, "aux", 2).astype(f32)
    back = swap(ends.astype(BF16), "blk", 1)
    owns = owns[:part] + swap(owns[part:].astype(BF16), "aux", 2).astype(f32)
    z = lax.axis_index("blk")
    return jnp.where((z == 0) | (z == 3), back.astype(f32), owns)


def local(integrals, pair_codes, counts, coeff):
    if lax.axis_size("blk") == 4 and lax.axis_size("aux") == 4:
        return local_line(integrals, pair_codes, counts, coeff)
    return local_long(integrals, pair_codes, counts, coeff)


def solution(mesh):
    in_specs = (
        P(("grp", "blk"), "aux", None, None),
        P(("grp", "blk")),
        P(("grp", "blk")),
        P(("grp", "blk"), None),
    )
    out_specs = P(("grp", "blk", "aux"), None)
    return jax.shard_map(local, mesh=mesh, in_specs=in_specs, out_specs=out_specs, check_vma=False)
```

```python
import functools

import jax
import jax.numpy as jnp
from jax import lax
from jax.experimental import pallas as pl
from jax.experimental.pallas import tpu as pltpu
from jax.sharding import PartitionSpec as P

BF16 = jnp.bfloat16
META = 16


def transform_slots(ints, columns, blocks):
    slots, paux, width, _ = ints.shape
    nocc = blocks.shape[2]

    def one_group(inputs):
        group_ints, group_cols = inputs
        chosen = blocks[group_cols]
        return jnp.einsum(
            "spml,sli->spmi", group_ints, chosen, preferred_element_type=jnp.float32
        ).astype(BF16)

    grouped = lax.map(
        one_group, (ints.reshape(slots // 8, 8, paux, width, width), columns.reshape(slots // 8, 8))
    )
    return grouped.reshape(slots, paux, width, nocc)


def local_long(integrals, pair_codes, counts, coeff):
    slots, paux, width, _ = integrals.shape
    nocc = coeff.shape[1]
    nblk = lax.axis_size("blk")
    per_dev = coeff.shape[0] // width
    cap = slots // nblk
    alive = (jnp.arange(cap)[None, :] < counts[:, None]).reshape(slots)
    masked = integrals * alive.astype(BF16)[:, None, None, None]
    local_blocks = coeff.reshape(per_dev, width, nocc)
    half = transform_slots(masked, pair_codes % per_dev, local_blocks)
    half_in, rows_in = (
        lax.all_to_all(half, "blk", split_axis=0, concat_axis=0, tiled=True),
        lax.all_to_all(pair_codes // per_dev, "blk", split_axis=0, concat_axis=0, tiled=True),
    )
    selector = (rows_in[:, None] == jnp.arange(per_dev, dtype=jnp.int32)[None, :]).astype(BF16)
    fitted = jnp.einsum("sk,spmi->pkmi", selector, half_in, preferred_element_type=jnp.float32)
    fitted = fitted.astype(BF16).reshape(paux, per_dev * width, nocc)
    partial_value = jnp.einsum(
        "nj,pni->pji", coeff, fitted, preferred_element_type=jnp.float32
    ).astype(BF16)
    occupied = lax.psum(partial_value.astype(jnp.float32).astype(BF16), "blk")
    return lax.psum_scatter(
        jnp.einsum("pnj,pji->ni", fitted, occupied, preferred_element_type=jnp.float32).astype(BF16),
        "aux",
        scatter_dimension=0,
        tiled=True,
    ).astype(jnp.float32)


LANES = 128


def after(x, *others):
    return lax.optimization_barrier((x, *others))[0]


def swap(x, axis, k):
    return lax.ppermute(x, axis, [(i, i ^ k) for i in range(4)])


def gray(k):
    return k ^ (k >> 1)


def middle(x):
    return lax.ppermute(x, "blk", [(1, 2), (2, 1)])


def pack_kernel(codes, counts, coeff, ints, out, short, quarter, note, code, count, sems):
    part, nocc = quarter.shape
    a = lax.axis_index("aux")
    top = nocc // LANES * part + META
    copies = (
        pltpu.make_async_copy(
            coeff.at[pl.ds(pl.multiple_of(a * part, part), part)], quarter, sems.at[0]
        ),
        pltpu.make_async_copy(codes, code, sems.at[1]),
        pltpu.make_async_copy(counts, count, sems.at[2]),
        pltpu.make_async_copy(ints, out.at[pl.ds(top, ints.shape[0])], sems.at[3]),
    )
    for copy in copies:
        copy.start()
    note[...] = jnp.zeros_like(note)
    for copy in copies[:3]:
        copy.wait()
    note[0:1, : code.shape[1]] = code[...].astype(jnp.float32)
    note[8:9, : count.shape[1]] = count[...].astype(jnp.float32)
    out[top - META : top, :] = note[...].astype(BF16)
    for c in range(nocc // LANES):
        out[c * part : (c + 1) * part, :] = quarter[:, c * LANES : (c + 1) * LANES]
    short[...] = out[:top, :]
    copies[3].wait()


def stack_kernel(x, y, both):
    size = both.shape[1]
    both[0] = x[:size, :]
    both[1] = y[:size, :]


def copy_kernel(x, y):
    y[...] = x[...]


def gather_quarters(coeff, at_k, refs):
    a = lax.axis_index("aux")
    part = (refs[0].shape[0] - META) * LANES // coeff.shape[1]
    for j, ref in enumerate(refs):
        at = pl.ds(pl.multiple_of(at_k * 4 * part + (a ^ j) * part, part), part)
        for c in range(coeff.shape[1] // LANES):
            coeff[at, c * LANES : (c + 1) * LANES] = ref[c * part : (c + 1) * part, :]


def place(dense, ref, top, codes, counts, k, left, rows):
    z = lax.axis_index("blk")
    width = ref.shape[1]
    slots = (ref.shape[0] - top) // width
    cap = slots // 4
    for s in range(slots):
        target = s // cap
        code = codes[s]

        @pl.when(s % cap < counts[target])
        def _():
            row = gray(target ^ z) * rows + code // 2 * width
            col = left + code % 2 * width
            dense[
                pl.ds(pl.multiple_of(row, width), width),
                pl.ds(pl.multiple_of(col, width), width),
            ] = ref[top + s * width : top + (s + 1) * width, :]


def noted(notes, k):
    return notes.at[k - 1, 0], notes.at[k - 1, 1]


def dot(x, y):
    return jnp.dot(x, y, preferred_element_type=jnp.float32)


def dot_t(x, y):
    return lax.dot_general(x, y, (((1,), (1,)), ((), ())), preferred_element_type=jnp.float32)


def place_kernel(codes, counts, notes, i0, i1, dense):
    rows = dense.shape[1] // 2
    dense[...] = jnp.zeros_like(dense)
    place(dense, i0, 0, codes, counts, 0, 0, rows)
    place(dense, i1, 0, *noted(notes, 1), 1, rows, rows)


def fit(dense, dense3, coeff, first):
    two = dense.shape[1]
    rows = two // 2
    part = pl.ds(first, rows)
    fitted = dot(dense[part, :], coeff[:two, :]) + dot(dense3[part, :], coeff[two : two + rows, :])
    return dot_t(fitted.astype(BF16), coeff[...])


def first_kernel(notes, dense, i3, own, *refs):
    early, late, early2, late2, early13, late13, dense3, coeff, left, overlap = refs
    rows = own.shape[0]
    dense3[...] = jnp.zeros_like(dense3)
    place(dense3, i3, late.shape[0], *noted(notes, 3), 3, 0, rows)
    coeff[:rows, :] = own[...]
    for i, k in enumerate((1, 3)):
        gather_quarters(coeff, gray(k), (early.at[i], early13.at[i], early2.at[i], early13.at[2 + i]))
    gather_quarters(coeff, gray(2), (late, late13.at[0], late2, late13.at[1]))
    left[...] = fit(dense, dense3, coeff, rows)
    overlap[...] = dot_t(coeff[3 * rows :, :], coeff[...]).astype(BF16)


def chain(left, dense, dense3, dense2, coeff):
    at, total = 0, None
    for columns in (dense, dense3, dense2):
        width = columns.shape[1]
        term = dot(dot(left, columns[...]).astype(BF16), coeff[at : at + width, :])
        total = term if total is None else total + term
        at += width
    return total


def cut(total, kept, given):
    a = lax.axis_index("aux")
    part = total.shape[0] // 4
    for i in (0, 2):
        at = pl.ds(i // 2 * part, part)
        kept[at, :] = total[pl.ds(pl.multiple_of((a ^ i) * part, part), part), :]
        given[at, :] = total[pl.ds(pl.multiple_of((a ^ i ^ 1) * part, part), part), :].astype(BF16)


def end_kernel(notes, i2, dense, dense3, coeff, left, overlap, kept, given, dense2, total):
    rows = total.shape[0]
    dense2[...] = jnp.zeros_like(dense2)
    place(dense2, i2, 0, *noted(notes, 2), 2, 0, rows)
    whole = left[...] + dot(dense2[rows : 2 * rows, :], overlap[...])
    total[...] = chain(whole.astype(BF16), dense, dense3, dense2, coeff)
    cut(total, kept, given)


def own_kernel(dense, dense3, dense2, coeff, overlap, kept, given, total):
    rows = total.shape[0]
    whole = fit(dense, dense3, coeff, 0) + dot(dense2[:rows, :], overlap[...])
    total[...] = chain(whole.astype(BF16), dense, dense3, dense2, coeff)
    cut(total, kept, given)


def local_line(integrals, pair_codes, counts, coeff):
    slots, _, width, _ = integrals.shape
    rows, nocc = coeff.shape
    part = rows // 4
    nbf = rows * 4
    sds = jax.ShapeDtypeStruct
    vmem = pl.BlockSpec(memory_space=pltpu.VMEM)
    smem = pl.BlockSpec(memory_space=pltpu.SMEM)
    params = pltpu.CompilerParams(vmem_limit_bytes=20 * 2**20)
    cost = lambda flops, size: pl.CostEstimate(
        flops=flops, bytes_accessed=size, transcendentals=0
    )

    ints = integrals.reshape(slots * width, width)
    top = nocc // LANES * part
    quarter = sds((top + META, LANES), BF16)
    packed, quarters = pl.pallas_call(
        pack_kernel,
        out_shape=(sds((top + META + slots * width, LANES), BF16), quarter),
        in_specs=[pl.BlockSpec(memory_space=pl.ANY)] * 4,
        out_specs=(vmem, vmem),
        scratch_shapes=[
            pltpu.VMEM((part, nocc), BF16),
            pltpu.VMEM((META, LANES), jnp.float32),
            pltpu.VMEM((1, slots), jnp.int32),
            pltpu.VMEM((1, counts.shape[0]), jnp.int32),
            pltpu.SemaphoreType.DMA((4,)),
        ],
        compiler_params=pltpu.CompilerParams(vmem_limit_bytes=60 * 2**20),
        cost_estimate=cost(0, 4 * (part * nocc + slots * width * width)),
    )(pair_codes[None], counts[None], coeff, ints)

    ahead = cost(4 * 10**10, nbf * nocc * 4)
    stack = pl.pallas_call(
        stack_kernel,
        out_shape=sds((2, top + META, LANES), BF16),
        in_specs=[vmem, vmem],
        out_specs=vmem,
        compiler_params=params,
        cost_estimate=ahead,
    )
    hold = pl.pallas_call(
        copy_kernel,
        out_shape=quarter,
        in_specs=[vmem],
        out_specs=vmem,
        compiler_params=params,
        cost_estimate=ahead,
    )
    f32 = jnp.float32
    c1 = swap(quarters, "blk", 1)
    mid = middle(packed)
    i1 = swap(ints, "blk", 1)
    onward = hold(c1)
    c2 = middle(onward)
    early = stack(c1, mid)
    early2 = swap(early, "aux", 2)
    i2 = middle(i1)
    late = hold(after(c2, i1))
    late2 = swap(late, "aux", 2)
    early13 = swap(jnp.concatenate([early, early2]), "aux", 1)
    notes = jnp.stack([c[top : top + META : 8, :slots] for c in (c1, late, mid)]).astype(jnp.int32)
    dense = pl.pallas_call(
        place_kernel,
        out_shape=sds((nbf, 2 * rows), BF16),
        in_specs=[smem] * 3 + [vmem] * 2,
        out_specs=vmem,
        compiler_params=params,
    )(pair_codes, counts, notes, ints, i1)
    late13 = swap(after(jnp.stack([late, late2]), dense), "aux", 1)
    dense3, full, left, overlap = pl.pallas_call(
        first_kernel,
        out_shape=(
            sds((nbf, rows), BF16),
            sds((nbf, nocc), BF16),
            sds((rows, nbf), f32),
            sds((rows, nbf), BF16),
        ),
        in_specs=[smem] + [vmem] * 9,
        out_specs=(vmem,) * 4,
        compiler_params=params,
    )(notes, dense, mid, coeff, early, late, early2, late2, early13, late13)
    pieces = (sds((2 * part, nocc), f32), sds((2 * part, nocc), BF16))
    estimate = cost(2 * rows * nbf * (rows + nbf + nocc), nbf * nocc * 8)
    *end_rows, dense2 = pl.pallas_call(
        end_kernel,
        out_shape=pieces + (sds((nbf, rows), BF16),),
        in_specs=[smem] + [vmem] * 6,
        out_specs=(vmem,) * 3,
        scratch_shapes=[pltpu.VMEM((rows, nocc), f32)],
        compiler_params=params,
        cost_estimate=estimate,
    )(notes, i2, dense, dense3, full, left, overlap)
    pair = lambda kept, given: kept + swap(given, "aux", 1).astype(f32)
    ends = pair(*end_rows)
    over = ends[part:].astype(BF16)
    own_rows = pl.pallas_call(
        own_kernel,
        out_shape=pieces,
        in_specs=[vmem] * 5,
        out_specs=(vmem,) * 2,
        scratch_shapes=[pltpu.VMEM((rows, nocc), f32)],
        compiler_params=params,
        cost_estimate=estimate,
    )(dense, dense3, after(dense2, over), full, overlap)

    owns = pair(*own_rows)
    ends = ends[:part] + swap(over, "aux", 2).astype(f32)
    back = swap(ends.astype(BF16), "blk", 1)
    owns = owns[:part] + swap(owns[part:].astype(BF16), "aux", 2).astype(f32)
    z = lax.axis_index("blk")
    return jnp.where((z == 0) | (z == 3), back.astype(f32), owns)


def local(integrals, pair_codes, counts, coeff):
    if lax.axis_size("blk") == 4 and lax.axis_size("aux") == 4:
        return local_line(integrals, pair_codes, counts, coeff)
    return local_long(integrals, pair_codes, counts, coeff)


def solution(mesh):
    in_specs = (
        P(("grp", "blk"), "aux", None, None),
        P(("grp", "blk")),
        P(("grp", "blk")),
        P(("grp", "blk"), None),
    )
    out_specs = P(("grp", "blk", "aux"), None)
    return jax.shard_map(local, mesh=mesh, in_specs=in_specs, out_specs=out_specs, check_vma=False)
```

```python
import functools

import jax
import jax.numpy as jnp
from jax import lax
from jax.experimental import pallas as pl
from jax.experimental.pallas import tpu as pltpu
from jax.sharding import PartitionSpec as P

BF16 = jnp.bfloat16
META = 16


def transform_slots(ints, columns, blocks):
    slots, paux, width, _ = ints.shape
    nocc = blocks.shape[2]

    def one_group(inputs):
        group_ints, group_cols = inputs
        chosen = blocks[group_cols]
        return jnp.einsum(
            "spml,sli->spmi", group_ints, chosen, preferred_element_type=jnp.float32
        ).astype(BF16)

    grouped = lax.map(
        one_group, (ints.reshape(slots // 8, 8, paux, width, width), columns.reshape(slots // 8, 8))
    )
    return grouped.reshape(slots, paux, width, nocc)


def local_long(integrals, pair_codes, counts, coeff):
    slots, paux, width, _ = integrals.shape
    nocc = coeff.shape[1]
    nblk = lax.axis_size("blk")
    per_dev = coeff.shape[0] // width
    cap = slots // nblk
    alive = (jnp.arange(cap)[None, :] < counts[:, None]).reshape(slots)
    masked = integrals * alive.astype(BF16)[:, None, None, None]
    local_blocks = coeff.reshape(per_dev, width, nocc)
    half = transform_slots(masked, pair_codes % per_dev, local_blocks)
    half_in, rows_in = (
        lax.all_to_all(half, "blk", split_axis=0, concat_axis=0, tiled=True),
        lax.all_to_all(pair_codes // per_dev, "blk", split_axis=0, concat_axis=0, tiled=True),
    )
    selector = (rows_in[:, None] == jnp.arange(per_dev, dtype=jnp.int32)[None, :]).astype(BF16)
    fitted = jnp.einsum("sk,spmi->pkmi", selector, half_in, preferred_element_type=jnp.float32)
    fitted = fitted.astype(BF16).reshape(paux, per_dev * width, nocc)
    partial_value = jnp.einsum(
        "nj,pni->pji", coeff, fitted, preferred_element_type=jnp.float32
    ).astype(BF16)
    occupied = lax.psum(partial_value.astype(jnp.float32).astype(BF16), "blk")
    return lax.psum_scatter(
        jnp.einsum("pnj,pji->ni", fitted, occupied, preferred_element_type=jnp.float32).astype(BF16),
        "aux",
        scatter_dimension=0,
        tiled=True,
    ).astype(jnp.float32)


LANES = 128


def after(x, *others):
    return lax.optimization_barrier((x, *others))[0]


def swap(x, axis, k):
    return lax.ppermute(x, axis, [(i, i ^ k) for i in range(4)])


def gray(k):
    return k ^ (k >> 1)


def middle(x):
    return lax.ppermute(x, "blk", [(1, 2), (2, 1)])


def inward(x):
    return lax.ppermute(x, "blk", [(0, 1), (3, 2)])


def pack_kernel(codes, counts, coeff, out, quarter, note, code, count, sems):
    part, nocc = quarter.shape
    a = lax.axis_index("aux")
    copies = (
        pltpu.make_async_copy(
            coeff.at[pl.ds(pl.multiple_of(a * part, part), part)], quarter, sems.at[0]
        ),
        pltpu.make_async_copy(codes, code, sems.at[1]),
        pltpu.make_async_copy(counts, count, sems.at[2]),
    )
    for copy in copies:
        copy.start()
    note[...] = jnp.zeros_like(note)
    for copy in copies:
        copy.wait()
    note[0:1, : code.shape[1]] = code[...].astype(jnp.float32)
    note[8:9, : count.shape[1]] = count[...].astype(jnp.float32)
    top = nocc // LANES * part
    out[top : top + META, :] = note[...].astype(BF16)
    for c in range(nocc // LANES):
        out[c * part : (c + 1) * part, :] = quarter[:, c * LANES : (c + 1) * LANES]


def stack_kernel(x, y, both):
    both[0] = x[...]
    both[1] = y[...]


def copy_kernel(x, y):
    y[...] = x[...]


def gather_quarters(coeff, at_k, refs):
    a = lax.axis_index("aux")
    part = (refs[0].shape[0] - META) * LANES // coeff.shape[1]
    for j, ref in enumerate(refs):
        at = pl.ds(pl.multiple_of(at_k * 4 * part + (a ^ j) * part, part), part)
        for c in range(coeff.shape[1] // LANES):
            coeff[at, c * LANES : (c + 1) * LANES] = ref[c * part : (c + 1) * part, :]


def place(dense, ref, notes, k, left, rows):
    z = lax.axis_index("blk")
    slots, width, _ = ref.shape
    cap = slots // 4
    for s in range(slots):
        target = s // cap
        code = notes[k, 0, s]

        @pl.when(s % cap < notes[k, 1, target])
        def _():
            row = gray(target ^ z) * rows + code // 2 * width
            col = left + code % 2 * width
            dense[
                pl.ds(pl.multiple_of(row, width), width),
                pl.ds(pl.multiple_of(col, width), width),
            ] = ref[s]


def dot(x, y):
    return jnp.dot(x, y, preferred_element_type=jnp.float32)


def dot_t(x, y):
    return lax.dot_general(x, y, (((1,), (1,)), ((), ())), preferred_element_type=jnp.float32)


def place_kernel(notes, i0, i1, dense):
    rows = dense.shape[1] // 2
    dense[...] = jnp.zeros_like(dense)
    place(dense, i0, notes, 0, 0, rows)
    place(dense, i1, notes, 1, rows, rows)


def fit(dense, dense3, coeff, first):
    two = dense.shape[1]
    rows = two // 2
    part = pl.ds(first, rows)
    fitted = dot(dense[part, :], coeff[:two, :]) + dot(dense3[part, :], coeff[two : two + rows, :])
    return dot_t(fitted.astype(BF16), coeff[...])


def first_kernel(notes, dense, i3, own, *refs):
    early, late, early2, late2, early13, late13, dense3, coeff, left, overlap = refs
    rows = own.shape[0]
    dense3[...] = jnp.zeros_like(dense3)
    place(dense3, i3, notes, 3, 0, rows)
    coeff[:rows, :] = own[...]
    for i, k in enumerate((1, 3)):
        gather_quarters(coeff, gray(k), (early.at[i], early13.at[i], early2.at[i], early13.at[2 + i]))
    gather_quarters(coeff, gray(2), (late, late13.at[0], late2, late13.at[1]))
    left[...] = fit(dense, dense3, coeff, rows)
    overlap[...] = dot_t(coeff[3 * rows :, :], coeff[...]).astype(BF16)


def chain(left, dense, dense3, dense2, coeff):
    at, total = 0, None
    for columns in (dense, dense3, dense2):
        width = columns.shape[1]
        term = dot(dot(left, columns[...]).astype(BF16), coeff[at : at + width, :])
        total = term if total is None else total + term
        at += width
    return total


def cut(total, mine, p1, p2, p3):
    a = lax.axis_index("aux")
    size = mine.shape[0]
    mine[...] = total[pl.ds(pl.multiple_of(a * size, size), size), :]
    for j, out in enumerate((p1, p2, p3), 1):
        out[...] = total[pl.ds(pl.multiple_of((a ^ j) * size, size), size), :].astype(BF16)


def end_kernel(notes, i2, dense, dense3, coeff, left, overlap, mine, p1, p2, p3, dense2, total):
    rows = total.shape[0]
    dense2[...] = jnp.zeros_like(dense2)
    place(dense2, i2, notes, 2, 0, rows)
    whole = left[...] + dot(dense2[rows : 2 * rows, :], overlap[...])
    total[...] = chain(whole.astype(BF16), dense, dense3, dense2, coeff)
    cut(total, mine, p1, p2, p3)


def own_kernel(dense, dense3, dense2, coeff, overlap, mine, p1, p2, p3, total):
    rows = total.shape[0]
    whole = fit(dense, dense3, coeff, 0) + dot(dense2[:rows, :], overlap[...])
    total[...] = chain(whole.astype(BF16), dense, dense3, dense2, coeff)
    cut(total, mine, p1, p2, p3)


def local_line(integrals, pair_codes, counts, coeff):
    slots, _, width, _ = integrals.shape
    rows, nocc = coeff.shape
    part = rows // 4
    nbf = rows * 4
    sds = jax.ShapeDtypeStruct
    vmem = pl.BlockSpec(memory_space=pltpu.VMEM)
    smem = pl.BlockSpec(memory_space=pltpu.SMEM)
    params = pltpu.CompilerParams(vmem_limit_bytes=20 * 2**20)
    cost = lambda flops, size: pl.CostEstimate(
        flops=flops, bytes_accessed=size, transcendentals=0
    )

    ints = integrals.reshape(slots, width, width)
    top = nocc // LANES * part
    packed = pl.pallas_call(
        pack_kernel,
        out_shape=sds((top + META, LANES), BF16),
        in_specs=[pl.BlockSpec(memory_space=pl.ANY)] * 3,
        out_specs=vmem,
        scratch_shapes=[
            pltpu.VMEM((part, nocc), BF16),
            pltpu.VMEM((META, LANES), jnp.float32),
            pltpu.VMEM((1, slots), jnp.int32),
            pltpu.VMEM((1, counts.shape[0]), jnp.int32),
            pltpu.SemaphoreType.DMA((3,)),
        ],
        compiler_params=pltpu.CompilerParams(vmem_limit_bytes=60 * 2**20),
        cost_estimate=cost(0, 4 * part * nocc),
    )(pair_codes[None], counts[None], coeff)

    ahead = cost(4 * 10**10, nbf * nocc * 4)
    quarter = sds((top + META, LANES), BF16)
    stack = pl.pallas_call(
        stack_kernel,
        out_shape=sds((2, top + META, LANES), BF16),
        in_specs=[vmem, vmem],
        out_specs=vmem,
        compiler_params=params,
        cost_estimate=ahead,
    )
    hold = pl.pallas_call(
        copy_kernel,
        out_shape=quarter,
        in_specs=[vmem],
        out_specs=vmem,
        compiler_params=params,
        cost_estimate=ahead,
    )
    f32 = jnp.float32
    c1 = inward(packed)
    c3 = middle(packed)
    i1 = inward(ints)
    onward = hold(c1)
    c2 = middle(onward)
    early = stack(c1, c3)
    early2 = swap(early, "aux", 2)
    i3 = middle(after(ints, onward))
    i2 = middle(i1)
    late = hold(after(c2, i1))
    late2 = swap(late, "aux", 2)
    early13 = swap(jnp.concatenate([early, early2]), "aux", 1)
    mine_late = after(packed, late)
    notes = jnp.stack([c[top::8, :slots] for c in (mine_late, c1, late, c3)]).astype(jnp.int32)
    dense = pl.pallas_call(
        place_kernel,
        out_shape=sds((nbf, 2 * rows), BF16),
        in_specs=[smem] + [vmem] * 2,
        out_specs=vmem,
        compiler_params=params,
    )(notes, ints, i1)
    late13 = swap(after(jnp.stack([late, late2]), dense), "aux", 1)
    dense3, full, left, overlap = pl.pallas_call(
        first_kernel,
        out_shape=(
            sds((nbf, rows), BF16),
            sds((nbf, nocc), BF16),
            sds((rows, nbf), f32),
            sds((rows, nbf), BF16),
        ),
        in_specs=[smem] + [vmem] * 9,
        out_specs=(vmem,) * 4,
        compiler_params=params,
    )(notes, dense, i3, coeff, early, late, early2, late2, early13, late13)
    pieces = (sds((part, nocc), f32),) + (sds((part, nocc), BF16),) * 3
    estimate = cost(2 * rows * nbf * (rows + nbf + nocc), nbf * nocc * 8)
    *end_parts, dense2 = pl.pallas_call(
        end_kernel,
        out_shape=pieces + (sds((nbf, rows), BF16),),
        in_specs=[smem] + [vmem] * 6,
        out_specs=(vmem,) * 5,
        scratch_shapes=[pltpu.VMEM((rows, nocc), f32)],
        compiler_params=params,
        cost_estimate=estimate,
    )(notes, i2, dense, dense3, full, left, overlap)
    own_parts = pl.pallas_call(
        own_kernel,
        out_shape=pieces,
        in_specs=[vmem] * 5,
        out_specs=(vmem,) * 4,
        scratch_shapes=[pltpu.VMEM((rows, nocc), f32)],
        compiler_params=params,
        cost_estimate=estimate,
    )(dense, dense3, dense2, full, overlap)

    def summed(mine, p1, p2, p3):
        got = [swap(p, "aux", k) for k, p in ((2, p2), (3, p3), (1, p1))]
        return mine + got[0].astype(f32) + got[1].astype(f32) + got[2].astype(f32)

    back = swap(summed(*end_parts).astype(BF16), "blk", 1)
    z = lax.axis_index("blk")
    return jnp.where((z == 0) | (z == 3), back.astype(f32), summed(*own_parts))


def local(integrals, pair_codes, counts, coeff):
    if lax.axis_size("blk") == 4 and lax.axis_size("aux") == 4:
        return local_line(integrals, pair_codes, counts, coeff)
    return local_long(integrals, pair_codes, counts, coeff)


def solution(mesh):
    in_specs = (
        P(("grp", "blk"), "aux", None, None),
        P(("grp", "blk")),
        P(("grp", "blk")),
        P(("grp", "blk"), None),
    )
    out_specs = P(("grp", "blk", "aux"), None)
    return jax.shard_map(local, mesh=mesh, in_specs=in_specs, out_specs=out_specs, check_vma=False)
```

```python
import functools

import jax
import jax.numpy as jnp
from jax import lax
from jax.experimental import pallas as pl
from jax.experimental.pallas import tpu as pltpu
from jax.sharding import PartitionSpec as P

BF16 = jnp.bfloat16
META = 16


def transform_slots(ints, columns, blocks):
    slots, paux, width, _ = ints.shape
    nocc = blocks.shape[2]

    def one_group(inputs):
        group_ints, group_cols = inputs
        chosen = blocks[group_cols]
        return jnp.einsum(
            "spml,sli->spmi", group_ints, chosen, preferred_element_type=jnp.float32
        ).astype(BF16)

    grouped = lax.map(
        one_group, (ints.reshape(slots // 8, 8, paux, width, width), columns.reshape(slots // 8, 8))
    )
    return grouped.reshape(slots, paux, width, nocc)


def local_long(integrals, pair_codes, counts, coeff):
    slots, paux, width, _ = integrals.shape
    nocc = coeff.shape[1]
    nblk = lax.axis_size("blk")
    per_dev = coeff.shape[0] // width
    cap = slots // nblk
    alive = (jnp.arange(cap)[None, :] < counts[:, None]).reshape(slots)
    masked = integrals * alive.astype(BF16)[:, None, None, None]
    local_blocks = coeff.reshape(per_dev, width, nocc)
    half = transform_slots(masked, pair_codes % per_dev, local_blocks)
    half_in, rows_in = (
        lax.all_to_all(half, "blk", split_axis=0, concat_axis=0, tiled=True),
        lax.all_to_all(pair_codes // per_dev, "blk", split_axis=0, concat_axis=0, tiled=True),
    )
    selector = (rows_in[:, None] == jnp.arange(per_dev, dtype=jnp.int32)[None, :]).astype(BF16)
    fitted = jnp.einsum("sk,spmi->pkmi", selector, half_in, preferred_element_type=jnp.float32)
    fitted = fitted.astype(BF16).reshape(paux, per_dev * width, nocc)
    partial_value = jnp.einsum(
        "nj,pni->pji", coeff, fitted, preferred_element_type=jnp.float32
    ).astype(BF16)
    occupied = lax.psum(partial_value.astype(jnp.float32).astype(BF16), "blk")
    return lax.psum_scatter(
        jnp.einsum("pnj,pji->ni", fitted, occupied, preferred_element_type=jnp.float32).astype(BF16),
        "aux",
        scatter_dimension=0,
        tiled=True,
    ).astype(jnp.float32)


LANES = 128


def after(x, *others):
    return lax.optimization_barrier((x, *others))[0]


def swap(x, axis, k):
    return lax.ppermute(x, axis, [(i, i ^ k) for i in range(4)])


def gray(k):
    return k ^ (k >> 1)


def middle(x):
    return lax.ppermute(x, "blk", [(1, 2), (2, 1)])


def pack_kernel(codes, counts, coeff, out, quarter, note, code, count, sems):
    part, nocc = quarter.shape
    a = lax.axis_index("aux")
    copies = (
        pltpu.make_async_copy(
            coeff.at[pl.ds(pl.multiple_of(a * part, part), part)], quarter, sems.at[0]
        ),
        pltpu.make_async_copy(codes, code, sems.at[1]),
        pltpu.make_async_copy(counts, count, sems.at[2]),
    )
    for copy in copies:
        copy.start()
    note[...] = jnp.zeros_like(note)
    for copy in copies:
        copy.wait()
    note[0:1, : code.shape[1]] = code[...].astype(jnp.float32)
    note[8:9, : count.shape[1]] = count[...].astype(jnp.float32)
    top = nocc // LANES * part
    out[top : top + META, :] = note[...].astype(BF16)
    for c in range(nocc // LANES):
        out[c * part : (c + 1) * part, :] = quarter[:, c * LANES : (c + 1) * LANES]


def stack_kernel(x, y, both):
    both[0] = x[...]
    both[1] = y[...]


def copy_kernel(x, y):
    y[...] = x[...]


def gather_quarters(coeff, at_k, refs):
    a = lax.axis_index("aux")
    part = (refs[0].shape[0] - META) * LANES // coeff.shape[1]
    for j, ref in enumerate(refs):
        at = pl.ds(pl.multiple_of(at_k * 4 * part + (a ^ j) * part, part), part)
        for c in range(coeff.shape[1] // LANES):
            coeff[at, c * LANES : (c + 1) * LANES] = ref[c * part : (c + 1) * part, :]


def place(dense, ref, codes, counts, k, left, rows):
    z = lax.axis_index("blk")
    slots, width, _ = ref.shape
    cap = slots // 4
    for s in range(slots):
        target = s // cap
        code = codes[s]

        @pl.when(s % cap < counts[target])
        def _():
            row = gray(target ^ z) * rows + code // 2 * width
            col = left + code % 2 * width
            dense[
                pl.ds(pl.multiple_of(row, width), width),
                pl.ds(pl.multiple_of(col, width), width),
            ] = ref[s]


def noted(notes, k):
    return notes.at[k - 1, 0], notes.at[k - 1, 1]


def dot(x, y):
    return jnp.dot(x, y, preferred_element_type=jnp.float32)


def dot_t(x, y):
    return lax.dot_general(x, y, (((1,), (1,)), ((), ())), preferred_element_type=jnp.float32)


def place_kernel(codes, counts, notes, i0, i1, dense):
    rows = dense.shape[1] // 2
    dense[...] = jnp.zeros_like(dense)
    place(dense, i0, codes, counts, 0, 0, rows)
    place(dense, i1, *noted(notes, 1), 1, rows, rows)


def fit(dense, dense3, coeff, first):
    two = dense.shape[1]
    rows = two // 2
    part = pl.ds(first, rows)
    fitted = dot(dense[part, :], coeff[:two, :]) + dot(dense3[part, :], coeff[two : two + rows, :])
    return dot_t(fitted.astype(BF16), coeff[...])


def first_kernel(notes, dense, i3, own, *refs):
    early, late, early2, late2, early13, late13, dense3, coeff, left, overlap = refs
    rows = own.shape[0]
    dense3[...] = jnp.zeros_like(dense3)
    place(dense3, i3, *noted(notes, 3), 3, 0, rows)
    coeff[:rows, :] = own[...]
    for i, k in enumerate((1, 3)):
        gather_quarters(coeff, gray(k), (early.at[i], early13.at[i], early2.at[i], early13.at[2 + i]))
    gather_quarters(coeff, gray(2), (late, late13.at[0], late2, late13.at[1]))
    left[...] = fit(dense, dense3, coeff, rows)
    overlap[...] = dot_t(coeff[3 * rows :, :], coeff[...]).astype(BF16)


def chain(left, dense, dense3, dense2, coeff):
    at, total = 0, None
    for columns in (dense, dense3, dense2):
        width = columns.shape[1]
        term = dot(dot(left, columns[...]).astype(BF16), coeff[at : at + width, :])
        total = term if total is None else total + term
        at += width
    return total


def cut(total, kept, given):
    a = lax.axis_index("aux")
    part = total.shape[0] // 4
    for i in (0, 2):
        at = pl.ds(i // 2 * part, part)
        kept[at, :] = total[pl.ds(pl.multiple_of((a ^ i) * part, part), part), :]
        given[at, :] = total[pl.ds(pl.multiple_of((a ^ i ^ 1) * part, part), part), :].astype(BF16)


def end_kernel(notes, i2, dense, dense3, coeff, left, overlap, kept, given, dense2, total):
    rows = total.shape[0]
    dense2[...] = jnp.zeros_like(dense2)
    place(dense2, i2, *noted(notes, 2), 2, 0, rows)
    whole = left[...] + dot(dense2[rows : 2 * rows, :], overlap[...])
    total[...] = chain(whole.astype(BF16), dense, dense3, dense2, coeff)
    cut(total, kept, given)


def own_kernel(dense, dense3, dense2, coeff, overlap, kept, given, total):
    rows = total.shape[0]
    whole = fit(dense, dense3, coeff, 0) + dot(dense2[:rows, :], overlap[...])
    total[...] = chain(whole.astype(BF16), dense, dense3, dense2, coeff)
    cut(total, kept, given)


def local_line(integrals, pair_codes, counts, coeff):
    slots, _, width, _ = integrals.shape
    rows, nocc = coeff.shape
    part = rows // 4
    nbf = rows * 4
    sds = jax.ShapeDtypeStruct
    vmem = pl.BlockSpec(memory_space=pltpu.VMEM)
    smem = pl.BlockSpec(memory_space=pltpu.SMEM)
    params = pltpu.CompilerParams(vmem_limit_bytes=20 * 2**20)
    cost = lambda flops, size: pl.CostEstimate(
        flops=flops, bytes_accessed=size, transcendentals=0
    )

    ints = integrals.reshape(slots, width, width)
    top = nocc // LANES * part
    packed = pl.pallas_call(
        pack_kernel,
        out_shape=sds((top + META, LANES), BF16),
        in_specs=[pl.BlockSpec(memory_space=pl.ANY)] * 3,
        out_specs=vmem,
        scratch_shapes=[
            pltpu.VMEM((part, nocc), BF16),
            pltpu.VMEM((META, LANES), jnp.float32),
            pltpu.VMEM((1, slots), jnp.int32),
            pltpu.VMEM((1, counts.shape[0]), jnp.int32),
            pltpu.SemaphoreType.DMA((3,)),
        ],
        compiler_params=pltpu.CompilerParams(vmem_limit_bytes=60 * 2**20),
        cost_estimate=cost(0, 4 * part * nocc),
    )(pair_codes[None], counts[None], coeff)

    ahead = cost(4 * 10**10, nbf * nocc * 4)
    quarter = sds((top + META, LANES), BF16)
    stack = pl.pallas_call(
        stack_kernel,
        out_shape=sds((2, top + META, LANES), BF16),
        in_specs=[vmem, vmem],
        out_specs=vmem,
        compiler_params=params,
        cost_estimate=ahead,
    )
    hold = pl.pallas_call(
        copy_kernel,
        out_shape=quarter,
        in_specs=[vmem],
        out_specs=vmem,
        compiler_params=params,
        cost_estimate=ahead,
    )
    f32 = jnp.float32
    c1 = swap(packed, "blk", 1)
    c3 = middle(packed)
    c2 = swap(packed, "blk", 2)
    i1 = swap(ints, "blk", 1)
    i3 = middle(ints)
    early = stack(c1, c3)
    early2 = swap(early, "aux", 2)
    i2 = middle(i1)
    late = hold(after(c2, i1))
    late2 = swap(late, "aux", 2)
    early13 = swap(jnp.concatenate([early, early2]), "aux", 1)
    notes = jnp.stack([c[top::8, :slots] for c in (c1, late, c3)]).astype(jnp.int32)
    dense = pl.pallas_call(
        place_kernel,
        out_shape=sds((nbf, 2 * rows), BF16),
        in_specs=[smem] * 3 + [vmem] * 2,
        out_specs=vmem,
        compiler_params=params,
    )(pair_codes, counts, notes, ints, i1)
    late13 = swap(after(jnp.stack([late, late2]), dense), "aux", 1)
    dense3, full, left, overlap = pl.pallas_call(
        first_kernel,
        out_shape=(
            sds((nbf, rows), BF16),
            sds((nbf, nocc), BF16),
            sds((rows, nbf), f32),
            sds((rows, nbf), BF16),
        ),
        in_specs=[smem] + [vmem] * 9,
        out_specs=(vmem,) * 4,
        compiler_params=params,
    )(notes, dense, i3, coeff, early, late, early2, late2, early13, late13)
    pieces = (sds((2 * part, nocc), f32), sds((2 * part, nocc), BF16))
    estimate = cost(2 * rows * nbf * (rows + nbf + nocc), nbf * nocc * 8)
    *end_rows, dense2 = pl.pallas_call(
        end_kernel,
        out_shape=pieces + (sds((nbf, rows), BF16),),
        in_specs=[smem] + [vmem] * 6,
        out_specs=(vmem,) * 3,
        scratch_shapes=[pltpu.VMEM((rows, nocc), f32)],
        compiler_params=params,
        cost_estimate=estimate,
    )(notes, i2, dense, dense3, full, left, overlap)
    pair = lambda kept, given: kept + swap(given, "aux", 1).astype(f32)
    ends = pair(*end_rows)
    over = ends[part:].astype(BF16)
    own_rows = pl.pallas_call(
        own_kernel,
        out_shape=pieces,
        in_specs=[vmem] * 5,
        out_specs=(vmem,) * 2,
        scratch_shapes=[pltpu.VMEM((rows, nocc), f32)],
        compiler_params=params,
        cost_estimate=estimate,
    )(dense, dense3, after(dense2, over), full, overlap)

    owns = pair(*own_rows)
    ends = ends[:part] + swap(over, "aux", 2).astype(f32)
    back = swap(ends.astype(BF16), "blk", 1)
    owns = owns[:part] + swap(owns[part:].astype(BF16), "aux", 2).astype(f32)
    z = lax.axis_index("blk")
    return jnp.where((z == 0) | (z == 3), back.astype(f32), owns)


def local(integrals, pair_codes, counts, coeff):
    if lax.axis_size("blk") == 4 and lax.axis_size("aux") == 4:
        return local_line(integrals, pair_codes, counts, coeff)
    return local_long(integrals, pair_codes, counts, coeff)


def solution(mesh):
    in_specs = (
        P(("grp", "blk"), "aux", None, None),
        P(("grp", "blk")),
        P(("grp", "blk")),
        P(("grp", "blk"), None),
    )
    out_specs = P(("grp", "blk", "aux"), None)
    return jax.shard_map(local, mesh=mesh, in_specs=in_specs, out_specs=out_specs, check_vma=False)
```

```python
import functools

import jax
import jax.numpy as jnp
from jax import lax
from jax.experimental import pallas as pl
from jax.experimental.pallas import tpu as pltpu
from jax.sharding import PartitionSpec as P

BF16 = jnp.bfloat16
META = 16


def transform_slots(ints, columns, blocks):
    slots, paux, width, _ = ints.shape
    nocc = blocks.shape[2]

    def one_group(inputs):
        group_ints, group_cols = inputs
        chosen = blocks[group_cols]
        return jnp.einsum(
            "spml,sli->spmi", group_ints, chosen, preferred_element_type=jnp.float32
        ).astype(BF16)

    grouped = lax.map(
        one_group, (ints.reshape(slots // 8, 8, paux, width, width), columns.reshape(slots // 8, 8))
    )
    return grouped.reshape(slots, paux, width, nocc)


def local_long(integrals, pair_codes, counts, coeff):
    slots, paux, width, _ = integrals.shape
    nocc = coeff.shape[1]
    nblk = lax.axis_size("blk")
    per_dev = coeff.shape[0] // width
    cap = slots // nblk
    alive = (jnp.arange(cap)[None, :] < counts[:, None]).reshape(slots)
    masked = integrals * alive.astype(BF16)[:, None, None, None]
    local_blocks = coeff.reshape(per_dev, width, nocc)
    half = transform_slots(masked, pair_codes % per_dev, local_blocks)
    half_in, rows_in = (
        lax.all_to_all(half, "blk", split_axis=0, concat_axis=0, tiled=True),
        lax.all_to_all(pair_codes // per_dev, "blk", split_axis=0, concat_axis=0, tiled=True),
    )
    selector = (rows_in[:, None] == jnp.arange(per_dev, dtype=jnp.int32)[None, :]).astype(BF16)
    fitted = jnp.einsum("sk,spmi->pkmi", selector, half_in, preferred_element_type=jnp.float32)
    fitted = fitted.astype(BF16).reshape(paux, per_dev * width, nocc)
    partial_value = jnp.einsum(
        "nj,pni->pji", coeff, fitted, preferred_element_type=jnp.float32
    ).astype(BF16)
    occupied = lax.psum(partial_value.astype(jnp.float32).astype(BF16), "blk")
    return lax.psum_scatter(
        jnp.einsum("pnj,pji->ni", fitted, occupied, preferred_element_type=jnp.float32).astype(BF16),
        "aux",
        scatter_dimension=0,
        tiled=True,
    ).astype(jnp.float32)


LANES = 128


def after(x, *others):
    return lax.optimization_barrier((x, *others))[0]


def swap(x, axis, k):
    return lax.ppermute(x, axis, [(i, i ^ k) for i in range(4)])


def gray(k):
    return k ^ (k >> 1)


def middle(x):
    return lax.ppermute(x, "blk", [(1, 2), (2, 1)])


def pack_kernel(codes, counts, coeff, out, quarter, note, code, count, sems):
    part, nocc = quarter.shape
    a = lax.axis_index("aux")
    copies = (
        pltpu.make_async_copy(
            coeff.at[pl.ds(pl.multiple_of(a * part, part), part)], quarter, sems.at[0]
        ),
        pltpu.make_async_copy(codes, code, sems.at[1]),
        pltpu.make_async_copy(counts, count, sems.at[2]),
    )
    for copy in copies:
        copy.start()
    note[...] = jnp.zeros_like(note)
    for copy in copies:
        copy.wait()
    note[0:1, : code.shape[1]] = code[...].astype(jnp.float32)
    note[8:9, : count.shape[1]] = count[...].astype(jnp.float32)
    top = nocc // LANES * part
    out[top : top + META, :] = note[...].astype(BF16)
    for c in range(nocc // LANES):
        out[c * part : (c + 1) * part, :] = quarter[:, c * LANES : (c + 1) * LANES]


def stack_kernel(x, y, both):
    both[0] = x[...]
    both[1] = y[...]


def copy_kernel(x, y):
    y[...] = x[...]


def gather_quarters(coeff, at_k, refs):
    a = lax.axis_index("aux")
    part = (refs[0].shape[0] - META) * LANES // coeff.shape[1]
    for j, ref in enumerate(refs):
        at = pl.ds(pl.multiple_of(at_k * 4 * part + (a ^ j) * part, part), part)
        for c in range(coeff.shape[1] // LANES):
            coeff[at, c * LANES : (c + 1) * LANES] = ref[c * part : (c + 1) * part, :]


def place(dense, ref, codes, counts, k, left, rows):
    z = lax.axis_index("blk")
    slots, width, _ = ref.shape
    cap = slots // 4
    for s in range(slots):
        target = s // cap
        code = codes[s]

        @pl.when(s % cap < counts[target])
        def _():
            row = gray(target ^ z) * rows + code // 2 * width
            col = left + code % 2 * width
            dense[
                pl.ds(pl.multiple_of(row, width), width),
                pl.ds(pl.multiple_of(col, width), width),
            ] = ref[s]


def noted(notes, k):
    return notes.at[k - 1, 0], notes.at[k - 1, 1]


def dot(x, y):
    return jnp.dot(x, y, preferred_element_type=jnp.float32)


def dot_t(x, y):
    return lax.dot_general(x, y, (((1,), (1,)), ((), ())), preferred_element_type=jnp.float32)


def place_kernel(codes, counts, notes, i0, i1, dense):
    rows = dense.shape[1] // 2
    dense[...] = jnp.zeros_like(dense)
    place(dense, i0, codes, counts, 0, 0, rows)
    place(dense, i1, *noted(notes, 1), 1, rows, rows)


def first_kernel(notes, dense, i3, own, *refs):
    early, late, early2, late2, early13, late13, dense3, coeff, left, overlap = refs
    rows = own.shape[0]
    dense3[...] = jnp.zeros_like(dense3)
    place(dense3, i3, *noted(notes, 3), 3, 0, rows)
    coeff[:rows, :] = own[...]
    for i, k in enumerate((1, 3)):
        gather_quarters(coeff, gray(k), (early.at[i], early13.at[i], early2.at[i], early13.at[2 + i]))
    gather_quarters(coeff, gray(2), (late, late13.at[0], late2, late13.at[1]))
    two = 2 * rows
    fitted = dot(dense[:two, :], coeff[:two, :]) + dot(dense3[:two, :], coeff[two : 3 * rows, :])
    left[...] = dot_t(fitted.astype(BF16), coeff[...])
    overlap[...] = dot_t(coeff[3 * rows :, :], coeff[...]).astype(BF16)


def chain(left, dense, dense3, dense2, coeff):
    at, total = 0, None
    for columns in (dense, dense3, dense2):
        width = columns.shape[1]
        term = dot(dot(left, columns[...]).astype(BF16), coeff[at : at + width, :])
        total = term if total is None else total + term
        at += width
    return total


def cut(total, mine, p1, p2, p3):
    a = lax.axis_index("aux")
    size = mine.shape[0]
    mine[...] = total[pl.ds(pl.multiple_of(a * size, size), size), :]
    for j, out in enumerate((p1, p2, p3), 1):
        out[...] = total[pl.ds(pl.multiple_of((a ^ j) * size, size), size), :].astype(BF16)


def end_kernel(notes, i2, dense, dense3, coeff, left, overlap, mine, p1, p2, p3, dense2, total):
    rows = total.shape[0]
    dense2[...] = jnp.zeros_like(dense2)
    place(dense2, i2, *noted(notes, 2), 2, 0, rows)
    whole = left[rows:, :] + dot(dense2[rows : 2 * rows, :], overlap[...])
    total[...] = chain(whole.astype(BF16), dense, dense3, dense2, coeff)
    cut(total, mine, p1, p2, p3)


def own_kernel(dense, dense3, dense2, coeff, left, overlap, mine, p1, p2, p3, total):
    rows = total.shape[0]
    whole = left[:rows, :] + dot(dense2[:rows, :], overlap[...])
    total[...] = chain(whole.astype(BF16), dense, dense3, dense2, coeff)
    cut(total, mine, p1, p2, p3)


def local_line(integrals, pair_codes, counts, coeff):
    slots, _, width, _ = integrals.shape
    rows, nocc = coeff.shape
    part = rows // 4
    nbf = rows * 4
    sds = jax.ShapeDtypeStruct
    vmem = pl.BlockSpec(memory_space=pltpu.VMEM)
    smem = pl.BlockSpec(memory_space=pltpu.SMEM)
    params = pltpu.CompilerParams(vmem_limit_bytes=20 * 2**20)
    cost = lambda flops, size: pl.CostEstimate(
        flops=flops, bytes_accessed=size, transcendentals=0
    )

    ints = integrals.reshape(slots, width, width)
    top = nocc // LANES * part
    packed = pl.pallas_call(
        pack_kernel,
        out_shape=sds((top + META, LANES), BF16),
        in_specs=[pl.BlockSpec(memory_space=pl.ANY)] * 3,
        out_specs=vmem,
        scratch_shapes=[
            pltpu.VMEM((part, nocc), BF16),
            pltpu.VMEM((META, LANES), jnp.float32),
            pltpu.VMEM((1, slots), jnp.int32),
            pltpu.VMEM((1, counts.shape[0]), jnp.int32),
            pltpu.SemaphoreType.DMA((3,)),
        ],
        compiler_params=pltpu.CompilerParams(vmem_limit_bytes=60 * 2**20),
        cost_estimate=cost(0, 4 * part * nocc),
    )(pair_codes[None], counts[None], coeff)

    ahead = cost(4 * 10**10, nbf * nocc * 4)
    quarter = sds((top + META, LANES), BF16)
    stack = pl.pallas_call(
        stack_kernel,
        out_shape=sds((2, top + META, LANES), BF16),
        in_specs=[vmem, vmem],
        out_specs=vmem,
        compiler_params=params,
        cost_estimate=ahead,
    )
    hold = pl.pallas_call(
        copy_kernel,
        out_shape=quarter,
        in_specs=[vmem],
        out_specs=vmem,
        compiler_params=params,
        cost_estimate=ahead,
    )
    f32 = jnp.float32
    c1 = swap(packed, "blk", 1)
    c3 = middle(packed)
    i1 = swap(ints, "blk", 1)
    onward = hold(c1)
    c2 = middle(onward)
    early = stack(c1, c3)
    early2 = swap(early, "aux", 2)
    i3 = middle(after(ints, onward))
    i2 = middle(i1)
    late = hold(after(c2, i1))
    late2 = swap(late, "aux", 2)
    early13 = swap(jnp.concatenate([early, early2]), "aux", 1)
    notes = jnp.stack([c[top::8, :slots] for c in (c1, late, c3)]).astype(jnp.int32)
    dense = pl.pallas_call(
        place_kernel,
        out_shape=sds((nbf, 2 * rows), BF16),
        in_specs=[smem] * 3 + [vmem] * 2,
        out_specs=vmem,
        compiler_params=params,
    )(pair_codes, counts, notes, ints, i1)
    late13 = swap(after(jnp.stack([late, late2]), dense), "aux", 1)
    dense3, full, left, overlap = pl.pallas_call(
        first_kernel,
        out_shape=(
            sds((nbf, rows), BF16),
            sds((nbf, nocc), BF16),
            sds((2 * rows, nbf), f32),
            sds((rows, nbf), BF16),
        ),
        in_specs=[smem] + [vmem] * 9,
        out_specs=(vmem,) * 4,
        compiler_params=params,
    )(notes, dense, i3, coeff, early, late, early2, late2, early13, late13)
    pieces = (sds((part, nocc), f32),) + (sds((part, nocc), BF16),) * 3
    estimate = cost(2 * rows * nbf * (rows + nbf + nocc), nbf * nocc * 8)
    *end_rows, dense2 = pl.pallas_call(
        end_kernel,
        out_shape=pieces + (sds((nbf, rows), BF16),),
        in_specs=[smem] + [vmem] * 6,
        out_specs=(vmem,) * 5,
        scratch_shapes=[pltpu.VMEM((rows, nocc), f32)],
        compiler_params=params,
        cost_estimate=estimate,
    )(notes, i2, dense, dense3, full, left, overlap)
    own_rows = pl.pallas_call(
        own_kernel,
        out_shape=pieces,
        in_specs=[vmem] * 6,
        out_specs=(vmem,) * 4,
        scratch_shapes=[pltpu.VMEM((rows, nocc), f32)],
        compiler_params=params,
        cost_estimate=estimate,
    )(dense, dense3, dense2, full, left, overlap)

    def summed(mine, p1, p2, p3):
        got = [swap(p, "aux", k) for k, p in ((2, p2), (3, p3), (1, p1))]
        return mine + got[0].astype(f32) + got[1].astype(f32) + got[2].astype(f32)

    ends = summed(*end_rows).astype(BF16)
    back = swap(ends, "blk", 1)
    mine, p1, p2, p3 = own_rows
    owns = summed(mine, p1, p2, p3)
    z = lax.axis_index("blk")
    return jnp.where((z == 0) | (z == 3), back.astype(f32), owns)


def local(integrals, pair_codes, counts, coeff):
    if lax.axis_size("blk") == 4 and lax.axis_size("aux") == 4:
        return local_line(integrals, pair_codes, counts, coeff)
    return local_long(integrals, pair_codes, counts, coeff)


def solution(mesh):
    in_specs = (
        P(("grp", "blk"), "aux", None, None),
        P(("grp", "blk")),
        P(("grp", "blk")),
        P(("grp", "blk"), None),
    )
    out_specs = P(("grp", "blk", "aux"), None)
    return jax.shard_map(local, mesh=mesh, in_specs=in_specs, out_specs=out_specs, check_vma=False)
```

```python
import functools

import jax
import jax.numpy as jnp
from jax import lax
from jax.experimental import pallas as pl
from jax.experimental.pallas import tpu as pltpu
from jax.sharding import PartitionSpec as P

BF16 = jnp.bfloat16
META = 16


def transform_slots(ints, columns, blocks):
    slots, paux, width, _ = ints.shape
    nocc = blocks.shape[2]

    def one_group(inputs):
        group_ints, group_cols = inputs
        chosen = blocks[group_cols]
        return jnp.einsum(
            "spml,sli->spmi", group_ints, chosen, preferred_element_type=jnp.float32
        ).astype(BF16)

    grouped = lax.map(
        one_group, (ints.reshape(slots // 8, 8, paux, width, width), columns.reshape(slots // 8, 8))
    )
    return grouped.reshape(slots, paux, width, nocc)


def local_long(integrals, pair_codes, counts, coeff):
    slots, paux, width, _ = integrals.shape
    nocc = coeff.shape[1]
    nblk = lax.axis_size("blk")
    per_dev = coeff.shape[0] // width
    cap = slots // nblk
    alive = (jnp.arange(cap)[None, :] < counts[:, None]).reshape(slots)
    masked = integrals * alive.astype(BF16)[:, None, None, None]
    local_blocks = coeff.reshape(per_dev, width, nocc)
    half = transform_slots(masked, pair_codes % per_dev, local_blocks)
    half_in, rows_in = (
        lax.all_to_all(half, "blk", split_axis=0, concat_axis=0, tiled=True),
        lax.all_to_all(pair_codes // per_dev, "blk", split_axis=0, concat_axis=0, tiled=True),
    )
    selector = (rows_in[:, None] == jnp.arange(per_dev, dtype=jnp.int32)[None, :]).astype(BF16)
    fitted = jnp.einsum("sk,spmi->pkmi", selector, half_in, preferred_element_type=jnp.float32)
    fitted = fitted.astype(BF16).reshape(paux, per_dev * width, nocc)
    partial_value = jnp.einsum(
        "nj,pni->pji", coeff, fitted, preferred_element_type=jnp.float32
    ).astype(BF16)
    occupied = lax.psum(partial_value.astype(jnp.float32).astype(BF16), "blk")
    return lax.psum_scatter(
        jnp.einsum("pnj,pji->ni", fitted, occupied, preferred_element_type=jnp.float32).astype(BF16),
        "aux",
        scatter_dimension=0,
        tiled=True,
    ).astype(jnp.float32)


LANES = 128


def after(x, *others):
    return lax.optimization_barrier((x, *others))[0]


def swap(x, axis, k):
    return lax.ppermute(x, axis, [(i, i ^ k) for i in range(4)])


def gray(k):
    return k ^ (k >> 1)


def middle(x):
    return lax.ppermute(x, "blk", [(1, 2), (2, 1)])


def inward(x):
    return lax.ppermute(x, "blk", [(0, 1), (3, 2)])


def pack_kernel(codes, counts, coeff, out, quarter, note, code, count, sems):
    part, nocc = quarter.shape
    a = lax.axis_index("aux")
    copies = (
        pltpu.make_async_copy(
            coeff.at[pl.ds(pl.multiple_of(a * part, part), part)], quarter, sems.at[0]
        ),
        pltpu.make_async_copy(codes, code, sems.at[1]),
        pltpu.make_async_copy(counts, count, sems.at[2]),
    )
    for copy in copies:
        copy.start()
    note[...] = jnp.zeros_like(note)
    for copy in copies:
        copy.wait()
    note[0:1, : code.shape[1]] = code[...].astype(jnp.float32)
    note[8:9, : count.shape[1]] = count[...].astype(jnp.float32)
    top = nocc // LANES * part
    out[top : top + META, :] = note[...].astype(BF16)
    for c in range(nocc // LANES):
        out[c * part : (c + 1) * part, :] = quarter[:, c * LANES : (c + 1) * LANES]


def stack_kernel(x, y, both):
    both[0] = x[...]
    both[1] = y[...]


def copy_kernel(x, y):
    y[...] = x[...]


def gather_quarters(coeff, at_k, refs):
    a = lax.axis_index("aux")
    part = (refs[0].shape[0] - META) * LANES // coeff.shape[1]
    for j, ref in enumerate(refs):
        at = pl.ds(pl.multiple_of(at_k * 4 * part + (a ^ j) * part, part), part)
        for c in range(coeff.shape[1] // LANES):
            coeff[at, c * LANES : (c + 1) * LANES] = ref[c * part : (c + 1) * part, :]


def place(dense, ref, codes, counts, k, left, rows):
    z = lax.axis_index("blk")
    slots, width, _ = ref.shape
    cap = slots // 4
    for s in range(slots):
        target = s // cap
        code = codes[s]

        @pl.when(s % cap < counts[target])
        def _():
            row = gray(target ^ z) * rows + code // 2 * width
            col = left + code % 2 * width
            dense[
                pl.ds(pl.multiple_of(row, width), width),
                pl.ds(pl.multiple_of(col, width), width),
            ] = ref[s]


def noted(notes, k):
    return notes.at[k - 1, 0], notes.at[k - 1, 1]


def dot(x, y):
    return jnp.dot(x, y, preferred_element_type=jnp.float32)


def dot_t(x, y):
    return lax.dot_general(x, y, (((1,), (1,)), ((), ())), preferred_element_type=jnp.float32)


def in_middle(kernel):
    def run(*refs):
        z = lax.axis_index("blk")

        @pl.when((z == 1) | (z == 2))
        def _():
            kernel(*refs)

    return run


@in_middle
def place_kernel(codes, counts, notes, i0, i1, dense):
    rows = dense.shape[1] // 2
    dense[...] = jnp.zeros_like(dense)
    place(dense, i0, codes, counts, 0, 0, rows)
    place(dense, i1, *noted(notes, 1), 1, rows, rows)


@in_middle
def first_kernel(notes, dense, i3, own, *refs):
    early, late, early2, late2, early13, late13, dense3, coeff, left, overlap = refs
    rows = own.shape[0]
    dense3[...] = jnp.zeros_like(dense3)
    place(dense3, i3, *noted(notes, 3), 3, 0, rows)
    coeff[:rows, :] = own[...]
    for i, k in enumerate((1, 3)):
        gather_quarters(coeff, gray(k), (early.at[i], early13.at[i], early2.at[i], early13.at[2 + i]))
    gather_quarters(coeff, gray(2), (late, late13.at[0], late2, late13.at[1]))
    two = 2 * rows
    fitted = dot(dense[:two, :], coeff[:two, :]) + dot(dense3[:two, :], coeff[two : 3 * rows, :])
    left[...] = dot_t(fitted.astype(BF16), coeff[...])
    overlap[...] = dot_t(coeff[3 * rows :, :], coeff[...]).astype(BF16)


def chain(left, dense, dense3, dense2, coeff):
    at, total = 0, None
    for columns in (dense, dense3, dense2):
        width = columns.shape[1]
        term = dot(dot(left, columns[...]).astype(BF16), coeff[at : at + width, :])
        total = term if total is None else total + term
        at += width
    return total


def cut(total, mine, p1, p2, p3):
    a = lax.axis_index("aux")
    size = mine.shape[0]
    mine[...] = total[pl.ds(pl.multiple_of(a * size, size), size), :]
    for j, out in enumerate((p1, p2, p3), 1):
        out[...] = total[pl.ds(pl.multiple_of((a ^ j) * size, size), size), :].astype(BF16)


@in_middle
def end_kernel(notes, i2, dense, dense3, coeff, left, overlap, mine, p1, p2, p3, dense2, total):
    rows = total.shape[0]
    dense2[...] = jnp.zeros_like(dense2)
    place(dense2, i2, *noted(notes, 2), 2, 0, rows)
    whole = left[rows:, :] + dot(dense2[rows : 2 * rows, :], overlap[...])
    total[...] = chain(whole.astype(BF16), dense, dense3, dense2, coeff)
    cut(total, mine, p1, p2, p3)


@in_middle
def own_kernel(dense, dense3, dense2, coeff, left, overlap, mine, p1, p2, p3, total):
    rows = total.shape[0]
    whole = left[:rows, :] + dot(dense2[:rows, :], overlap[...])
    total[...] = chain(whole.astype(BF16), dense, dense3, dense2, coeff)
    cut(total, mine, p1, p2, p3)


def local_line(integrals, pair_codes, counts, coeff):
    slots, _, width, _ = integrals.shape
    rows, nocc = coeff.shape
    part = rows // 4
    nbf = rows * 4
    sds = jax.ShapeDtypeStruct
    vmem = pl.BlockSpec(memory_space=pltpu.VMEM)
    smem = pl.BlockSpec(memory_space=pltpu.SMEM)
    params = pltpu.CompilerParams(vmem_limit_bytes=20 * 2**20)
    cost = lambda flops, size: pl.CostEstimate(
        flops=flops, bytes_accessed=size, transcendentals=0
    )

    ints = integrals.reshape(slots, width, width)
    top = nocc // LANES * part
    packed = pl.pallas_call(
        pack_kernel,
        out_shape=sds((top + META, LANES), BF16),
        in_specs=[pl.BlockSpec(memory_space=pl.ANY)] * 3,
        out_specs=vmem,
        scratch_shapes=[
            pltpu.VMEM((part, nocc), BF16),
            pltpu.VMEM((META, LANES), jnp.float32),
            pltpu.VMEM((1, slots), jnp.int32),
            pltpu.VMEM((1, counts.shape[0]), jnp.int32),
            pltpu.SemaphoreType.DMA((3,)),
        ],
        compiler_params=pltpu.CompilerParams(vmem_limit_bytes=60 * 2**20),
        cost_estimate=cost(0, 4 * part * nocc),
    )(pair_codes[None], counts[None], coeff)

    ahead = cost(4 * 10**10, nbf * nocc * 4)
    quarter = sds((top + META, LANES), BF16)
    stack = pl.pallas_call(
        stack_kernel,
        out_shape=sds((2, top + META, LANES), BF16),
        in_specs=[vmem, vmem],
        out_specs=vmem,
        compiler_params=params,
        cost_estimate=ahead,
    )
    hold = pl.pallas_call(
        copy_kernel,
        out_shape=quarter,
        in_specs=[vmem],
        out_specs=vmem,
        compiler_params=params,
        cost_estimate=ahead,
    )
    f32 = jnp.float32
    c1 = swap(packed, "blk", 1)
    c3 = middle(packed)
    i1 = inward(ints)
    onward = hold(c1)
    c2 = middle(onward)
    early = stack(c1, c3)
    early2 = swap(early, "aux", 2)
    i3 = middle(after(ints, onward))
    i2 = middle(i1)
    late = hold(after(c2, i1))
    late2 = swap(late, "aux", 2)
    early13 = swap(jnp.concatenate([early, early2]), "aux", 1)
    notes = jnp.stack([c[top::8, :slots] for c in (c1, late, c3)]).astype(jnp.int32)
    dense = pl.pallas_call(
        place_kernel,
        out_shape=sds((nbf, 2 * rows), BF16),
        in_specs=[smem] * 3 + [vmem] * 2,
        out_specs=vmem,
        compiler_params=params,
    )(pair_codes, counts, notes, ints, i1)
    late13 = swap(after(jnp.stack([late, late2]), dense), "aux", 1)
    dense3, full, left, overlap = pl.pallas_call(
        first_kernel,
        out_shape=(
            sds((nbf, rows), BF16),
            sds((nbf, nocc), BF16),
            sds((2 * rows, nbf), f32),
            sds((rows, nbf), BF16),
        ),
        in_specs=[smem] + [vmem] * 9,
        out_specs=(vmem,) * 4,
        compiler_params=params,
    )(notes, dense, i3, coeff, early, late, early2, late2, early13, late13)
    pieces = (sds((part, nocc), f32),) + (sds((part, nocc), BF16),) * 3
    estimate = cost(2 * rows * nbf * (rows + nbf + nocc), nbf * nocc * 8)
    *end_rows, dense2 = pl.pallas_call(
        end_kernel,
        out_shape=pieces + (sds((nbf, rows), BF16),),
        in_specs=[smem] + [vmem] * 6,
        out_specs=(vmem,) * 5,
        scratch_shapes=[pltpu.VMEM((rows, nocc), f32)],
        compiler_params=params,
        cost_estimate=estimate,
    )(notes, i2, dense, dense3, full, left, overlap)
    own_rows = pl.pallas_call(
        own_kernel,
        out_shape=pieces,
        in_specs=[vmem] * 6,
        out_specs=(vmem,) * 4,
        scratch_shapes=[pltpu.VMEM((rows, nocc), f32)],
        compiler_params=params,
        cost_estimate=estimate,
    )(dense, dense3, dense2, full, left, overlap)

    def summed(mine, p1, p2, p3):
        got = [swap(p, "aux", k) for k, p in ((2, p2), (3, p3), (1, p1))]
        return mine + got[0].astype(f32) + got[1].astype(f32) + got[2].astype(f32)

    ends = summed(*end_rows).astype(BF16)
    back = swap(ends, "blk", 1)
    mine, p1, p2, p3 = own_rows
    owns = summed(mine, p1, p2, p3)
    z = lax.axis_index("blk")
    return jnp.where((z == 0) | (z == 3), back.astype(f32), owns)


def local(integrals, pair_codes, counts, coeff):
    if lax.axis_size("blk") == 4 and lax.axis_size("aux") == 4:
        return local_line(integrals, pair_codes, counts, coeff)
    return local_long(integrals, pair_codes, counts, coeff)


def solution(mesh):
    in_specs = (
        P(("grp", "blk"), "aux", None, None),
        P(("grp", "blk")),
        P(("grp", "blk")),
        P(("grp", "blk"), None),
    )
    out_specs = P(("grp", "blk", "aux"), None)
    return jax.shard_map(local, mesh=mesh, in_specs=in_specs, out_specs=out_specs, check_vma=False)
```

```python
import functools

import jax
import jax.numpy as jnp
from jax import lax
from jax.experimental import pallas as pl
from jax.experimental.pallas import tpu as pltpu
from jax.sharding import PartitionSpec as P

BF16 = jnp.bfloat16
META = 16


def transform_slots(ints, columns, blocks):
    slots, paux, width, _ = ints.shape
    nocc = blocks.shape[2]

    def one_group(inputs):
        group_ints, group_cols = inputs
        chosen = blocks[group_cols]
        return jnp.einsum(
            "spml,sli->spmi", group_ints, chosen, preferred_element_type=jnp.float32
        ).astype(BF16)

    grouped = lax.map(
        one_group, (ints.reshape(slots // 8, 8, paux, width, width), columns.reshape(slots // 8, 8))
    )
    return grouped.reshape(slots, paux, width, nocc)


def local_long(integrals, pair_codes, counts, coeff):
    slots, paux, width, _ = integrals.shape
    nocc = coeff.shape[1]
    nblk = lax.axis_size("blk")
    per_dev = coeff.shape[0] // width
    cap = slots // nblk
    alive = (jnp.arange(cap)[None, :] < counts[:, None]).reshape(slots)
    masked = integrals * alive.astype(BF16)[:, None, None, None]
    local_blocks = coeff.reshape(per_dev, width, nocc)
    half = transform_slots(masked, pair_codes % per_dev, local_blocks)
    half_in, rows_in = (
        lax.all_to_all(half, "blk", split_axis=0, concat_axis=0, tiled=True),
        lax.all_to_all(pair_codes // per_dev, "blk", split_axis=0, concat_axis=0, tiled=True),
    )
    selector = (rows_in[:, None] == jnp.arange(per_dev, dtype=jnp.int32)[None, :]).astype(BF16)
    fitted = jnp.einsum("sk,spmi->pkmi", selector, half_in, preferred_element_type=jnp.float32)
    fitted = fitted.astype(BF16).reshape(paux, per_dev * width, nocc)
    partial_value = jnp.einsum(
        "nj,pni->pji", coeff, fitted, preferred_element_type=jnp.float32
    ).astype(BF16)
    occupied = lax.psum(partial_value.astype(jnp.float32).astype(BF16), "blk")
    return lax.psum_scatter(
        jnp.einsum("pnj,pji->ni", fitted, occupied, preferred_element_type=jnp.float32).astype(BF16),
        "aux",
        scatter_dimension=0,
        tiled=True,
    ).astype(jnp.float32)


LANES = 128


def after(x, *others):
    return lax.optimization_barrier((x, *others))[0]


def swap(x, axis, k):
    return lax.ppermute(x, axis, [(i, i ^ k) for i in range(4)])


def gray(k):
    return k ^ (k >> 1)


def middle(x):
    return lax.ppermute(x, "blk", [(1, 2), (2, 1)])


def inward(x):
    return lax.ppermute(x, "blk", [(0, 1), (3, 2)])


def pack_kernel(codes, counts, coeff, out, quarter, note, code, count, sems):
    part, nocc = quarter.shape
    a = lax.axis_index("aux")
    copies = (
        pltpu.make_async_copy(
            coeff.at[pl.ds(pl.multiple_of(a * part, part), part)], quarter, sems.at[0]
        ),
        pltpu.make_async_copy(codes, code, sems.at[1]),
        pltpu.make_async_copy(counts, count, sems.at[2]),
    )
    for copy in copies:
        copy.start()
    note[...] = jnp.zeros_like(note)
    for copy in copies:
        copy.wait()
    note[0:1, : code.shape[1]] = code[...].astype(jnp.float32)
    note[8:9, : count.shape[1]] = count[...].astype(jnp.float32)
    top = nocc // LANES * part
    out[top : top + META, :] = note[...].astype(BF16)
    for c in range(nocc // LANES):
        out[c * part : (c + 1) * part, :] = quarter[:, c * LANES : (c + 1) * LANES]


def stack_kernel(x, y, both):
    both[0] = x[...]
    both[1] = y[...]


def copy_kernel(x, y):
    y[...] = x[...]


def gather_quarters(coeff, at_k, refs):
    a = lax.axis_index("aux")
    part = (refs[0].shape[0] - META) * LANES // coeff.shape[1]
    for j, ref in enumerate(refs):
        at = pl.ds(pl.multiple_of(at_k * 4 * part + (a ^ j) * part, part), part)
        for c in range(coeff.shape[1] // LANES):
            coeff[at, c * LANES : (c + 1) * LANES] = ref[c * part : (c + 1) * part, :]


def place(dense, ref, codes, counts, k, left, rows):
    z = lax.axis_index("blk")
    slots, width, _ = ref.shape
    cap = slots // 4
    for s in range(slots):
        target = s // cap
        code = codes[s]

        @pl.when(s % cap < counts[target])
        def _():
            row = gray(target ^ z) * rows + code // 2 * width
            col = left + code % 2 * width
            dense[
                pl.ds(pl.multiple_of(row, width), width),
                pl.ds(pl.multiple_of(col, width), width),
            ] = ref[s]


def noted(notes, k):
    return notes.at[k - 1, 0], notes.at[k - 1, 1]


def dot(x, y):
    return jnp.dot(x, y, preferred_element_type=jnp.float32)


def dot_t(x, y):
    return lax.dot_general(x, y, (((1,), (1,)), ((), ())), preferred_element_type=jnp.float32)


def in_middle(kernel):
    def run(*refs):
        z = lax.axis_index("blk")

        @pl.when((z == 1) | (z == 2))
        def _():
            kernel(*refs)

    return run


@in_middle
def place_kernel(codes, counts, notes, i0, i1, dense):
    rows = dense.shape[1] // 2
    dense[...] = jnp.zeros_like(dense)
    place(dense, i0, codes, counts, 0, 0, rows)
    place(dense, i1, *noted(notes, 1), 1, rows, rows)


@in_middle
def first_kernel(notes, dense, i3, own, *refs):
    early, late, early2, late2, early13, late13, dense3, coeff, left, overlap = refs
    rows = own.shape[0]
    dense3[...] = jnp.zeros_like(dense3)
    place(dense3, i3, *noted(notes, 3), 3, 0, rows)
    coeff[:rows, :] = own[...]
    for i, k in enumerate((1, 3)):
        gather_quarters(coeff, gray(k), (early.at[i], early13.at[i], early2.at[i], early13.at[2 + i]))
    gather_quarters(coeff, gray(2), (late, late13.at[0], late2, late13.at[1]))
    two = 2 * rows
    fitted = dot(dense[:two, :], coeff[:two, :]) + dot(dense3[:two, :], coeff[two : 3 * rows, :])
    left[...] = dot_t(fitted.astype(BF16), coeff[...])
    overlap[...] = dot_t(coeff[3 * rows :, :], coeff[...]).astype(BF16)


def chain(left, dense, dense3, dense2, coeff):
    at, total = 0, None
    for columns in (dense, dense3, dense2):
        width = columns.shape[1]
        term = dot(dot(left, columns[...]).astype(BF16), coeff[at : at + width, :])
        total = term if total is None else total + term
        at += width
    return total


def cut(total, mine, p1, p2, p3):
    a = lax.axis_index("aux")
    size = mine.shape[0]
    mine[...] = total[pl.ds(pl.multiple_of(a * size, size), size), :]
    for j, out in enumerate((p1, p2, p3), 1):
        out[...] = total[pl.ds(pl.multiple_of((a ^ j) * size, size), size), :].astype(BF16)


@in_middle
def end_kernel(notes, i2, dense, dense3, coeff, left, overlap, mine, p1, p2, p3, dense2, total):
    rows = total.shape[0]
    dense2[...] = jnp.zeros_like(dense2)
    place(dense2, i2, *noted(notes, 2), 2, 0, rows)
    whole = left[rows:, :] + dot(dense2[rows : 2 * rows, :], overlap[...])
    total[...] = chain(whole.astype(BF16), dense, dense3, dense2, coeff)
    cut(total, mine, p1, p2, p3)


@in_middle
def own_kernel(dense, dense3, dense2, coeff, left, overlap, mine, p1, p2, p3, total):
    rows = total.shape[0]
    whole = left[:rows, :] + dot(dense2[:rows, :], overlap[...])
    total[...] = chain(whole.astype(BF16), dense, dense3, dense2, coeff)
    cut(total, mine, p1, p2, p3)


def local_line(integrals, pair_codes, counts, coeff):
    slots, _, width, _ = integrals.shape
    rows, nocc = coeff.shape
    part = rows // 4
    nbf = rows * 4
    sds = jax.ShapeDtypeStruct
    vmem = pl.BlockSpec(memory_space=pltpu.VMEM)
    smem = pl.BlockSpec(memory_space=pltpu.SMEM)
    params = pltpu.CompilerParams(vmem_limit_bytes=20 * 2**20)
    cost = lambda flops, size: pl.CostEstimate(
        flops=flops, bytes_accessed=size, transcendentals=0
    )

    ints = integrals.reshape(slots, width, width)
    top = nocc // LANES * part
    packed = pl.pallas_call(
        pack_kernel,
        out_shape=sds((top + META, LANES), BF16),
        in_specs=[pl.BlockSpec(memory_space=pl.ANY)] * 3,
        out_specs=vmem,
        scratch_shapes=[
            pltpu.VMEM((part, nocc), BF16),
            pltpu.VMEM((META, LANES), jnp.float32),
            pltpu.VMEM((1, slots), jnp.int32),
            pltpu.VMEM((1, counts.shape[0]), jnp.int32),
            pltpu.SemaphoreType.DMA((3,)),
        ],
        compiler_params=pltpu.CompilerParams(vmem_limit_bytes=60 * 2**20),
        cost_estimate=cost(0, 4 * part * nocc),
    )(pair_codes[None], counts[None], coeff)

    ahead = cost(4 * 10**10, nbf * nocc * 4)
    quarter = sds((top + META, LANES), BF16)
    stack = pl.pallas_call(
        stack_kernel,
        out_shape=sds((2, top + META, LANES), BF16),
        in_specs=[vmem, vmem],
        out_specs=vmem,
        compiler_params=params,
        cost_estimate=ahead,
    )
    hold = pl.pallas_call(
        copy_kernel,
        out_shape=quarter,
        in_specs=[vmem],
        out_specs=vmem,
        compiler_params=params,
        cost_estimate=ahead,
    )
    f32 = jnp.float32
    c1 = swap(packed, "blk", 1)
    c3 = middle(packed)
    onward = hold(c1)
    c2 = middle(onward)
    early = stack(c1, c3)
    early2 = swap(early, "aux", 2)
    later = after(ints, onward)
    i1 = inward(later)
    i3 = middle(later)
    i2 = middle(i1)
    late = hold(c2)
    late2 = swap(late, "aux", 2)
    early13 = swap(jnp.concatenate([early, early2]), "aux", 1)
    notes = jnp.stack([c[top::8, :slots] for c in (c1, late, c3)]).astype(jnp.int32)
    dense = pl.pallas_call(
        place_kernel,
        out_shape=sds((nbf, 2 * rows), BF16),
        in_specs=[smem] * 3 + [vmem] * 2,
        out_specs=vmem,
        compiler_params=params,
    )(pair_codes, counts, notes, ints, i1)
    late13 = swap(after(jnp.stack([late, late2]), dense), "aux", 1)
    dense3, full, left, overlap = pl.pallas_call(
        first_kernel,
        out_shape=(
            sds((nbf, rows), BF16),
            sds((nbf, nocc), BF16),
            sds((2 * rows, nbf), f32),
            sds((rows, nbf), BF16),
        ),
        in_specs=[smem] + [vmem] * 9,
        out_specs=(vmem,) * 4,
        compiler_params=params,
    )(notes, dense, i3, coeff, early, late, early2, late2, early13, late13)
    pieces = (sds((part, nocc), f32),) + (sds((part, nocc), BF16),) * 3
    estimate = cost(2 * rows * nbf * (rows + nbf + nocc), nbf * nocc * 8)
    *end_rows, dense2 = pl.pallas_call(
        end_kernel,
        out_shape=pieces + (sds((nbf, rows), BF16),),
        in_specs=[smem] + [vmem] * 6,
        out_specs=(vmem,) * 5,
        scratch_shapes=[pltpu.VMEM((rows, nocc), f32)],
        compiler_params=params,
        cost_estimate=estimate,
    )(notes, i2, dense, dense3, full, left, overlap)
    own_rows = pl.pallas_call(
        own_kernel,
        out_shape=pieces,
        in_specs=[vmem] * 6,
        out_specs=(vmem,) * 4,
        scratch_shapes=[pltpu.VMEM((rows, nocc), f32)],
        compiler_params=params,
        cost_estimate=estimate,
    )(dense, dense3, dense2, full, left, overlap)

    def summed(mine, p1, p2, p3):
        got = [swap(p, "aux", k) for k, p in ((2, p2), (3, p3), (1, p1))]
        return mine + got[0].astype(f32) + got[1].astype(f32) + got[2].astype(f32)

    ends = summed(*end_rows).astype(BF16)
    back = swap(ends, "blk", 1)
    mine, p1, p2, p3 = own_rows
    owns = summed(mine, p1, p2, p3)
    z = lax.axis_index("blk")
    return jnp.where((z == 0) | (z == 3), back.astype(f32), owns)


def local(integrals, pair_codes, counts, coeff):
    if lax.axis_size("blk") == 4 and lax.axis_size("aux") == 4:
        return local_line(integrals, pair_codes, counts, coeff)
    return local_long(integrals, pair_codes, counts, coeff)


def solution(mesh):
    in_specs = (
        P(("grp", "blk"), "aux", None, None),
        P(("grp", "blk")),
        P(("grp", "blk")),
        P(("grp", "blk"), None),
    )
    out_specs = P(("grp", "blk", "aux"), None)
    return jax.shard_map(local, mesh=mesh, in_specs=in_specs, out_specs=out_specs, check_vma=False)
```

```python
import functools

import jax
import jax.numpy as jnp
from jax import lax
from jax.experimental import pallas as pl
from jax.experimental.pallas import tpu as pltpu
from jax.sharding import PartitionSpec as P

BF16 = jnp.bfloat16
META = 16


def transform_slots(ints, columns, blocks):
    slots, paux, width, _ = ints.shape
    nocc = blocks.shape[2]

    def one_group(inputs):
        group_ints, group_cols = inputs
        chosen = blocks[group_cols]
        return jnp.einsum(
            "spml,sli->spmi", group_ints, chosen, preferred_element_type=jnp.float32
        ).astype(BF16)

    grouped = lax.map(
        one_group, (ints.reshape(slots // 8, 8, paux, width, width), columns.reshape(slots // 8, 8))
    )
    return grouped.reshape(slots, paux, width, nocc)


def local_long(integrals, pair_codes, counts, coeff):
    slots, paux, width, _ = integrals.shape
    nocc = coeff.shape[1]
    nblk = lax.axis_size("blk")
    per_dev = coeff.shape[0] // width
    cap = slots // nblk
    alive = (jnp.arange(cap)[None, :] < counts[:, None]).reshape(slots)
    masked = integrals * alive.astype(BF16)[:, None, None, None]
    local_blocks = coeff.reshape(per_dev, width, nocc)
    half = transform_slots(masked, pair_codes % per_dev, local_blocks)
    half_in, rows_in = (
        lax.all_to_all(half, "blk", split_axis=0, concat_axis=0, tiled=True),
        lax.all_to_all(pair_codes // per_dev, "blk", split_axis=0, concat_axis=0, tiled=True),
    )
    selector = (rows_in[:, None] == jnp.arange(per_dev, dtype=jnp.int32)[None, :]).astype(BF16)
    fitted = jnp.einsum("sk,spmi->pkmi", selector, half_in, preferred_element_type=jnp.float32)
    fitted = fitted.astype(BF16).reshape(paux, per_dev * width, nocc)
    partial_value = jnp.einsum(
        "nj,pni->pji", coeff, fitted, preferred_element_type=jnp.float32
    ).astype(BF16)
    occupied = lax.psum(partial_value.astype(jnp.float32).astype(BF16), "blk")
    return lax.psum_scatter(
        jnp.einsum("pnj,pji->ni", fitted, occupied, preferred_element_type=jnp.float32).astype(BF16),
        "aux",
        scatter_dimension=0,
        tiled=True,
    ).astype(jnp.float32)


LANES = 128


def after(x, *others):
    return lax.optimization_barrier((x, *others))[0]


def swap(x, axis, k):
    return lax.ppermute(x, axis, [(i, i ^ k) for i in range(4)])


def gray(k):
    return k ^ (k >> 1)


def middle(x):
    return lax.ppermute(x, "blk", [(1, 2), (2, 1)])


def pack_kernel(codes, counts, coeff, out, quarter, note, code, count, sems):
    part, nocc = quarter.shape
    a = lax.axis_index("aux")
    copies = (
        pltpu.make_async_copy(
            coeff.at[pl.ds(pl.multiple_of(a * part, part), part)], quarter, sems.at[0]
        ),
        pltpu.make_async_copy(codes, code, sems.at[1]),
        pltpu.make_async_copy(counts, count, sems.at[2]),
    )
    for copy in copies:
        copy.start()
    note[...] = jnp.zeros_like(note)
    for copy in copies:
        copy.wait()
    note[0:1, : code.shape[1]] = code[...].astype(jnp.float32)
    note[8:9, : count.shape[1]] = count[...].astype(jnp.float32)
    top = nocc // LANES * part
    out[top : top + META, :] = note[...].astype(BF16)
    for c in range(nocc // LANES):
        out[c * part : (c + 1) * part, :] = quarter[:, c * LANES : (c + 1) * LANES]


def stack_kernel(x, y, both):
    both[0] = x[...]
    both[1] = y[...]


def copy_kernel(x, y):
    y[...] = x[...]


def gather_quarters(coeff, at_k, refs):
    a = lax.axis_index("aux")
    part = (refs[0].shape[0] - META) * LANES // coeff.shape[1]
    for j, ref in enumerate(refs):
        at = pl.ds(pl.multiple_of(at_k * 4 * part + (a ^ j) * part, part), part)
        for c in range(coeff.shape[1] // LANES):
            coeff[at, c * LANES : (c + 1) * LANES] = ref[c * part : (c + 1) * part, :]


def place(dense, ref, codes, counts, k, left, rows):
    z = lax.axis_index("blk")
    slots, width, _ = ref.shape
    cap = slots // 4
    for s in range(slots):
        target = s // cap
        code = codes[s]

        @pl.when(s % cap < counts[target])
        def _():
            row = gray(target ^ z) * rows + code // 2 * width
            col = left + code % 2 * width
            dense[
                pl.ds(pl.multiple_of(row, width), width),
                pl.ds(pl.multiple_of(col, width), width),
            ] = ref[s]


def noted(notes, k):
    return notes.at[k - 1, 0], notes.at[k - 1, 1]


def dot(x, y):
    return jnp.dot(x, y, preferred_element_type=jnp.float32)


def dot_t(x, y):
    return lax.dot_general(x, y, (((1,), (1,)), ((), ())), preferred_element_type=jnp.float32)


def place_kernel(codes, counts, notes, i0, i1, dense):
    rows = dense.shape[1] // 2
    dense[...] = jnp.zeros_like(dense)
    place(dense, i0, codes, counts, 0, 0, rows)
    place(dense, i1, *noted(notes, 1), 1, rows, rows)


def first_kernel(notes, dense, i3, own, *refs):
    early, late, early2, late2, early13, late13, dense3, coeff, left, overlap = refs
    rows = own.shape[0]
    dense3[...] = jnp.zeros_like(dense3)
    place(dense3, i3, *noted(notes, 3), 3, 0, rows)
    coeff[:rows, :] = own[...]
    for i, k in enumerate((1, 3)):
        gather_quarters(coeff, gray(k), (early.at[i], early13.at[i], early2.at[i], early13.at[2 + i]))
    gather_quarters(coeff, gray(2), (late, late13.at[0], late2, late13.at[1]))
    two = 2 * rows
    fitted = dot(dense[:two, :], coeff[:two, :]) + dot(dense3[:two, :], coeff[two : 3 * rows, :])
    left[...] = dot_t(fitted.astype(BF16), coeff[...])
    overlap[...] = dot_t(coeff[3 * rows :, :], coeff[...]).astype(BF16)


def chain(left, dense, dense3, dense2, coeff):
    at, total = 0, None
    for columns in (dense, dense3, dense2):
        width = columns.shape[1]
        term = dot(dot(left, columns[...]).astype(BF16), coeff[at : at + width, :])
        total = term if total is None else total + term
        at += width
    return total


def cut(total, mine, p1, p2, p3):
    a = lax.axis_index("aux")
    size = mine.shape[0]
    mine[...] = total[pl.ds(pl.multiple_of(a * size, size), size), :]
    for j, out in enumerate((p1, p2, p3), 1):
        out[...] = total[pl.ds(pl.multiple_of((a ^ j) * size, size), size), :].astype(BF16)


def cut_pair(total, kept, given):
    a = lax.axis_index("aux")
    part = total.shape[0] // 4
    for i in (0, 2):
        at = pl.ds(i // 2 * part, part)
        kept[at, :] = total[pl.ds(pl.multiple_of((a ^ i) * part, part), part), :]
        given[at, :] = total[pl.ds(pl.multiple_of((a ^ i ^ 1) * part, part), part), :].astype(BF16)


def end_kernel(notes, i2, dense, dense3, coeff, left, overlap, mine, p1, p2, p3, dense2, total):
    rows = total.shape[0]
    dense2[...] = jnp.zeros_like(dense2)
    place(dense2, i2, *noted(notes, 2), 2, 0, rows)
    whole = left[rows:, :] + dot(dense2[rows : 2 * rows, :], overlap[...])
    total[...] = chain(whole.astype(BF16), dense, dense3, dense2, coeff)
    cut(total, mine, p1, p2, p3)


def own_kernel(dense, dense3, dense2, coeff, left, overlap, kept, given, total):
    rows = total.shape[0]
    whole = left[:rows, :] + dot(dense2[:rows, :], overlap[...])
    total[...] = chain(whole.astype(BF16), dense, dense3, dense2, coeff)
    cut_pair(total, kept, given)


def local_line(integrals, pair_codes, counts, coeff):
    slots, _, width, _ = integrals.shape
    rows, nocc = coeff.shape
    part = rows // 4
    nbf = rows * 4
    sds = jax.ShapeDtypeStruct
    vmem = pl.BlockSpec(memory_space=pltpu.VMEM)
    smem = pl.BlockSpec(memory_space=pltpu.SMEM)
    params = pltpu.CompilerParams(vmem_limit_bytes=20 * 2**20)
    cost = lambda flops, size: pl.CostEstimate(
        flops=flops, bytes_accessed=size, transcendentals=0
    )

    ints = integrals.reshape(slots, width, width)
    top = nocc // LANES * part
    packed = pl.pallas_call(
        pack_kernel,
        out_shape=sds((top + META, LANES), BF16),
        in_specs=[pl.BlockSpec(memory_space=pl.ANY)] * 3,
        out_specs=vmem,
        scratch_shapes=[
            pltpu.VMEM((part, nocc), BF16),
            pltpu.VMEM((META, LANES), jnp.float32),
            pltpu.VMEM((1, slots), jnp.int32),
            pltpu.VMEM((1, counts.shape[0]), jnp.int32),
            pltpu.SemaphoreType.DMA((3,)),
        ],
        compiler_params=pltpu.CompilerParams(vmem_limit_bytes=60 * 2**20),
        cost_estimate=cost(0, 4 * part * nocc),
    )(pair_codes[None], counts[None], coeff)

    ahead = cost(4 * 10**10, nbf * nocc * 4)
    quarter = sds((top + META, LANES), BF16)
    stack = pl.pallas_call(
        stack_kernel,
        out_shape=sds((2, top + META, LANES), BF16),
        in_specs=[vmem, vmem],
        out_specs=vmem,
        compiler_params=params,
        cost_estimate=ahead,
    )
    hold = pl.pallas_call(
        copy_kernel,
        out_shape=quarter,
        in_specs=[vmem],
        out_specs=vmem,
        compiler_params=params,
        cost_estimate=ahead,
    )
    f32 = jnp.float32
    c1 = swap(packed, "blk", 1)
    c3 = middle(packed)
    i1 = swap(ints, "blk", 1)
    onward = hold(c1)
    c2 = middle(onward)
    early = stack(c1, c3)
    early2 = swap(early, "aux", 2)
    i3 = middle(after(ints, onward))
    i2 = middle(i1)
    late = hold(after(c2, i1))
    late2 = swap(late, "aux", 2)
    early13 = swap(jnp.concatenate([early, early2]), "aux", 1)
    notes = jnp.stack([c[top::8, :slots] for c in (c1, late, c3)]).astype(jnp.int32)
    dense = pl.pallas_call(
        place_kernel,
        out_shape=sds((nbf, 2 * rows), BF16),
        in_specs=[smem] * 3 + [vmem] * 2,
        out_specs=vmem,
        compiler_params=params,
    )(pair_codes, counts, notes, ints, i1)
    late13 = swap(after(jnp.stack([late, late2]), dense), "aux", 1)
    dense3, full, left, overlap = pl.pallas_call(
        first_kernel,
        out_shape=(
            sds((nbf, rows), BF16),
            sds((nbf, nocc), BF16),
            sds((2 * rows, nbf), f32),
            sds((rows, nbf), BF16),
        ),
        in_specs=[smem] + [vmem] * 9,
        out_specs=(vmem,) * 4,
        compiler_params=params,
    )(notes, dense, i3, coeff, early, late, early2, late2, early13, late13)
    pieces = (sds((part, nocc), f32),) + (sds((part, nocc), BF16),) * 3
    estimate = cost(2 * rows * nbf * (rows + nbf + nocc), nbf * nocc * 8)
    *end_rows, dense2 = pl.pallas_call(
        end_kernel,
        out_shape=pieces + (sds((nbf, rows), BF16),),
        in_specs=[smem] + [vmem] * 6,
        out_specs=(vmem,) * 5,
        scratch_shapes=[pltpu.VMEM((rows, nocc), f32)],
        compiler_params=params,
        cost_estimate=estimate,
    )(notes, i2, dense, dense3, full, left, overlap)
    kept, given = pl.pallas_call(
        own_kernel,
        out_shape=(sds((2 * part, nocc), f32), sds((2 * part, nocc), BF16)),
        in_specs=[vmem] * 6,
        out_specs=(vmem,) * 2,
        scratch_shapes=[pltpu.VMEM((rows, nocc), f32)],
        compiler_params=params,
        cost_estimate=estimate,
    )(dense, dense3, dense2, full, left, overlap)

    mine, p1, p2, p3 = end_rows
    got = [swap(p, "aux", k) for k, p in ((2, p2), (3, p3), (1, p1))]
    ends = mine + got[0].astype(f32) + got[1].astype(f32) + got[2].astype(f32)
    back = swap(ends.astype(BF16), "blk", 1)
    pair = kept + swap(given, "aux", 1).astype(f32)
    owns = pair[:part] + swap(pair[part:].astype(BF16), "aux", 2).astype(f32)
    z = lax.axis_index("blk")
    return jnp.where((z == 0) | (z == 3), back.astype(f32), owns)


def local(integrals, pair_codes, counts, coeff):
    if lax.axis_size("blk") == 4 and lax.axis_size("aux") == 4:
        return local_line(integrals, pair_codes, counts, coeff)
    return local_long(integrals, pair_codes, counts, coeff)


def solution(mesh):
    in_specs = (
        P(("grp", "blk"), "aux", None, None),
        P(("grp", "blk")),
        P(("grp", "blk")),
        P(("grp", "blk"), None),
    )
    out_specs = P(("grp", "blk", "aux"), None)
    return jax.shard_map(local, mesh=mesh, in_specs=in_specs, out_specs=out_specs, check_vma=False)
```

```python
import functools

import jax
import jax.numpy as jnp
from jax import lax
from jax.experimental import pallas as pl
from jax.experimental.pallas import tpu as pltpu
from jax.sharding import PartitionSpec as P

BF16 = jnp.bfloat16
META = 16


def transform_slots(ints, columns, blocks):
    slots, paux, width, _ = ints.shape
    nocc = blocks.shape[2]

    def one_group(inputs):
        group_ints, group_cols = inputs
        chosen = blocks[group_cols]
        return jnp.einsum(
            "spml,sli->spmi", group_ints, chosen, preferred_element_type=jnp.float32
        ).astype(BF16)

    grouped = lax.map(
        one_group, (ints.reshape(slots // 8, 8, paux, width, width), columns.reshape(slots // 8, 8))
    )
    return grouped.reshape(slots, paux, width, nocc)


def local_long(integrals, pair_codes, counts, coeff):
    slots, paux, width, _ = integrals.shape
    nocc = coeff.shape[1]
    nblk = lax.axis_size("blk")
    per_dev = coeff.shape[0] // width
    cap = slots // nblk
    alive = (jnp.arange(cap)[None, :] < counts[:, None]).reshape(slots)
    masked = integrals * alive.astype(BF16)[:, None, None, None]
    local_blocks = coeff.reshape(per_dev, width, nocc)
    half = transform_slots(masked, pair_codes % per_dev, local_blocks)
    half_in, rows_in = (
        lax.all_to_all(half, "blk", split_axis=0, concat_axis=0, tiled=True),
        lax.all_to_all(pair_codes // per_dev, "blk", split_axis=0, concat_axis=0, tiled=True),
    )
    selector = (rows_in[:, None] == jnp.arange(per_dev, dtype=jnp.int32)[None, :]).astype(BF16)
    fitted = jnp.einsum("sk,spmi->pkmi", selector, half_in, preferred_element_type=jnp.float32)
    fitted = fitted.astype(BF16).reshape(paux, per_dev * width, nocc)
    partial_value = jnp.einsum(
        "nj,pni->pji", coeff, fitted, preferred_element_type=jnp.float32
    ).astype(BF16)
    occupied = lax.psum(partial_value.astype(jnp.float32).astype(BF16), "blk")
    return lax.psum_scatter(
        jnp.einsum("pnj,pji->ni", fitted, occupied, preferred_element_type=jnp.float32).astype(BF16),
        "aux",
        scatter_dimension=0,
        tiled=True,
    ).astype(jnp.float32)


LANES = 128


def after(x, *others):
    return lax.optimization_barrier((x, *others))[0]


def swap(x, axis, k):
    return lax.ppermute(x, axis, [(i, i ^ k) for i in range(4)])


def gray(k):
    return k ^ (k >> 1)


def middle(x):
    return lax.ppermute(x, "blk", [(1, 2), (2, 1)])


def pack_kernel(codes, counts, coeff, out, quarter, note, code, count, sems):
    part, nocc = quarter.shape
    a = lax.axis_index("aux")
    copies = (
        pltpu.make_async_copy(
            coeff.at[pl.ds(pl.multiple_of(a * part, part), part)], quarter, sems.at[0]
        ),
        pltpu.make_async_copy(codes, code, sems.at[1]),
        pltpu.make_async_copy(counts, count, sems.at[2]),
    )
    for copy in copies:
        copy.start()
    note[...] = jnp.zeros_like(note)
    for copy in copies:
        copy.wait()
    note[0:1, : code.shape[1]] = code[...].astype(jnp.float32)
    note[8:9, : count.shape[1]] = count[...].astype(jnp.float32)
    top = nocc // LANES * part
    out[top : top + META, :] = note[...].astype(BF16)
    for c in range(nocc // LANES):
        out[c * part : (c + 1) * part, :] = quarter[:, c * LANES : (c + 1) * LANES]


def stack_kernel(x, y, both):
    both[0] = x[...]
    both[1] = y[...]


def copy_kernel(x, y):
    y[...] = x[...]


def gather_quarters(coeff, at_k, refs):
    a = lax.axis_index("aux")
    part = (refs[0].shape[0] - META) * LANES // coeff.shape[1]
    for j, ref in enumerate(refs):
        at = pl.ds(pl.multiple_of(at_k * 4 * part + (a ^ j) * part, part), part)
        for c in range(coeff.shape[1] // LANES):
            coeff[at, c * LANES : (c + 1) * LANES] = ref[c * part : (c + 1) * part, :]


def place(dense, ref, codes, counts, k, left, rows):
    z = lax.axis_index("blk")
    slots, width, _ = ref.shape
    cap = slots // 4
    for s in range(slots):
        target = s // cap
        code = codes[s]

        @pl.when(s % cap < counts[target])
        def _():
            row = gray(target ^ z) * rows + code // 2 * width
            col = left + code % 2 * width
            dense[
                pl.ds(pl.multiple_of(row, width), width),
                pl.ds(pl.multiple_of(col, width), width),
            ] = ref[s]


def noted(notes, k):
    return notes.at[k - 1, 0], notes.at[k - 1, 1]


def dot(x, y):
    return jnp.dot(x, y, preferred_element_type=jnp.float32)


def dot_t(x, y):
    return lax.dot_general(x, y, (((1,), (1,)), ((), ())), preferred_element_type=jnp.float32)


def place_kernel(codes, counts, notes, i0, i1, dense):
    rows = dense.shape[1] // 2
    dense[...] = jnp.zeros_like(dense)
    place(dense, i0, codes, counts, 0, 0, rows)
    place(dense, i1, *noted(notes, 1), 1, rows, rows)


def first_kernel(notes, dense, i3, own, *refs):
    early, late, early2, late2, early13, late13, dense3, coeff, left, overlap = refs
    rows = own.shape[0]
    dense3[...] = jnp.zeros_like(dense3)
    place(dense3, i3, *noted(notes, 3), 3, 0, rows)
    coeff[:rows, :] = own[...]
    for i, k in enumerate((1, 3)):
        gather_quarters(coeff, gray(k), (early.at[i], early13.at[i], early2.at[i], early13.at[2 + i]))
    gather_quarters(coeff, gray(2), (late, late13.at[0], late2, late13.at[1]))
    two = 2 * rows
    fitted = dot(dense[:two, :], coeff[:two, :]) + dot(dense3[:two, :], coeff[two : 3 * rows, :])
    left[...] = dot_t(fitted.astype(BF16), coeff[...])
    overlap[...] = dot_t(coeff[3 * rows :, :], coeff[...]).astype(BF16)


def chain(left, dense, dense3, dense2, coeff):
    at, total = 0, None
    for columns in (dense, dense3, dense2):
        width = columns.shape[1]
        term = dot(dot(left, columns[...]).astype(BF16), coeff[at : at + width, :])
        total = term if total is None else total + term
        at += width
    return total


def cut(total, mine, p1, p2, p3):
    a = lax.axis_index("aux")
    size = mine.shape[0]
    mine[...] = total[pl.ds(pl.multiple_of(a * size, size), size), :]
    for j, out in enumerate((p1, p2, p3), 1):
        out[...] = total[pl.ds(pl.multiple_of((a ^ j) * size, size), size), :].astype(BF16)


def cut_pair(total, kept, given):
    a = lax.axis_index("aux")
    part = total.shape[0] // 4
    for i in (0, 2):
        at = pl.ds(i // 2 * part, part)
        kept[at, :] = total[pl.ds(pl.multiple_of((a ^ i) * part, part), part), :]
        given[at, :] = total[pl.ds(pl.multiple_of((a ^ i ^ 1) * part, part), part), :].astype(BF16)


def end_kernel(notes, i2, dense, dense3, coeff, left, overlap, mine, p1, p2, p3, dense2, total):
    rows = total.shape[0]
    dense2[...] = jnp.zeros_like(dense2)
    place(dense2, i2, *noted(notes, 2), 2, 0, rows)
    whole = left[rows:, :] + dot(dense2[rows : 2 * rows, :], overlap[...])
    total[...] = chain(whole.astype(BF16), dense, dense3, dense2, coeff)
    cut(total, mine, p1, p2, p3)


def own_kernel(dense, dense3, dense2, coeff, left, overlap, kept, given, total):
    rows = total.shape[0]
    whole = left[:rows, :] + dot(dense2[:rows, :], overlap[...])
    total[...] = chain(whole.astype(BF16), dense, dense3, dense2, coeff)
    cut_pair(total, kept, given)


def local_line(integrals, pair_codes, counts, coeff):
    slots, _, width, _ = integrals.shape
    rows, nocc = coeff.shape
    part = rows // 4
    nbf = rows * 4
    sds = jax.ShapeDtypeStruct
    vmem = pl.BlockSpec(memory_space=pltpu.VMEM)
    smem = pl.BlockSpec(memory_space=pltpu.SMEM)
    params = pltpu.CompilerParams(vmem_limit_bytes=20 * 2**20)
    cost = lambda flops, size: pl.CostEstimate(
        flops=flops, bytes_accessed=size, transcendentals=0
    )

    ints = integrals.reshape(slots, width, width)
    top = nocc // LANES * part
    packed = pl.pallas_call(
        pack_kernel,
        out_shape=sds((top + META, LANES), BF16),
        in_specs=[pl.BlockSpec(memory_space=pl.ANY)] * 3,
        out_specs=vmem,
        scratch_shapes=[
            pltpu.VMEM((part, nocc), BF16),
            pltpu.VMEM((META, LANES), jnp.float32),
            pltpu.VMEM((1, slots), jnp.int32),
            pltpu.VMEM((1, counts.shape[0]), jnp.int32),
            pltpu.SemaphoreType.DMA((3,)),
        ],
        compiler_params=pltpu.CompilerParams(vmem_limit_bytes=60 * 2**20),
        cost_estimate=cost(0, 4 * part * nocc),
    )(pair_codes[None], counts[None], coeff)

    ahead = cost(4 * 10**10, nbf * nocc * 4)
    quarter = sds((top + META, LANES), BF16)
    stack = pl.pallas_call(
        stack_kernel,
        out_shape=sds((2, top + META, LANES), BF16),
        in_specs=[vmem, vmem],
        out_specs=vmem,
        compiler_params=params,
        cost_estimate=ahead,
    )
    hold = pl.pallas_call(
        copy_kernel,
        out_shape=quarter,
        in_specs=[vmem],
        out_specs=vmem,
        compiler_params=params,
        cost_estimate=ahead,
    )
    f32 = jnp.float32
    c1 = swap(packed, "blk", 1)
    c3 = middle(packed)
    i1 = swap(ints, "blk", 1)
    onward = hold(c1)
    c2 = middle(onward)
    early = stack(c1, c3)
    early2 = swap(early, "aux", 2)
    i3 = middle(after(ints, onward))
    i2 = middle(i1)
    late = hold(after(c2, i1))
    late2 = swap(late, "aux", 2)
    early13 = swap(jnp.concatenate([early, early2]), "aux", 1)
    notes = jnp.stack([c[top::8, :slots] for c in (c1, late, c3)]).astype(jnp.int32)
    dense = pl.pallas_call(
        place_kernel,
        out_shape=sds((nbf, 2 * rows), BF16),
        in_specs=[smem] * 3 + [vmem] * 2,
        out_specs=vmem,
        compiler_params=params,
    )(pair_codes, counts, notes, ints, i1)
    late13 = swap(after(jnp.stack([late, late2]), dense), "aux", 1)
    dense3, full, left, overlap = pl.pallas_call(
        first_kernel,
        out_shape=(
            sds((nbf, rows), BF16),
            sds((nbf, nocc), BF16),
            sds((2 * rows, nbf), f32),
            sds((rows, nbf), BF16),
        ),
        in_specs=[smem] + [vmem] * 9,
        out_specs=(vmem,) * 4,
        compiler_params=params,
    )(notes, dense, i3, coeff, early, late, early2, late2, early13, late13)
    pieces = (sds((part, nocc), f32),) + (sds((part, nocc), BF16),) * 3
    estimate = cost(2 * rows * nbf * (rows + nbf + nocc), nbf * nocc * 8)
    *end_rows, dense2 = pl.pallas_call(
        end_kernel,
        out_shape=pieces + (sds((nbf, rows), BF16),),
        in_specs=[smem] + [vmem] * 6,
        out_specs=(vmem,) * 5,
        scratch_shapes=[pltpu.VMEM((rows, nocc), f32)],
        compiler_params=params,
        cost_estimate=estimate,
    )(notes, i2, dense, dense3, full, left, overlap)
    kept, given = pl.pallas_call(
        own_kernel,
        out_shape=(sds((2 * part, nocc), f32), sds((2 * part, nocc), BF16)),
        in_specs=[vmem] * 6,
        out_specs=(vmem,) * 2,
        scratch_shapes=[pltpu.VMEM((rows, nocc), f32)],
        compiler_params=params,
        cost_estimate=estimate,
    )(dense, dense3, dense2, full, left, overlap)

    mine, p1, p2, p3 = end_rows
    got = [swap(p, "aux", k) for k, p in ((1, p1), (2, p2), (3, p3))]
    ends = mine + got[0].astype(f32) + got[1].astype(f32) + got[2].astype(f32)
    back = swap(ends.astype(BF16), "blk", 1)
    across = [(4 * z + a, 4 * z + (a ^ 2)) for z in (1, 2) for a in range(4)]
    pair = kept + swap(given, "aux", 1).astype(f32)
    owns = pair[:part] + lax.ppermute(pair[part:].astype(BF16), ("blk", "aux"), across).astype(f32)
    z = lax.axis_index("blk")
    return jnp.where((z == 0) | (z == 3), back.astype(f32), owns)


def local(integrals, pair_codes, counts, coeff):
    if lax.axis_size("blk") == 4 and lax.axis_size("aux") == 4:
        return local_line(integrals, pair_codes, counts, coeff)
    return local_long(integrals, pair_codes, counts, coeff)


def solution(mesh):
    in_specs = (
        P(("grp", "blk"), "aux", None, None),
        P(("grp", "blk")),
        P(("grp", "blk")),
        P(("grp", "blk"), None),
    )
    out_specs = P(("grp", "blk", "aux"), None)
    return jax.shard_map(local, mesh=mesh, in_specs=in_specs, out_specs=out_specs, check_vma=False)
```

```python
import functools

import jax
import jax.numpy as jnp
from jax import lax
from jax.experimental import pallas as pl
from jax.experimental.pallas import tpu as pltpu
from jax.sharding import PartitionSpec as P

BF16 = jnp.bfloat16
META = 16


def transform_slots(ints, columns, blocks):
    slots, paux, width, _ = ints.shape
    nocc = blocks.shape[2]

    def one_group(inputs):
        group_ints, group_cols = inputs
        chosen = blocks[group_cols]
        return jnp.einsum(
            "spml,sli->spmi", group_ints, chosen, preferred_element_type=jnp.float32
        ).astype(BF16)

    grouped = lax.map(
        one_group, (ints.reshape(slots // 8, 8, paux, width, width), columns.reshape(slots // 8, 8))
    )
    return grouped.reshape(slots, paux, width, nocc)


def local_long(integrals, pair_codes, counts, coeff):
    slots, paux, width, _ = integrals.shape
    nocc = coeff.shape[1]
    nblk = lax.axis_size("blk")
    per_dev = coeff.shape[0] // width
    cap = slots // nblk
    alive = (jnp.arange(cap)[None, :] < counts[:, None]).reshape(slots)
    masked = integrals * alive.astype(BF16)[:, None, None, None]
    local_blocks = coeff.reshape(per_dev, width, nocc)
    half = transform_slots(masked, pair_codes % per_dev, local_blocks)
    half_in, rows_in = (
        lax.all_to_all(half, "blk", split_axis=0, concat_axis=0, tiled=True),
        lax.all_to_all(pair_codes // per_dev, "blk", split_axis=0, concat_axis=0, tiled=True),
    )
    selector = (rows_in[:, None] == jnp.arange(per_dev, dtype=jnp.int32)[None, :]).astype(BF16)
    fitted = jnp.einsum("sk,spmi->pkmi", selector, half_in, preferred_element_type=jnp.float32)
    fitted = fitted.astype(BF16).reshape(paux, per_dev * width, nocc)
    partial_value = jnp.einsum(
        "nj,pni->pji", coeff, fitted, preferred_element_type=jnp.float32
    ).astype(BF16)
    occupied = lax.psum(partial_value.astype(jnp.float32).astype(BF16), "blk")
    return lax.psum_scatter(
        jnp.einsum("pnj,pji->ni", fitted, occupied, preferred_element_type=jnp.float32).astype(BF16),
        "aux",
        scatter_dimension=0,
        tiled=True,
    ).astype(jnp.float32)


LANES = 128


def after(x, *others):
    return lax.optimization_barrier((x, *others))[0]


def swap(x, axis, k):
    return lax.ppermute(x, axis, [(i, i ^ k) for i in range(4)])


def gray(k):
    return k ^ (k >> 1)


def middle(x):
    return lax.ppermute(x, "blk", [(1, 2), (2, 1)])


def pack_kernel(codes, counts, coeff, out, quarter, note, code, count, sems):
    part, nocc = quarter.shape
    a = lax.axis_index("aux")
    copies = (
        pltpu.make_async_copy(
            coeff.at[pl.ds(pl.multiple_of(a * part, part), part)], quarter, sems.at[0]
        ),
        pltpu.make_async_copy(codes, code, sems.at[1]),
        pltpu.make_async_copy(counts, count, sems.at[2]),
    )
    for copy in copies:
        copy.start()
    note[...] = jnp.zeros_like(note)
    for copy in copies:
        copy.wait()
    note[0:1, : code.shape[1]] = code[...].astype(jnp.float32)
    note[8:9, : count.shape[1]] = count[...].astype(jnp.float32)
    top = nocc // LANES * part
    out[top : top + META, :] = note[...].astype(BF16)
    for c in range(nocc // LANES):
        out[c * part : (c + 1) * part, :] = quarter[:, c * LANES : (c + 1) * LANES]


def stack_kernel(x, y, both):
    both[0] = x[...]
    both[1] = y[...]


def copy_kernel(x, y):
    y[...] = x[...]


def gather_quarters(coeff, at_k, refs):
    a = lax.axis_index("aux")
    part = (refs[0].shape[0] - META) * LANES // coeff.shape[1]
    for j, ref in enumerate(refs):
        at = pl.ds(pl.multiple_of(at_k * 4 * part + (a ^ j) * part, part), part)
        for c in range(coeff.shape[1] // LANES):
            coeff[at, c * LANES : (c + 1) * LANES] = ref[c * part : (c + 1) * part, :]


def place(dense, ref, codes, counts, k, left, rows):
    z = lax.axis_index("blk")
    slots, width, _ = ref.shape
    cap = slots // 4
    for s in range(slots):
        target = s // cap
        code = codes[s]

        @pl.when(s % cap < counts[target])
        def _():
            row = gray(target ^ z) * rows + code // 2 * width
            col = left + code % 2 * width
            dense[
                pl.ds(pl.multiple_of(row, width), width),
                pl.ds(pl.multiple_of(col, width), width),
            ] = ref[s]


def noted(notes, k):
    return notes.at[k - 1, 0], notes.at[k - 1, 1]


def dot(x, y):
    return jnp.dot(x, y, preferred_element_type=jnp.float32)


def dot_t(x, y):
    return lax.dot_general(x, y, (((1,), (1,)), ((), ())), preferred_element_type=jnp.float32)


def place_kernel(codes, counts, notes, i0, i1, dense):
    rows = dense.shape[1] // 2
    dense[...] = jnp.zeros_like(dense)
    place(dense, i0, codes, counts, 0, 0, rows)
    place(dense, i1, *noted(notes, 1), 1, rows, rows)


def first_kernel(notes, dense, i3, own, *refs):
    early, late, early2, late2, early13, late13, dense3, coeff, left, overlap = refs
    rows = own.shape[0]
    dense3[...] = jnp.zeros_like(dense3)
    place(dense3, i3, *noted(notes, 3), 3, 0, rows)
    coeff[:rows, :] = own[...]
    for i, k in enumerate((1, 3)):
        gather_quarters(coeff, gray(k), (early.at[i], early13.at[i], early2.at[i], early13.at[2 + i]))
    gather_quarters(coeff, gray(2), (late, late13.at[0], late2, late13.at[1]))
    two = 2 * rows
    fitted = dot(dense[:two, :], coeff[:two, :]) + dot(dense3[:two, :], coeff[two : 3 * rows, :])
    left[...] = dot_t(fitted.astype(BF16), coeff[...])
    overlap[...] = dot_t(coeff[3 * rows :, :], coeff[...]).astype(BF16)


def chain(left, dense, dense3, dense2, coeff):
    at, total = 0, None
    for columns in (dense, dense3, dense2):
        width = columns.shape[1]
        term = dot(dot(left, columns[...]).astype(BF16), coeff[at : at + width, :])
        total = term if total is None else total + term
        at += width
    return total


def end_kernel(notes, i2, dense, dense3, coeff, left, overlap, total, dense2):
    rows = dense2.shape[1]
    dense2[...] = jnp.zeros_like(dense2)
    place(dense2, i2, *noted(notes, 2), 2, 0, rows)
    whole = left[rows:, :] + dot(dense2[rows : 2 * rows, :], overlap[...])
    total[...] = chain(whole.astype(BF16), dense, dense3, dense2, coeff).astype(BF16)


def own_kernel(dense, dense3, dense2, coeff, left, overlap, total):
    rows = dense2.shape[1]
    whole = left[:rows, :] + dot(dense2[:rows, :], overlap[...])
    total[...] = chain(whole.astype(BF16), dense, dense3, dense2, coeff).astype(BF16)


def local_line(integrals, pair_codes, counts, coeff):
    slots, _, width, _ = integrals.shape
    rows, nocc = coeff.shape
    part = rows // 4
    nbf = rows * 4
    sds = jax.ShapeDtypeStruct
    vmem = pl.BlockSpec(memory_space=pltpu.VMEM)
    smem = pl.BlockSpec(memory_space=pltpu.SMEM)
    params = pltpu.CompilerParams(vmem_limit_bytes=20 * 2**20)
    cost = lambda flops, size: pl.CostEstimate(
        flops=flops, bytes_accessed=size, transcendentals=0
    )

    ints = integrals.reshape(slots, width, width)
    top = nocc // LANES * part
    packed = pl.pallas_call(
        pack_kernel,
        out_shape=sds((top + META, LANES), BF16),
        in_specs=[pl.BlockSpec(memory_space=pl.ANY)] * 3,
        out_specs=vmem,
        scratch_shapes=[
            pltpu.VMEM((part, nocc), BF16),
            pltpu.VMEM((META, LANES), jnp.float32),
            pltpu.VMEM((1, slots), jnp.int32),
            pltpu.VMEM((1, counts.shape[0]), jnp.int32),
            pltpu.SemaphoreType.DMA((3,)),
        ],
        compiler_params=pltpu.CompilerParams(vmem_limit_bytes=60 * 2**20),
        cost_estimate=cost(0, 4 * part * nocc),
    )(pair_codes[None], counts[None], coeff)

    ahead = cost(4 * 10**10, nbf * nocc * 4)
    quarter = sds((top + META, LANES), BF16)
    stack = pl.pallas_call(
        stack_kernel,
        out_shape=sds((2, top + META, LANES), BF16),
        in_specs=[vmem, vmem],
        out_specs=vmem,
        compiler_params=params,
        cost_estimate=ahead,
    )
    hold = pl.pallas_call(
        copy_kernel,
        out_shape=quarter,
        in_specs=[vmem],
        out_specs=vmem,
        compiler_params=params,
        cost_estimate=ahead,
    )
    f32 = jnp.float32
    c1 = swap(packed, "blk", 1)
    c3 = middle(packed)
    i1 = swap(ints, "blk", 1)
    onward = hold(c1)
    c2 = middle(onward)
    early = stack(c1, c3)
    early2 = swap(early, "aux", 2)
    i3 = middle(after(ints, onward))
    i2 = middle(i1)
    late = hold(after(c2, i1))
    late2 = swap(late, "aux", 2)
    early13 = swap(jnp.concatenate([early, early2]), "aux", 1)
    notes = jnp.stack([c[top::8, :slots] for c in (c1, late, c3)]).astype(jnp.int32)
    dense = pl.pallas_call(
        place_kernel,
        out_shape=sds((nbf, 2 * rows), BF16),
        in_specs=[smem] * 3 + [vmem] * 2,
        out_specs=vmem,
        compiler_params=params,
    )(pair_codes, counts, notes, ints, i1)
    late13 = swap(after(jnp.stack([late, late2]), dense), "aux", 1)
    dense3, full, left, overlap = pl.pallas_call(
        first_kernel,
        out_shape=(
            sds((nbf, rows), BF16),
            sds((nbf, nocc), BF16),
            sds((2 * rows, nbf), f32),
            sds((rows, nbf), BF16),
        ),
        in_specs=[smem] + [vmem] * 9,
        out_specs=(vmem,) * 4,
        compiler_params=params,
    )(notes, dense, i3, coeff, early, late, early2, late2, early13, late13)
    whole = sds((rows, nocc), BF16)
    estimate = cost(2 * rows * nbf * (rows + nbf + nocc), nbf * nocc * 8)
    end_rows, dense2 = pl.pallas_call(
        end_kernel,
        out_shape=(whole, sds((nbf, rows), BF16)),
        in_specs=[smem] + [vmem] * 6,
        out_specs=(vmem,) * 2,
        compiler_params=params,
        cost_estimate=estimate,
    )(notes, i2, dense, dense3, full, left, overlap)
    own_rows = pl.pallas_call(
        own_kernel,
        out_shape=whole,
        in_specs=[vmem] * 6,
        out_specs=vmem,
        compiler_params=params,
        cost_estimate=estimate,
    )(dense, dense3, dense2, full, left, overlap)

    def summed(x):
        got = lax.all_to_all(x.reshape(4, part, nocc), "aux", 0, 0)
        return (got[0].astype(f32) + got[1].astype(f32)) + (got[2].astype(f32) + got[3].astype(f32))

    back = swap(summed(end_rows).astype(BF16), "blk", 1)
    owns = summed(own_rows)
    z = lax.axis_index("blk")
    return jnp.where((z == 0) | (z == 3), back.astype(f32), owns)


def local(integrals, pair_codes, counts, coeff):
    if lax.axis_size("blk") == 4 and lax.axis_size("aux") == 4:
        return local_line(integrals, pair_codes, counts, coeff)
    return local_long(integrals, pair_codes, counts, coeff)


def solution(mesh):
    in_specs = (
        P(("grp", "blk"), "aux", None, None),
        P(("grp", "blk")),
        P(("grp", "blk")),
        P(("grp", "blk"), None),
    )
    out_specs = P(("grp", "blk", "aux"), None)
    return jax.shard_map(local, mesh=mesh, in_specs=in_specs, out_specs=out_specs, check_vma=False)
```

```python
import functools

import jax
import jax.numpy as jnp
from jax import lax
from jax.experimental import pallas as pl
from jax.experimental.pallas import tpu as pltpu
from jax.sharding import PartitionSpec as P

BF16 = jnp.bfloat16
META = 16


def transform_slots(ints, columns, blocks):
    slots, paux, width, _ = ints.shape
    nocc = blocks.shape[2]

    def one_group(inputs):
        group_ints, group_cols = inputs
        chosen = blocks[group_cols]
        return jnp.einsum(
            "spml,sli->spmi", group_ints, chosen, preferred_element_type=jnp.float32
        ).astype(BF16)

    grouped = lax.map(
        one_group, (ints.reshape(slots // 8, 8, paux, width, width), columns.reshape(slots // 8, 8))
    )
    return grouped.reshape(slots, paux, width, nocc)


def local_long(integrals, pair_codes, counts, coeff):
    slots, paux, width, _ = integrals.shape
    nocc = coeff.shape[1]
    nblk = lax.axis_size("blk")
    per_dev = coeff.shape[0] // width
    cap = slots // nblk
    alive = (jnp.arange(cap)[None, :] < counts[:, None]).reshape(slots)
    masked = integrals * alive.astype(BF16)[:, None, None, None]
    local_blocks = coeff.reshape(per_dev, width, nocc)
    half = transform_slots(masked, pair_codes % per_dev, local_blocks)
    half_in, rows_in = (
        lax.all_to_all(half, "blk", split_axis=0, concat_axis=0, tiled=True),
        lax.all_to_all(pair_codes // per_dev, "blk", split_axis=0, concat_axis=0, tiled=True),
    )
    selector = (rows_in[:, None] == jnp.arange(per_dev, dtype=jnp.int32)[None, :]).astype(BF16)
    fitted = jnp.einsum("sk,spmi->pkmi", selector, half_in, preferred_element_type=jnp.float32)
    fitted = fitted.astype(BF16).reshape(paux, per_dev * width, nocc)
    partial_value = jnp.einsum(
        "nj,pni->pji", coeff, fitted, preferred_element_type=jnp.float32
    ).astype(BF16)
    occupied = lax.psum(partial_value.astype(jnp.float32).astype(BF16), "blk")
    return lax.psum_scatter(
        jnp.einsum("pnj,pji->ni", fitted, occupied, preferred_element_type=jnp.float32).astype(BF16),
        "aux",
        scatter_dimension=0,
        tiled=True,
    ).astype(jnp.float32)


LANES = 128


def after(x, *others):
    return lax.optimization_barrier((x, *others))[0]


def swap(x, axis, k):
    return lax.ppermute(x, axis, [(i, i ^ k) for i in range(4)])


def gray(k):
    return k ^ (k >> 1)


def middle(x):
    return lax.ppermute(x, "blk", [(1, 2), (2, 1)])


def pack_kernel(codes, counts, coeff, out, quarter, note, code, count, sems):
    part, nocc = quarter.shape
    a = lax.axis_index("aux")
    copies = (
        pltpu.make_async_copy(
            coeff.at[pl.ds(pl.multiple_of(a * part, part), part)], quarter, sems.at[0]
        ),
        pltpu.make_async_copy(codes, code, sems.at[1]),
        pltpu.make_async_copy(counts, count, sems.at[2]),
    )
    for copy in copies:
        copy.start()
    note[...] = jnp.zeros_like(note)
    for copy in copies:
        copy.wait()
    note[0:1, : code.shape[1]] = code[...].astype(jnp.float32)
    note[8:9, : count.shape[1]] = count[...].astype(jnp.float32)
    top = nocc // LANES * part
    out[top : top + META, :] = note[...].astype(BF16)
    for c in range(nocc // LANES):
        out[c * part : (c + 1) * part, :] = quarter[:, c * LANES : (c + 1) * LANES]


def stack_kernel(x, y, both):
    both[0] = x[...]
    both[1] = y[...]


def copy_kernel(x, y):
    y[...] = x[...]


def gather_quarters(coeff, at_k, refs):
    a = lax.axis_index("aux")
    part = (refs[0].shape[0] - META) * LANES // coeff.shape[1]
    for j, ref in enumerate(refs):
        at = pl.ds(pl.multiple_of(at_k * 4 * part + (a ^ j) * part, part), part)
        for c in range(coeff.shape[1] // LANES):
            coeff[at, c * LANES : (c + 1) * LANES] = ref[c * part : (c + 1) * part, :]


def place(dense, ref, codes, counts, k, left, rows):
    z = lax.axis_index("blk")
    slots, width, _ = ref.shape
    cap = slots // 4
    for s in range(slots):
        target = s // cap
        code = codes[s]

        @pl.when(s % cap < counts[target])
        def _():
            row = gray(target ^ z) * rows + code // 2 * width
            col = left + code % 2 * width
            dense[
                pl.ds(pl.multiple_of(row, width), width),
                pl.ds(pl.multiple_of(col, width), width),
            ] = ref[s]


def noted(notes, k):
    return notes.at[k - 1, 0], notes.at[k - 1, 1]


def dot(x, y):
    return jnp.dot(x, y, preferred_element_type=jnp.float32)


def dot_t(x, y):
    return lax.dot_general(x, y, (((1,), (1,)), ((), ())), preferred_element_type=jnp.float32)


def place_kernel(codes, counts, notes, i0, i1, dense):
    rows = dense.shape[1] // 2
    dense[...] = jnp.zeros_like(dense)
    place(dense, i0, codes, counts, 0, 0, rows)
    place(dense, i1, *noted(notes, 1), 1, rows, rows)


def first_kernel(notes, dense, i3, own, *refs):
    early, late, early2, late2, early13, late13, dense3, coeff, left, overlap = refs
    rows = own.shape[0]
    dense3[...] = jnp.zeros_like(dense3)
    place(dense3, i3, *noted(notes, 3), 3, 0, rows)
    coeff[:rows, :] = own[...]
    for i, k in enumerate((1, 3)):
        gather_quarters(coeff, gray(k), (early.at[i], early13.at[i], early2.at[i], early13.at[2 + i]))
    gather_quarters(coeff, gray(2), (late, late13.at[0], late2, late13.at[1]))
    two = 2 * rows
    fitted = dot(dense[:two, :], coeff[:two, :]) + dot(dense3[:two, :], coeff[two : 3 * rows, :])
    left[...] = dot_t(fitted.astype(BF16), coeff[...])
    overlap[...] = dot_t(coeff[3 * rows :, :], coeff[...]).astype(BF16)


def chain(left, dense, dense3, dense2, coeff, wide):
    at = 0
    for columns in (dense, dense3, dense2):
        width = columns.shape[1]
        wide[:, at : at + width] = dot(left, columns[...]).astype(BF16)
        at += width
    return dot(wide[...], coeff[...])


def cut(total, mine, p1, p2, p3):
    a = lax.axis_index("aux")
    size = mine.shape[0]
    mine[...] = total[pl.ds(pl.multiple_of(a * size, size), size), :]
    for j, out in enumerate((p1, p2, p3), 1):
        out[...] = total[pl.ds(pl.multiple_of((a ^ j) * size, size), size), :].astype(BF16)


def end_kernel(notes, i2, dense, dense3, coeff, left, overlap, mine, p1, p2, p3, dense2, total, wide):
    rows = total.shape[0]
    dense2[...] = jnp.zeros_like(dense2)
    place(dense2, i2, *noted(notes, 2), 2, 0, rows)
    whole = left[rows:, :] + dot(dense2[rows : 2 * rows, :], overlap[...])
    total[...] = chain(whole.astype(BF16), dense, dense3, dense2, coeff, wide)
    cut(total, mine, p1, p2, p3)


def own_kernel(dense, dense3, dense2, coeff, left, overlap, mine, p1, p2, p3, total, wide):
    rows = total.shape[0]
    whole = left[:rows, :] + dot(dense2[:rows, :], overlap[...])
    total[...] = chain(whole.astype(BF16), dense, dense3, dense2, coeff, wide)
    cut(total, mine, p1, p2, p3)


def local_line(integrals, pair_codes, counts, coeff):
    slots, _, width, _ = integrals.shape
    rows, nocc = coeff.shape
    part = rows // 4
    nbf = rows * 4
    sds = jax.ShapeDtypeStruct
    vmem = pl.BlockSpec(memory_space=pltpu.VMEM)
    smem = pl.BlockSpec(memory_space=pltpu.SMEM)
    params = pltpu.CompilerParams(vmem_limit_bytes=20 * 2**20)
    cost = lambda flops, size: pl.CostEstimate(
        flops=flops, bytes_accessed=size, transcendentals=0
    )

    ints = integrals.reshape(slots, width, width)
    top = nocc // LANES * part
    packed = pl.pallas_call(
        pack_kernel,
        out_shape=sds((top + META, LANES), BF16),
        in_specs=[pl.BlockSpec(memory_space=pl.ANY)] * 3,
        out_specs=vmem,
        scratch_shapes=[
            pltpu.VMEM((part, nocc), BF16),
            pltpu.VMEM((META, LANES), jnp.float32),
            pltpu.VMEM((1, slots), jnp.int32),
            pltpu.VMEM((1, counts.shape[0]), jnp.int32),
            pltpu.SemaphoreType.DMA((3,)),
        ],
        compiler_params=pltpu.CompilerParams(vmem_limit_bytes=60 * 2**20),
        cost_estimate=cost(0, 4 * part * nocc),
    )(pair_codes[None], counts[None], coeff)

    ahead = cost(4 * 10**10, nbf * nocc * 4)
    quarter = sds((top + META, LANES), BF16)
    stack = pl.pallas_call(
        stack_kernel,
        out_shape=sds((2, top + META, LANES), BF16),
        in_specs=[vmem, vmem],
        out_specs=vmem,
        compiler_params=params,
        cost_estimate=ahead,
    )
    hold = pl.pallas_call(
        copy_kernel,
        out_shape=quarter,
        in_specs=[vmem],
        out_specs=vmem,
        compiler_params=params,
        cost_estimate=ahead,
    )
    f32 = jnp.float32
    c1 = swap(packed, "blk", 1)
    c3 = middle(packed)
    i1 = swap(ints, "blk", 1)
    onward = hold(c1)
    c2 = middle(onward)
    early = stack(c1, c3)
    early2 = swap(early, "aux", 2)
    i3 = middle(after(ints, onward))
    i2 = middle(i1)
    late = hold(after(c2, i1))
    late2 = swap(late, "aux", 2)
    early13 = swap(jnp.concatenate([early, early2]), "aux", 1)
    notes = jnp.stack([c[top::8, :slots] for c in (c1, late, c3)]).astype(jnp.int32)
    dense = pl.pallas_call(
        place_kernel,
        out_shape=sds((nbf, 2 * rows), BF16),
        in_specs=[smem] * 3 + [vmem] * 2,
        out_specs=vmem,
        compiler_params=params,
    )(pair_codes, counts, notes, ints, i1)
    late13 = swap(after(jnp.stack([late, late2]), dense), "aux", 1)
    dense3, full, left, overlap = pl.pallas_call(
        first_kernel,
        out_shape=(
            sds((nbf, rows), BF16),
            sds((nbf, nocc), BF16),
            sds((2 * rows, nbf), f32),
            sds((rows, nbf), BF16),
        ),
        in_specs=[smem] + [vmem] * 9,
        out_specs=(vmem,) * 4,
        compiler_params=params,
    )(notes, dense, i3, coeff, early, late, early2, late2, early13, late13)
    pieces = (sds((part, nocc), f32),) + (sds((part, nocc), BF16),) * 3
    estimate = cost(2 * rows * nbf * (rows + nbf + nocc), nbf * nocc * 8)
    *end_rows, dense2 = pl.pallas_call(
        end_kernel,
        out_shape=pieces + (sds((nbf, rows), BF16),),
        in_specs=[smem] + [vmem] * 6,
        out_specs=(vmem,) * 5,
        scratch_shapes=[pltpu.VMEM((rows, nocc), f32), pltpu.VMEM((rows, nbf), BF16)],
        compiler_params=params,
        cost_estimate=estimate,
    )(notes, i2, dense, dense3, full, left, overlap)
    own_rows = pl.pallas_call(
        own_kernel,
        out_shape=pieces,
        in_specs=[vmem] * 6,
        out_specs=(vmem,) * 4,
        scratch_shapes=[pltpu.VMEM((rows, nocc), f32), pltpu.VMEM((rows, nbf), BF16)],
        compiler_params=params,
        cost_estimate=estimate,
    )(dense, dense3, dense2, full, left, overlap)

    def summed(mine, p1, p2, p3):
        got = [swap(p, "aux", k) for k, p in ((2, p2), (3, p3), (1, p1))]
        return mine + got[0].astype(f32) + got[1].astype(f32) + got[2].astype(f32)

    ends = summed(*end_rows).astype(BF16)
    back = swap(ends, "blk", 1)
    mine, p1, p2, p3 = own_rows
    owns = summed(mine, p1, p2, p3)
    z = lax.axis_index("blk")
    return jnp.where((z == 0) | (z == 3), back.astype(f32), owns)


def local(integrals, pair_codes, counts, coeff):
    if lax.axis_size("blk") == 4 and lax.axis_size("aux") == 4:
        return local_line(integrals, pair_codes, counts, coeff)
    return local_long(integrals, pair_codes, counts, coeff)


def solution(mesh):
    in_specs = (
        P(("grp", "blk"), "aux", None, None),
        P(("grp", "blk")),
        P(("grp", "blk")),
        P(("grp", "blk"), None),
    )
    out_specs = P(("grp", "blk", "aux"), None)
    return jax.shard_map(local, mesh=mesh, in_specs=in_specs, out_specs=out_specs, check_vma=False)
```

```python
import functools

import jax
import jax.numpy as jnp
from jax import lax
from jax.experimental import pallas as pl
from jax.experimental.pallas import tpu as pltpu
from jax.sharding import PartitionSpec as P

BF16 = jnp.bfloat16
META = 16


def transform_slots(ints, columns, blocks):
    slots, paux, width, _ = ints.shape
    nocc = blocks.shape[2]

    def one_group(inputs):
        group_ints, group_cols = inputs
        chosen = blocks[group_cols]
        return jnp.einsum(
            "spml,sli->spmi", group_ints, chosen, preferred_element_type=jnp.float32
        ).astype(BF16)

    grouped = lax.map(
        one_group, (ints.reshape(slots // 8, 8, paux, width, width), columns.reshape(slots // 8, 8))
    )
    return grouped.reshape(slots, paux, width, nocc)


def local_long(integrals, pair_codes, counts, coeff):
    slots, paux, width, _ = integrals.shape
    nocc = coeff.shape[1]
    nblk = lax.axis_size("blk")
    per_dev = coeff.shape[0] // width
    cap = slots // nblk
    alive = (jnp.arange(cap)[None, :] < counts[:, None]).reshape(slots)
    masked = integrals * alive.astype(BF16)[:, None, None, None]
    local_blocks = coeff.reshape(per_dev, width, nocc)
    half = transform_slots(masked, pair_codes % per_dev, local_blocks)
    half_in, rows_in = (
        lax.all_to_all(half, "blk", split_axis=0, concat_axis=0, tiled=True),
        lax.all_to_all(pair_codes // per_dev, "blk", split_axis=0, concat_axis=0, tiled=True),
    )
    selector = (rows_in[:, None] == jnp.arange(per_dev, dtype=jnp.int32)[None, :]).astype(BF16)
    fitted = jnp.einsum("sk,spmi->pkmi", selector, half_in, preferred_element_type=jnp.float32)
    fitted = fitted.astype(BF16).reshape(paux, per_dev * width, nocc)
    partial_value = jnp.einsum(
        "nj,pni->pji", coeff, fitted, preferred_element_type=jnp.float32
    ).astype(BF16)
    occupied = lax.psum(partial_value.astype(jnp.float32).astype(BF16), "blk")
    return lax.psum_scatter(
        jnp.einsum("pnj,pji->ni", fitted, occupied, preferred_element_type=jnp.float32).astype(BF16),
        "aux",
        scatter_dimension=0,
        tiled=True,
    ).astype(jnp.float32)


LANES = 128


def after(x, *others):
    return lax.optimization_barrier((x, *others))[0]


def swap(x, axis, k):
    return lax.ppermute(x, axis, [(i, i ^ k) for i in range(4)])


def gray(k):
    return k ^ (k >> 1)


def middle(x):
    return lax.ppermute(x, "blk", [(1, 2), (2, 1)])


def pack_kernel(codes, counts, coeff, out, quarter, note, code, count, sems):
    part, nocc = quarter.shape
    a = lax.axis_index("aux")
    copies = (
        pltpu.make_async_copy(
            coeff.at[pl.ds(pl.multiple_of(a * part, part), part)], quarter, sems.at[0]
        ),
        pltpu.make_async_copy(codes, code, sems.at[1]),
        pltpu.make_async_copy(counts, count, sems.at[2]),
    )
    for copy in copies:
        copy.start()
    note[...] = jnp.zeros_like(note)
    for copy in copies:
        copy.wait()
    note[0:1, : code.shape[1]] = code[...].astype(jnp.float32)
    note[8:9, : count.shape[1]] = count[...].astype(jnp.float32)
    top = nocc // LANES * part
    out[top : top + META, :] = note[...].astype(BF16)
    for c in range(nocc // LANES):
        out[c * part : (c + 1) * part, :] = quarter[:, c * LANES : (c + 1) * LANES]


def stack_kernel(x, y, both):
    both[0] = x[...]
    both[1] = y[...]


def copy_kernel(x, y):
    y[...] = x[...]


def gather_quarters(coeff, at_k, refs):
    a = lax.axis_index("aux")
    part = (refs[0].shape[0] - META) * LANES // coeff.shape[1]
    for j, ref in enumerate(refs):
        at = pl.ds(pl.multiple_of(at_k * 4 * part + (a ^ j) * part, part), part)
        for c in range(coeff.shape[1] // LANES):
            coeff[at, c * LANES : (c + 1) * LANES] = ref[c * part : (c + 1) * part, :]


def place(dense, ref, codes, counts, k, left, rows):
    z = lax.axis_index("blk")
    slots, width, _ = ref.shape
    cap = slots // 4
    for s in range(slots):
        target = s // cap
        code = codes[s]

        @pl.when(s % cap < counts[target])
        def _():
            row = gray(target ^ z) * rows + code // 2 * width
            col = left + code % 2 * width
            dense[
                pl.ds(pl.multiple_of(row, width), width),
                pl.ds(pl.multiple_of(col, width), width),
            ] = ref[s]


def noted(notes, k):
    return notes.at[k - 1, 0], notes.at[k - 1, 1]


def dot(x, y):
    return jnp.dot(x, y, preferred_element_type=jnp.float32)


def dot_t(x, y):
    return lax.dot_general(x, y, (((1,), (1,)), ((), ())), preferred_element_type=jnp.float32)


def place_kernel(codes, counts, notes, i0, i1, dense):
    rows = dense.shape[1] // 2
    dense[...] = jnp.zeros_like(dense)
    place(dense, i0, codes, counts, 0, 0, rows)
    place(dense, i1, *noted(notes, 1), 1, rows, rows)


def first_kernel(notes, dense, i3, own, *refs):
    early, late, early2, late2, early13, late13, dense3, coeff, left, overlap = refs
    rows = own.shape[0]
    dense3[...] = jnp.zeros_like(dense3)
    place(dense3, i3, *noted(notes, 3), 3, 0, rows)
    coeff[:rows, :] = own[...]
    for i, k in enumerate((1, 3)):
        gather_quarters(coeff, gray(k), (early.at[i], early13.at[i], early2.at[i], early13.at[2 + i]))
    gather_quarters(coeff, gray(2), (late, late13.at[0], late2, late13.at[1]))
    two = 2 * rows
    fitted = dot(dense[:two, :], coeff[:two, :]) + dot(dense3[:two, :], coeff[two : 3 * rows, :])
    left[...] = dot_t(fitted.astype(BF16), coeff[...])
    overlap[...] = dot_t(coeff[3 * rows :, :], coeff[...]).astype(BF16)


def chain(left, dense, dense3, dense2, coeff, wide):
    at = 0
    for columns in (dense, dense3, dense2):
        width = columns.shape[1]
        wide[:, at : at + width] = dot(left, columns[...]).astype(BF16)
        at += width
    return dot(wide[...], coeff[...])


def cut(total, mine, p1, p2, p3):
    a = lax.axis_index("aux")
    size = mine.shape[0]
    mine[...] = total[pl.ds(pl.multiple_of(a * size, size), size), :]
    for j, out in enumerate((p1, p2, p3), 1):
        out[...] = total[pl.ds(pl.multiple_of((a ^ j) * size, size), size), :].astype(BF16)


def end_kernel(notes, i2, dense, dense3, coeff, left, overlap, mine, p1, p2, p3, dense2, total, wide):
    rows = total.shape[0]
    dense2[...] = jnp.zeros_like(dense2)
    place(dense2, i2, *noted(notes, 2), 2, 0, rows)
    whole = left[rows:, :] + dot(dense2[rows : 2 * rows, :], overlap[...])
    total[...] = chain(whole.astype(BF16), dense, dense3, dense2, coeff, wide)
    cut(total, mine, p1, p2, p3)


def own_kernel(dense, dense3, dense2, coeff, left, overlap, mine, p1, p2, p3, total, wide):
    rows = total.shape[0]
    whole = left[:rows, :] + dot(dense2[:rows, :], overlap[...])
    total[...] = chain(whole.astype(BF16), dense, dense3, dense2, coeff, wide)
    cut(total, mine, p1, p2, p3)


def local_line(integrals, pair_codes, counts, coeff):
    slots, _, width, _ = integrals.shape
    rows, nocc = coeff.shape
    part = rows // 4
    nbf = rows * 4
    sds = jax.ShapeDtypeStruct
    vmem = pl.BlockSpec(memory_space=pltpu.VMEM)
    smem = pl.BlockSpec(memory_space=pltpu.SMEM)
    params = pltpu.CompilerParams(vmem_limit_bytes=20 * 2**20)
    cost = lambda flops, size: pl.CostEstimate(
        flops=flops, bytes_accessed=size, transcendentals=0
    )

    ints = integrals.reshape(slots, width, width)
    top = nocc // LANES * part
    packed = pl.pallas_call(
        pack_kernel,
        out_shape=sds((top + META, LANES), BF16),
        in_specs=[pl.BlockSpec(memory_space=pl.ANY)] * 3,
        out_specs=vmem,
        scratch_shapes=[
            pltpu.VMEM((part, nocc), BF16),
            pltpu.VMEM((META, LANES), jnp.float32),
            pltpu.VMEM((1, slots), jnp.int32),
            pltpu.VMEM((1, counts.shape[0]), jnp.int32),
            pltpu.SemaphoreType.DMA((3,)),
        ],
        compiler_params=pltpu.CompilerParams(vmem_limit_bytes=60 * 2**20),
        cost_estimate=cost(0, 4 * part * nocc),
    )(pair_codes[None], counts[None], coeff)

    ahead = cost(4 * 10**10, nbf * nocc * 4)
    quarter = sds((top + META, LANES), BF16)
    stack = pl.pallas_call(
        stack_kernel,
        out_shape=sds((2, top + META, LANES), BF16),
        in_specs=[vmem, vmem],
        out_specs=vmem,
        compiler_params=params,
        cost_estimate=ahead,
    )
    hold = pl.pallas_call(
        copy_kernel,
        out_shape=quarter,
        in_specs=[vmem],
        out_specs=vmem,
        compiler_params=params,
        cost_estimate=ahead,
    )
    f32 = jnp.float32
    c1 = swap(packed, "blk", 1)
    c3 = middle(packed)
    i1 = swap(ints, "blk", 1)
    onward = hold(c1)
    c2 = middle(onward)
    early = stack(c1, c3)
    early2 = swap(early, "aux", 2)
    i3 = middle(after(ints, onward))
    i2 = middle(i1)
    late = hold(after(c2, i1))
    late2 = swap(late, "aux", 2)
    early13 = swap(jnp.concatenate([early, early2]), "aux", 1)
    notes = jnp.stack([c[top::8, :slots] for c in (c1, late, c3)]).astype(jnp.int32)
    dense = pl.pallas_call(
        place_kernel,
        out_shape=sds((nbf, 2 * rows), BF16),
        in_specs=[smem] * 3 + [vmem] * 2,
        out_specs=vmem,
        compiler_params=params,
    )(pair_codes, counts, notes, ints, i1)
    late13 = swap(after(jnp.stack([late, late2]), dense), "aux", 1)
    dense3, full, left, overlap = pl.pallas_call(
        first_kernel,
        out_shape=(
            sds((nbf, rows), BF16),
            sds((nbf, nocc), BF16),
            sds((2 * rows, nbf), f32),
            sds((rows, nbf), BF16),
        ),
        in_specs=[smem] + [vmem] * 9,
        out_specs=(vmem,) * 4,
        compiler_params=params,
    )(notes, dense, i3, coeff, early, late, early2, late2, early13, late13)
    pieces = (sds((part, nocc), f32),) + (sds((part, nocc), BF16),) * 3
    estimate = cost(2 * rows * nbf * (rows + nbf + nocc), nbf * nocc * 8)
    *end_rows, dense2 = pl.pallas_call(
        end_kernel,
        out_shape=pieces + (sds((nbf, rows), BF16),),
        in_specs=[smem] + [vmem] * 6,
        out_specs=(vmem,) * 5,
        scratch_shapes=[pltpu.VMEM((rows, nocc), f32), pltpu.VMEM((rows, nbf), BF16)],
        compiler_params=params,
        cost_estimate=estimate,
    )(notes, i2, dense, dense3, full, left, overlap)
    own_rows = pl.pallas_call(
        own_kernel,
        out_shape=pieces,
        in_specs=[vmem] * 6,
        out_specs=(vmem,) * 4,
        scratch_shapes=[pltpu.VMEM((rows, nocc), f32), pltpu.VMEM((rows, nbf), BF16)],
        compiler_params=params,
        cost_estimate=estimate,
    )(dense, dense3, dense2, full, left, overlap)

    def summed(mine, p1, p2, p3):
        got = [swap(p, "aux", k) for k, p in ((2, p2), (3, p3), (1, p1))]
        return mine + got[0].astype(f32) + got[1].astype(f32) + got[2].astype(f32)

    ends = summed(*end_rows).astype(BF16)
    back = swap(ends, "blk", 1)
    mine, p1, p2, p3 = own_rows
    far = swap(p2, "aux", 2)
    owns = mine + far.astype(f32) + swap(p3, "aux", 3).astype(f32)
    owns = owns + swap(after(p1, far), "aux", 1).astype(f32)
    z = lax.axis_index("blk")
    return jnp.where((z == 0) | (z == 3), back.astype(f32), owns)


def local(integrals, pair_codes, counts, coeff):
    if lax.axis_size("blk") == 4 and lax.axis_size("aux") == 4:
        return local_line(integrals, pair_codes, counts, coeff)
    return local_long(integrals, pair_codes, counts, coeff)


def solution(mesh):
    in_specs = (
        P(("grp", "blk"), "aux", None, None),
        P(("grp", "blk")),
        P(("grp", "blk")),
        P(("grp", "blk"), None),
    )
    out_specs = P(("grp", "blk", "aux"), None)
    return jax.shard_map(local, mesh=mesh, in_specs=in_specs, out_specs=out_specs, check_vma=False)
```

```python
import functools

import jax
import jax.numpy as jnp
from jax import lax
from jax.experimental import pallas as pl
from jax.experimental.pallas import tpu as pltpu
from jax.sharding import PartitionSpec as P

BF16 = jnp.bfloat16
META = 16


def transform_slots(ints, columns, blocks):
    slots, paux, width, _ = ints.shape
    nocc = blocks.shape[2]

    def one_group(inputs):
        group_ints, group_cols = inputs
        chosen = blocks[group_cols]
        return jnp.einsum(
            "spml,sli->spmi", group_ints, chosen, preferred_element_type=jnp.float32
        ).astype(BF16)

    grouped = lax.map(
        one_group, (ints.reshape(slots // 8, 8, paux, width, width), columns.reshape(slots // 8, 8))
    )
    return grouped.reshape(slots, paux, width, nocc)


def local_long(integrals, pair_codes, counts, coeff):
    slots, paux, width, _ = integrals.shape
    nocc = coeff.shape[1]
    nblk = lax.axis_size("blk")
    per_dev = coeff.shape[0] // width
    cap = slots // nblk
    alive = (jnp.arange(cap)[None, :] < counts[:, None]).reshape(slots)
    masked = integrals * alive.astype(BF16)[:, None, None, None]
    local_blocks = coeff.reshape(per_dev, width, nocc)
    half = transform_slots(masked, pair_codes % per_dev, local_blocks)
    half_in, rows_in = (
        lax.all_to_all(half, "blk", split_axis=0, concat_axis=0, tiled=True),
        lax.all_to_all(pair_codes // per_dev, "blk", split_axis=0, concat_axis=0, tiled=True),
    )
    selector = (rows_in[:, None] == jnp.arange(per_dev, dtype=jnp.int32)[None, :]).astype(BF16)
    fitted = jnp.einsum("sk,spmi->pkmi", selector, half_in, preferred_element_type=jnp.float32)
    fitted = fitted.astype(BF16).reshape(paux, per_dev * width, nocc)
    partial_value = jnp.einsum(
        "nj,pni->pji", coeff, fitted, preferred_element_type=jnp.float32
    ).astype(BF16)
    occupied = lax.psum(partial_value.astype(jnp.float32).astype(BF16), "blk")
    return lax.psum_scatter(
        jnp.einsum("pnj,pji->ni", fitted, occupied, preferred_element_type=jnp.float32).astype(BF16),
        "aux",
        scatter_dimension=0,
        tiled=True,
    ).astype(jnp.float32)


LANES = 128


def after(x, *others):
    return lax.optimization_barrier((x, *others))[0]


def swap(x, axis, k):
    return lax.ppermute(x, axis, [(i, i ^ k) for i in range(4)])


def gray(k):
    return k ^ (k >> 1)


def middle(x):
    return lax.ppermute(x, "blk", [(1, 2), (2, 1)])


def pack_kernel(codes, counts, coeff, out, quarter, note, code, count, sems):
    part, nocc = quarter.shape
    a = lax.axis_index("aux")
    copies = (
        pltpu.make_async_copy(
            coeff.at[pl.ds(pl.multiple_of(a * part, part), part)], quarter, sems.at[0]
        ),
        pltpu.make_async_copy(codes, code, sems.at[1]),
        pltpu.make_async_copy(counts, count, sems.at[2]),
    )
    for copy in copies:
        copy.start()
    note[...] = jnp.zeros_like(note)
    for copy in copies:
        copy.wait()
    note[0:1, : code.shape[1]] = code[...].astype(jnp.float32)
    note[8:9, : count.shape[1]] = count[...].astype(jnp.float32)
    top = nocc // LANES * part
    out[top : top + META, :] = note[...].astype(BF16)
    for c in range(nocc // LANES):
        out[c * part : (c + 1) * part, :] = quarter[:, c * LANES : (c + 1) * LANES]


def stack_kernel(x, y, both):
    both[0] = x[...]
    both[1] = y[...]


def copy_kernel(x, y):
    y[...] = x[...]


def gather_quarters(coeff, at_k, refs):
    a = lax.axis_index("aux")
    part = (refs[0].shape[0] - META) * LANES // coeff.shape[1]
    for j, ref in enumerate(refs):
        at = pl.ds(pl.multiple_of(at_k * 4 * part + (a ^ j) * part, part), part)
        for c in range(coeff.shape[1] // LANES):
            coeff[at, c * LANES : (c + 1) * LANES] = ref[c * part : (c + 1) * part, :]


def place(dense, ref, codes, counts, k, left, rows):
    z = lax.axis_index("blk")
    slots, width, _ = ref.shape
    cap = slots // 4
    for s in range(slots):
        target = s // cap
        code = codes[s]

        @pl.when(s % cap < counts[target])
        def _():
            row = gray(target ^ z) * rows + code // 2 * width
            col = left + code % 2 * width
            dense[
                pl.ds(pl.multiple_of(row, width), width),
                pl.ds(pl.multiple_of(col, width), width),
            ] = ref[s]


def noted(notes, k):
    return notes.at[k - 1, 0], notes.at[k - 1, 1]


def dot(x, y):
    return jnp.dot(x, y, preferred_element_type=jnp.float32)


def dot_t(x, y):
    return lax.dot_general(x, y, (((1,), (1,)), ((), ())), preferred_element_type=jnp.float32)


def place_kernel(codes, counts, notes, i0, i1, dense):
    rows = dense.shape[1] // 2
    dense[...] = jnp.zeros_like(dense)
    place(dense, i0, codes, counts, 0, 0, rows)
    place(dense, i1, *noted(notes, 1), 1, rows, rows)


def first_kernel(notes, dense, i3, own, *refs):
    early, late, early2, late2, early13, late13, dense3, coeff, left, overlap = refs
    rows = own.shape[0]
    dense3[...] = jnp.zeros_like(dense3)
    place(dense3, i3, *noted(notes, 3), 3, 0, rows)
    coeff[:rows, :] = own[...]
    for i, k in enumerate((1, 3)):
        gather_quarters(coeff, gray(k), (early.at[i], early13.at[i], early2.at[i], early13.at[2 + i]))
    gather_quarters(coeff, gray(2), (late, late13.at[0], late2, late13.at[1]))
    two = 2 * rows
    fitted = dot(dense[:two, :], coeff[:two, :]) + dot(dense3[:two, :], coeff[two : 3 * rows, :])
    left[...] = dot_t(fitted.astype(BF16), coeff[...])
    overlap[...] = dot_t(coeff[3 * rows :, :], coeff[...]).astype(BF16)


def chain(left, dense, dense3, dense2, coeff, wide):
    at = 0
    for columns in (dense, dense3, dense2):
        width = columns.shape[1]
        wide[:, at : at + width] = dot(left, columns[...]).astype(BF16)
        at += width
    return dot(wide[...], coeff[...])


def by_aux(ref, first, rows):
    a = lax.axis_index("aux")
    size = rows // 4
    return jnp.concatenate(
        [ref[pl.ds(pl.multiple_of(first + (a ^ j) * size, size), size), :] for j in range(4)], 0
    )


def cut(total, mine, p1, p2, p3):
    size = mine.shape[0]
    mine[...] = total[:size, :]
    for j, out in enumerate((p1, p2, p3), 1):
        out[...] = total[j * size : (j + 1) * size, :].astype(BF16)


def end_kernel(notes, i2, dense, dense3, coeff, left, overlap, mine, p1, p2, p3, dense2, wide):
    rows = dense2.shape[1]
    dense2[...] = jnp.zeros_like(dense2)
    place(dense2, i2, *noted(notes, 2), 2, 0, rows)
    whole = by_aux(left, rows, rows) + dot(by_aux(dense2, rows, rows), overlap[...])
    total = chain(whole.astype(BF16), dense, dense3, dense2, coeff, wide)
    cut(total, mine, p1, p2, p3)


def own_kernel(dense, dense3, dense2, coeff, left, overlap, mine, p1, p2, p3, wide):
    rows = dense2.shape[1]
    whole = by_aux(left, 0, rows) + dot(by_aux(dense2, 0, rows), overlap[...])
    total = chain(whole.astype(BF16), dense, dense3, dense2, coeff, wide)
    cut(total, mine, p1, p2, p3)


def local_line(integrals, pair_codes, counts, coeff):
    slots, _, width, _ = integrals.shape
    rows, nocc = coeff.shape
    part = rows // 4
    nbf = rows * 4
    sds = jax.ShapeDtypeStruct
    vmem = pl.BlockSpec(memory_space=pltpu.VMEM)
    smem = pl.BlockSpec(memory_space=pltpu.SMEM)
    params = pltpu.CompilerParams(vmem_limit_bytes=20 * 2**20)
    cost = lambda flops, size: pl.CostEstimate(
        flops=flops, bytes_accessed=size, transcendentals=0
    )

    ints = integrals.reshape(slots, width, width)
    top = nocc // LANES * part
    packed = pl.pallas_call(
        pack_kernel,
        out_shape=sds((top + META, LANES), BF16),
        in_specs=[pl.BlockSpec(memory_space=pl.ANY)] * 3,
        out_specs=vmem,
        scratch_shapes=[
            pltpu.VMEM((part, nocc), BF16),
            pltpu.VMEM((META, LANES), jnp.float32),
            pltpu.VMEM((1, slots), jnp.int32),
            pltpu.VMEM((1, counts.shape[0]), jnp.int32),
            pltpu.SemaphoreType.DMA((3,)),
        ],
        compiler_params=pltpu.CompilerParams(vmem_limit_bytes=60 * 2**20),
        cost_estimate=cost(0, 4 * part * nocc),
    )(pair_codes[None], counts[None], coeff)

    ahead = cost(4 * 10**10, nbf * nocc * 4)
    quarter = sds((top + META, LANES), BF16)
    stack = pl.pallas_call(
        stack_kernel,
        out_shape=sds((2, top + META, LANES), BF16),
        in_specs=[vmem, vmem],
        out_specs=vmem,
        compiler_params=params,
        cost_estimate=ahead,
    )
    hold = pl.pallas_call(
        copy_kernel,
        out_shape=quarter,
        in_specs=[vmem],
        out_specs=vmem,
        compiler_params=params,
        cost_estimate=ahead,
    )
    f32 = jnp.float32
    c1 = swap(packed, "blk", 1)
    c3 = middle(packed)
    i1 = swap(ints, "blk", 1)
    onward = hold(c1)
    c2 = middle(onward)
    early = stack(c1, c3)
    early2 = swap(early, "aux", 2)
    i3 = middle(after(ints, onward))
    i2 = middle(i1)
    late = hold(after(c2, i1))
    late2 = swap(late, "aux", 2)
    early13 = swap(jnp.concatenate([early, early2]), "aux", 1)
    notes = jnp.stack([c[top::8, :slots] for c in (c1, late, c3)]).astype(jnp.int32)
    dense = pl.pallas_call(
        place_kernel,
        out_shape=sds((nbf, 2 * rows), BF16),
        in_specs=[smem] * 3 + [vmem] * 2,
        out_specs=vmem,
        compiler_params=params,
    )(pair_codes, counts, notes, ints, i1)
    late13 = swap(after(jnp.stack([late, late2]), dense), "aux", 1)
    dense3, full, left, overlap = pl.pallas_call(
        first_kernel,
        out_shape=(
            sds((nbf, rows), BF16),
            sds((nbf, nocc), BF16),
            sds((2 * rows, nbf), f32),
            sds((rows, nbf), BF16),
        ),
        in_specs=[smem] + [vmem] * 9,
        out_specs=(vmem,) * 4,
        compiler_params=params,
    )(notes, dense, i3, coeff, early, late, early2, late2, early13, late13)
    pieces = (sds((part, nocc), f32),) + (sds((part, nocc), BF16),) * 3
    estimate = cost(2 * rows * nbf * (rows + nbf + nocc), nbf * nocc * 8)
    *end_rows, dense2 = pl.pallas_call(
        end_kernel,
        out_shape=pieces + (sds((nbf, rows), BF16),),
        in_specs=[smem] + [vmem] * 6,
        out_specs=(vmem,) * 5,
        scratch_shapes=[pltpu.VMEM((rows, nbf), BF16)],
        compiler_params=params,
        cost_estimate=estimate,
    )(notes, i2, dense, dense3, full, left, overlap)
    own_rows = pl.pallas_call(
        own_kernel,
        out_shape=pieces,
        in_specs=[vmem] * 6,
        out_specs=(vmem,) * 4,
        scratch_shapes=[pltpu.VMEM((rows, nbf), BF16)],
        compiler_params=params,
        cost_estimate=estimate,
    )(dense, dense3, dense2, full, left, overlap)

    def summed(mine, p1, p2, p3):
        got = [swap(p, "aux", k) for k, p in ((2, p2), (3, p3), (1, p1))]
        return mine + got[0].astype(f32) + got[1].astype(f32) + got[2].astype(f32)

    ends = summed(*end_rows).astype(BF16)
    back = swap(ends, "blk", 1)
    mine, p1, p2, p3 = own_rows
    far = swap(p2, "aux", 2)
    owns = mine + far.astype(f32) + swap(p3, "aux", 3).astype(f32)
    owns = owns + swap(after(p1, far), "aux", 1).astype(f32)
    z = lax.axis_index("blk")
    return jnp.where((z == 0) | (z == 3), back.astype(f32), owns)


def local(integrals, pair_codes, counts, coeff):
    if lax.axis_size("blk") == 4 and lax.axis_size("aux") == 4:
        return local_line(integrals, pair_codes, counts, coeff)
    return local_long(integrals, pair_codes, counts, coeff)


def solution(mesh):
    in_specs = (
        P(("grp", "blk"), "aux", None, None),
        P(("grp", "blk")),
        P(("grp", "blk")),
        P(("grp", "blk"), None),
    )
    out_specs = P(("grp", "blk", "aux"), None)
    return jax.shard_map(local, mesh=mesh, in_specs=in_specs, out_specs=out_specs, check_vma=False)
```

```python
import functools

import jax
import jax.numpy as jnp
from jax import lax
from jax.experimental import pallas as pl
from jax.experimental.pallas import tpu as pltpu
from jax.sharding import PartitionSpec as P

BF16 = jnp.bfloat16
META = 16


def transform_slots(ints, columns, blocks):
    slots, paux, width, _ = ints.shape
    nocc = blocks.shape[2]

    def one_group(inputs):
        group_ints, group_cols = inputs
        chosen = blocks[group_cols]
        return jnp.einsum(
            "spml,sli->spmi", group_ints, chosen, preferred_element_type=jnp.float32
        ).astype(BF16)

    grouped = lax.map(
        one_group, (ints.reshape(slots // 8, 8, paux, width, width), columns.reshape(slots // 8, 8))
    )
    return grouped.reshape(slots, paux, width, nocc)


def local_long(integrals, pair_codes, counts, coeff):
    slots, paux, width, _ = integrals.shape
    nocc = coeff.shape[1]
    nblk = lax.axis_size("blk")
    per_dev = coeff.shape[0] // width
    cap = slots // nblk
    alive = (jnp.arange(cap)[None, :] < counts[:, None]).reshape(slots)
    masked = integrals * alive.astype(BF16)[:, None, None, None]
    local_blocks = coeff.reshape(per_dev, width, nocc)
    half = transform_slots(masked, pair_codes % per_dev, local_blocks)
    half_in, rows_in = (
        lax.all_to_all(half, "blk", split_axis=0, concat_axis=0, tiled=True),
        lax.all_to_all(pair_codes // per_dev, "blk", split_axis=0, concat_axis=0, tiled=True),
    )
    selector = (rows_in[:, None] == jnp.arange(per_dev, dtype=jnp.int32)[None, :]).astype(BF16)
    fitted = jnp.einsum("sk,spmi->pkmi", selector, half_in, preferred_element_type=jnp.float32)
    fitted = fitted.astype(BF16).reshape(paux, per_dev * width, nocc)
    partial_value = jnp.einsum(
        "nj,pni->pji", coeff, fitted, preferred_element_type=jnp.float32
    ).astype(BF16)
    occupied = lax.psum(partial_value.astype(jnp.float32).astype(BF16), "blk")
    return lax.psum_scatter(
        jnp.einsum("pnj,pji->ni", fitted, occupied, preferred_element_type=jnp.float32).astype(BF16),
        "aux",
        scatter_dimension=0,
        tiled=True,
    ).astype(jnp.float32)


LANES = 128


def after(x, *others):
    return lax.optimization_barrier((x, *others))[0]


def swap(x, axis, k):
    return lax.ppermute(x, axis, [(i, i ^ k) for i in range(4)])


def gray(k):
    return k ^ (k >> 1)


def middle(x):
    return lax.ppermute(x, "blk", [(1, 2), (2, 1)])


def pack_kernel(codes, counts, coeff, out, quarter, note, code, count, sems):
    part, nocc = quarter.shape
    a = lax.axis_index("aux")
    copies = (
        pltpu.make_async_copy(
            coeff.at[pl.ds(pl.multiple_of(a * part, part), part)], quarter, sems.at[0]
        ),
        pltpu.make_async_copy(codes, code, sems.at[1]),
        pltpu.make_async_copy(counts, count, sems.at[2]),
    )
    for copy in copies:
        copy.start()
    note[...] = jnp.zeros_like(note)
    for copy in copies:
        copy.wait()
    note[0:1, : code.shape[1]] = code[...].astype(jnp.float32)
    note[8:9, : count.shape[1]] = count[...].astype(jnp.float32)
    top = nocc // LANES * part
    out[top : top + META, :] = note[...].astype(BF16)
    for c in range(nocc // LANES):
        out[c * part : (c + 1) * part, :] = quarter[:, c * LANES : (c + 1) * LANES]


def stack_kernel(x, y, both):
    both[0] = x[...]
    both[1] = y[...]


def copy_kernel(x, y):
    y[...] = x[...]


def gather_quarters(coeff, at_k, refs):
    a = lax.axis_index("aux")
    part = (refs[0].shape[0] - META) * LANES // coeff.shape[1]
    for j, ref in enumerate(refs):
        at = pl.ds(pl.multiple_of(at_k * 4 * part + (a ^ j) * part, part), part)
        for c in range(coeff.shape[1] // LANES):
            coeff[at, c * LANES : (c + 1) * LANES] = ref[c * part : (c + 1) * part, :]


def place(dense, ref, codes, counts, k, left, rows):
    z = lax.axis_index("blk")
    slots, width, _ = ref.shape
    cap = slots // 4
    for s in range(slots):
        target = s // cap
        code = codes[s]

        @pl.when(s % cap < counts[target])
        def _():
            row = gray(target ^ z) * rows + code // 2 * width
            col = left + code % 2 * width
            dense[
                pl.ds(pl.multiple_of(row, width), width),
                pl.ds(pl.multiple_of(col, width), width),
            ] = ref[s]


def noted(notes, k):
    return notes.at[k - 1, 0], notes.at[k - 1, 1]


def dot(x, y):
    return jnp.dot(x, y, preferred_element_type=jnp.float32)


def dot_t(x, y):
    return lax.dot_general(x, y, (((1,), (1,)), ((), ())), preferred_element_type=jnp.float32)


def in_middle(kernel):
    def run(*refs):
        z = lax.axis_index("blk")

        @pl.when((z == 1) | (z == 2))
        def _():
            kernel(*refs)

    return run


@in_middle
def place_kernel(codes, counts, notes, i0, i1, dense):
    rows = dense.shape[1] // 2
    dense[...] = jnp.zeros_like(dense)
    place(dense, i0, codes, counts, 0, 0, rows)
    place(dense, i1, *noted(notes, 1), 1, rows, rows)


@in_middle
def first_kernel(notes, dense, i3, own, *refs):
    early, late, early2, late2, early13, late13, dense3, coeff, left, overlap = refs
    rows = own.shape[0]
    dense3[...] = jnp.zeros_like(dense3)
    place(dense3, i3, *noted(notes, 3), 3, 0, rows)
    coeff[:rows, :] = own[...]
    for i, k in enumerate((1, 3)):
        gather_quarters(coeff, gray(k), (early.at[i], early13.at[i], early2.at[i], early13.at[2 + i]))
    gather_quarters(coeff, gray(2), (late, late13.at[0], late2, late13.at[1]))
    two = 2 * rows
    fitted = dot(dense[:two, :], coeff[:two, :]) + dot(dense3[:two, :], coeff[two : 3 * rows, :])
    left[...] = dot_t(fitted.astype(BF16), coeff[...])
    overlap[...] = dot_t(coeff[3 * rows :, :], coeff[...]).astype(BF16)


def chain(left, dense, dense3, dense2, coeff, wide):
    at = 0
    for columns in (dense, dense3, dense2):
        width = columns.shape[1]
        wide[:, at : at + width] = dot(left, columns[...]).astype(BF16)
        at += width
    return dot(wide[...], coeff[...])


def by_aux(ref, first, rows):
    a = lax.axis_index("aux")
    size = rows // 4
    return jnp.concatenate(
        [ref[pl.ds(pl.multiple_of(first + (a ^ j) * size, size), size), :] for j in range(4)], 0
    )


def cut(total, mine, p1, p2, p3):
    size = mine.shape[0]
    mine[...] = total[:size, :]
    for j, out in enumerate((p1, p2, p3), 1):
        out[...] = total[j * size : (j + 1) * size, :].astype(BF16)


@in_middle
def end_kernel(notes, i2, dense, dense3, coeff, left, overlap, mine, p1, p2, p3, dense2, wide):
    rows = dense2.shape[1]
    dense2[...] = jnp.zeros_like(dense2)
    place(dense2, i2, *noted(notes, 2), 2, 0, rows)
    whole = by_aux(left, rows, rows) + dot(by_aux(dense2, rows, rows), overlap[...])
    total = chain(whole.astype(BF16), dense, dense3, dense2, coeff, wide)
    cut(total, mine, p1, p2, p3)


@in_middle
def own_kernel(dense, dense3, dense2, coeff, left, overlap, mine, p1, p2, p3, wide):
    rows = dense2.shape[1]
    whole = by_aux(left, 0, rows) + dot(by_aux(dense2, 0, rows), overlap[...])
    total = chain(whole.astype(BF16), dense, dense3, dense2, coeff, wide)
    cut(total, mine, p1, p2, p3)


def local_line(integrals, pair_codes, counts, coeff):
    slots, _, width, _ = integrals.shape
    rows, nocc = coeff.shape
    part = rows // 4
    nbf = rows * 4
    sds = jax.ShapeDtypeStruct
    vmem = pl.BlockSpec(memory_space=pltpu.VMEM)
    smem = pl.BlockSpec(memory_space=pltpu.SMEM)
    params = pltpu.CompilerParams(vmem_limit_bytes=20 * 2**20)
    cost = lambda flops, size: pl.CostEstimate(
        flops=flops, bytes_accessed=size, transcendentals=0
    )

    ints = integrals.reshape(slots, width, width)
    top = nocc // LANES * part
    packed = pl.pallas_call(
        pack_kernel,
        out_shape=sds((top + META, LANES), BF16),
        in_specs=[pl.BlockSpec(memory_space=pl.ANY)] * 3,
        out_specs=vmem,
        scratch_shapes=[
            pltpu.VMEM((part, nocc), BF16),
            pltpu.VMEM((META, LANES), jnp.float32),
            pltpu.VMEM((1, slots), jnp.int32),
            pltpu.VMEM((1, counts.shape[0]), jnp.int32),
            pltpu.SemaphoreType.DMA((3,)),
        ],
        compiler_params=pltpu.CompilerParams(vmem_limit_bytes=60 * 2**20),
        cost_estimate=cost(0, 4 * part * nocc),
    )(pair_codes[None], counts[None], coeff)

    ahead = cost(4 * 10**10, nbf * nocc * 4)
    quarter = sds((top + META, LANES), BF16)
    stack = pl.pallas_call(
        stack_kernel,
        out_shape=sds((2, top + META, LANES), BF16),
        in_specs=[vmem, vmem],
        out_specs=vmem,
        compiler_params=params,
        cost_estimate=ahead,
    )
    hold = pl.pallas_call(
        copy_kernel,
        out_shape=quarter,
        in_specs=[vmem],
        out_specs=vmem,
        compiler_params=params,
        cost_estimate=ahead,
    )
    f32 = jnp.float32
    c1 = swap(packed, "blk", 1)
    c3 = middle(packed)
    i1 = swap(ints, "blk", 1)
    onward = hold(c1)
    c2 = middle(onward)
    early = stack(c1, c3)
    early2 = swap(early, "aux", 2)
    i3 = middle(after(ints, onward))
    i2 = middle(i1)
    late = hold(after(c2, i1))
    late2 = swap(late, "aux", 2)
    early13 = swap(jnp.concatenate([early, early2]), "aux", 1)
    notes = jnp.stack([c[top::8, :slots] for c in (c1, late, c3)]).astype(jnp.int32)
    dense = pl.pallas_call(
        place_kernel,
        out_shape=sds((nbf, 2 * rows), BF16),
        in_specs=[smem] * 3 + [vmem] * 2,
        out_specs=vmem,
        compiler_params=params,
    )(pair_codes, counts, notes, ints, i1)
    late13 = swap(after(jnp.stack([late, late2]), dense), "aux", 1)
    dense3, full, left, overlap = pl.pallas_call(
        first_kernel,
        out_shape=(
            sds((nbf, rows), BF16),
            sds((nbf, nocc), BF16),
            sds((2 * rows, nbf), f32),
            sds((rows, nbf), BF16),
        ),
        in_specs=[smem] + [vmem] * 9,
        out_specs=(vmem,) * 4,
        compiler_params=params,
    )(notes, dense, i3, coeff, early, late, early2, late2, early13, late13)
    pieces = (sds((part, nocc), f32),) + (sds((part, nocc), BF16),) * 3
    estimate = cost(2 * rows * nbf * (rows + nbf + nocc), nbf * nocc * 8)
    *end_rows, dense2 = pl.pallas_call(
        end_kernel,
        out_shape=pieces + (sds((nbf, rows), BF16),),
        in_specs=[smem] + [vmem] * 6,
        out_specs=(vmem,) * 5,
        scratch_shapes=[pltpu.VMEM((rows, nbf), BF16)],
        compiler_params=params,
        cost_estimate=estimate,
    )(notes, i2, dense, dense3, full, left, overlap)
    own_rows = pl.pallas_call(
        own_kernel,
        out_shape=pieces,
        in_specs=[vmem] * 6,
        out_specs=(vmem,) * 4,
        scratch_shapes=[pltpu.VMEM((rows, nbf), BF16)],
        compiler_params=params,
        cost_estimate=estimate,
    )(dense, dense3, dense2, full, left, overlap)

    def summed(mine, p1, p2, p3):
        got = [swap(p, "aux", k) for k, p in ((2, p2), (3, p3), (1, p1))]
        return mine + got[0].astype(f32) + got[1].astype(f32) + got[2].astype(f32)

    ends = summed(*end_rows).astype(BF16)
    back = swap(ends, "blk", 1)
    mine, p1, p2, p3 = own_rows
    far = swap(p2, "aux", 2)
    owns = mine + far.astype(f32) + swap(p3, "aux", 3).astype(f32)
    owns = owns + swap(after(p1, far), "aux", 1).astype(f32)
    z = lax.axis_index("blk")
    return jnp.where((z == 0) | (z == 3), back.astype(f32), owns)


def local(integrals, pair_codes, counts, coeff):
    if lax.axis_size("blk") == 4 and lax.axis_size("aux") == 4:
        return local_line(integrals, pair_codes, counts, coeff)
    return local_long(integrals, pair_codes, counts, coeff)


def solution(mesh):
    in_specs = (
        P(("grp", "blk"), "aux", None, None),
        P(("grp", "blk")),
        P(("grp", "blk")),
        P(("grp", "blk"), None),
    )
    out_specs = P(("grp", "blk", "aux"), None)
    return jax.shard_map(local, mesh=mesh, in_specs=in_specs, out_specs=out_specs, check_vma=False)
```
